128 devices in a mesh: pos: 32 (over z, y, x_hi), depth: 2 (over x_lo), det: 2 (over core).
Axes of the slice: x: 4 (x_hi: 2, x_lo: 2; x = x_hi * 2 + x_lo), y: 4, z: 4, core: 2. Of those that a mesh axis runs over, the one named last changes fastest.
Arguments:
- offsets: int32 [256, 2], P('pos'), may hold values from 0 to 768
- counts: int32 [32], P('pos'), may hold values from 1 to 8, 128 in all
- probe_wave: bfloat16 [2, 256, 256], P(None, 'det'), may hold values from -4.1875 to 4.1875
- object_slices: float32 [2, 2, 1024, 1024], P('depth'), may hold values from -1.35 to 1.35, as said below
- measured: float32 [256, 256, 256], P('pos', 'det'), may hold values from 0 to 2
Outputs:
- slice_gradient: float32 [2, 2, 1024, 1024], P('depth', None, ('pos', 'det'))
The draws below stay inside these ranges and needn't reach their ends.
Inputs may be any that keep to these rules, and one draw needn't show every extreme that they name: The counts sum to 128; the largest is 8. `object_slices`: each (real, imaginary) pair is a transmission of modulus 0.74 to 1.35.
All inputs are finite; a program needn't handle non-finite values. No bound on the sum of `counts` on one device may be relied on, other than what follows from the above.
Results may differ from the reference program's by a relative error of at most 0.023.
Values may be sent and summed in bfloat16 or wider, within the bound.
A program may use at most 128 MiB of HBM per device.

```python
import math
import jax
import jax.numpy as jnp
import numpy as np
from jax import lax

WIN = 256
OBJ = 1024
PROP_DIV = 2
CAP = 8
GROUPS = 32
TOTAL = 128
POSITIONS = 256
SLICES = 2


def draw_object_slices(key, part):
    key = jax.random.fold_in(key, 7)
    amp_key, phase_key = jax.random.split(key)
    shape_full = (SLICES, OBJ, OBJ)
    log_amp = jnp.clip(0.1 * jax.random.normal(amp_key, shape_full, jnp.float32), -0.3, 0.3)
    phase_angle = jax.random.uniform(phase_key, shape_full, jnp.float32, -math.pi, math.pi)
    modulus = jnp.exp(log_amp)
    return jnp.stack([modulus * jnp.cos(phase_angle), modulus * jnp.sin(phase_angle)], axis=1)


def touch_ends(values, stream_key, smallest, top_value):
    extent = values.shape
    place = [jax.random.randint(jax.random.fold_in(stream_key, axis), (), 0, extent[axis]) for axis in range(len(extent))]
    values = values.at[tuple(place)].set(smallest)
    longest = extent.index(max(extent))
    place[longest] = (place[longest] + 1) % extent[longest]
    return values.at[tuple(place)].set(top_value)


def block_scale(key, shape, shards, low, top_value):
    factor_of, own = 1.0, jax.random.fold_in(key, 6)
    for dim, parts in shards:
        steps = jnp.exp(jax.random.uniform(jax.random.fold_in(own, dim), (parts,), jnp.float32, low / len(shards), top_value / len(shards)))
        factor_of = factor_of * jnp.repeat(steps, shape[dim] // parts).reshape([-1 if axis == dim else 1 for axis in range(len(shape))])
    return factor_of


def profile(number_of, total, limit, slope):
    loads = [(1 << 20) // math.isqrt(rank ** slope) + 1 for rank in range(2, number_of + 1)]
    surplus, holding = total - limit - (number_of - 1), [1] * (number_of - 1)
    while surplus > 0:
        movable = [i for i in range(number_of - 1) if holding[i] < limit]
        pool, left = sum([loads[i] for i in movable]), surplus
        for i in movable:
            more = min(limit - holding[i], max(1, left * loads[i] // pool), surplus)
            holding[i] = holding[i] + more
            surplus = surplus - more
    return np.array([limit] + holding)


def uneven(own_key, count, total, limit, skew):
    if count == 2:
        one = jax.random.randint(own_key, (), max(1, total - limit), min(limit, total - 1) + 1)
        return jnp.stack([one, total - one])
    sizes = jnp.asarray(profile(count, total, limit, skew), jnp.int32)
    couples = (count - 1) // 2
    donor, sink = sizes[1:1 + 2 * couples:2], sizes[2:2 + 2 * couples:2]
    margin = jnp.minimum(donor - 1, limit - sink)
    shifted = jax.random.randint(jax.random.fold_in(own_key, 1), (couples,), 0, 1 << 20) % (margin + 1)
    sizes = sizes.at[1:1 + 2 * couples:2].set(donor - shifted).at[2:2 + 2 * couples:2].set(sink + shifted)
    return sizes[jax.random.permutation(jax.random.fold_in(own_key, 2), count)]


def scatter_about(key, extent, deviation, most, pieces=(), held_as=jnp.bfloat16):
    array = jax.random.normal(key, extent, jnp.float32) * deviation
    if len(pieces) > 0:
        array = block_scale(key, extent, pieces, -0.22, 0.18) * array
    return jnp.clip(array, min=-most, max=most).astype(held_as)


def setup_inputs(seed: int = 0) -> dict:
    key_of = jax.random.split(jax.random.key(seed), 6)
    offsets = touch_ends(jax.random.randint(key_of[0], (POSITIONS, 2), 0, OBJ - WIN + 1), jax.random.fold_in(key_of[0], 1), 0, OBJ - WIN).astype(jnp.int32)
    counts = uneven(key_of[1], GROUPS, TOTAL, CAP, 2).astype(jnp.int32)
    probe_wave = scatter_about(key_of[2], (2, WIN, WIN), 0.7, 4.1875, ((1, 2),))
    object_slices = draw_object_slices(jax.random.fold_in(key_of[5], 71), 0)
    measured = jnp.clip(2.0 * jax.random.uniform(key_of[4], (POSITIONS, WIN, WIN), jnp.float32) ** block_scale(key_of[4], (POSITIONS, WIN, WIN), ((0, 32), (1, 2)), -0.2, 0.2), 0.0, 2.0)
    return {"offsets": offsets, "counts": counts, "probe_wave": probe_wave, "object_slices": object_slices, "measured": measured}


def dft_tables(window):
    indices = jnp.arange(window, dtype=jnp.int32)
    product = indices[:, None] * indices[None, :] % window
    angles = product.astype(jnp.float32) * (2.0 * math.pi / window)
    return (jnp.cos(angles).astype(jnp.bfloat16), jnp.sin(angles).astype(jnp.bfloat16))

def centred(indices, window):
    return jnp.where(indices < window // 2, indices, indices - window)

def propagator(rows_index, cols_index, window, divisor):
    first_freq = centred(rows_index, window)
    second_freq = centred(cols_index, window)
    phases = (first_freq[:, None] * first_freq[:, None] + second_freq[None, :] * second_freq[None, :]) % (2 * divisor * window)
    angles = phases.astype(jnp.float32) * (math.pi / (divisor * window))
    return (jnp.cos(angles), -jnp.sin(angles))

def matmul_f32(left_side, right_side):
    return jnp.dot(left_side, right_side, preferred_element_type=jnp.float32)

def front_full(field_in, cosine_table, sine_table):
    rounded = field_in.astype(jnp.bfloat16)
    first_real = matmul_f32(rounded[0], cosine_table) + matmul_f32(rounded[1], sine_table)
    first_imag = matmul_f32(rounded[1], cosine_table) - matmul_f32(rounded[0], sine_table)
    mid_real = first_real.astype(jnp.bfloat16)
    mid_imag = first_imag.astype(jnp.bfloat16)
    out_real = matmul_f32(cosine_table, mid_real) + matmul_f32(sine_table, mid_imag)
    out_imag = matmul_f32(cosine_table, mid_imag) - matmul_f32(sine_table, mid_real)
    return jnp.stack([out_real, out_imag])

def back_full(spectrum, cosine_table, sine_table):
    rounded = spectrum.astype(jnp.bfloat16)
    first_real = matmul_f32(cosine_table, rounded[0]) - matmul_f32(sine_table, rounded[1])
    first_imag = matmul_f32(cosine_table, rounded[1]) + matmul_f32(sine_table, rounded[0])
    mid_real = first_real.astype(jnp.bfloat16)
    mid_imag = first_imag.astype(jnp.bfloat16)
    out_real = matmul_f32(mid_real, cosine_table) - matmul_f32(mid_imag, sine_table)
    out_imag = matmul_f32(mid_imag, cosine_table) + matmul_f32(mid_real, sine_table)
    return jnp.stack([out_real, out_imag])

def complex_product(left_side, right_side, conjugate):
    left_real = left_side[0]
    left_imag = -left_side[1] if conjugate else left_side[1]
    return jnp.stack([left_real * right_side[0] - left_imag * right_side[1], left_real * right_side[1] + left_imag * right_side[0]])

def reference(offsets, counts, probe_wave, object_slices, measured):
    cosine_table, sine_table = dft_tables(WIN)
    indices = jnp.arange(WIN, dtype=jnp.int32)
    prop_real, prop_imag = propagator(indices, indices, WIN, PROP_DIV)
    kernel = jnp.stack([prop_real, prop_imag])

    def one_position(position, gradient):
        position = jnp.asarray(position).astype(jnp.int32)
        group_index = position // CAP
        within = position % CAP
        valid_flag = (within < counts[group_index]).astype(jnp.float32)
        row_start = offsets[position, 0]
        col_start = offsets[position, 1]
        zero_index = jnp.zeros((), jnp.int32)
        windows = [lax.dynamic_slice(object_slices[slice_index], (zero_index, row_start, col_start), (2, WIN, WIN)) for slice_index in range(SLICES)]
        stored_waves = []
        wave_in = probe_wave
        descent = None
        for slice_index in range(SLICES):
            stored_waves.append(wave_in)
            exit_wave = complex_product(wave_in.astype(jnp.float32), windows[slice_index], False)
            spectrum = front_full(exit_wave, cosine_table, sine_table)
            if slice_index < SLICES - 1:
                moved_wave = complex_product(kernel, spectrum, False) / (WIN * WIN)
                wave_in = back_full(moved_wave, cosine_table, sine_table).astype(jnp.bfloat16)
            else:
                far_field = spectrum / WIN
                magnitude = jnp.sqrt(far_field[0] * far_field[0] + far_field[1] * far_field[1])
                ratio_term = measured[position].T.astype(jnp.float32) / jnp.maximum(magnitude, 1.0)
                residual = (far_field - ratio_term[None] * far_field) * valid_flag
                descent = back_full(residual / WIN, cosine_table, sine_table).astype(jnp.bfloat16)
        for slice_index in range(SLICES - 1, -1, -1):
            descent_f = descent.astype(jnp.float32)
            contribution = complex_product(stored_waves[slice_index].astype(jnp.float32), descent_f, True)
            start_index = (jnp.int32(slice_index), zero_index, row_start, col_start)
            region = lax.dynamic_slice(gradient, start_index, (1, 2, WIN, WIN))
            gradient = lax.dynamic_update_slice(gradient, region + contribution[None], start_index)
            if slice_index > 0:
                back_wave = complex_product(windows[slice_index], descent_f, True)
                spectrum = front_full(back_wave, cosine_table, sine_table)
                moved_wave = complex_product(kernel, spectrum, True) / (WIN * WIN)
                descent = back_full(moved_wave, cosine_table, sine_table).astype(jnp.bfloat16)
        return gradient
    zeros_init = jnp.zeros((SLICES, 2, OBJ, OBJ), jnp.float32)
    return lax.fori_loop(0, POSITIONS, one_position, zeros_init)
```

```python
import math

import jax
import jax.numpy as jnp
import numpy as np
from jax import lax
from jax.experimental import pallas as pl
from jax.experimental.pallas import tpu as pltpu
from jax.sharding import PartitionSpec as P

PROP_DIV = 2
WIN = 256
HALF = WIN // 2
BANDS = 4
PLANE = 8
CAP = 8
CLS = 16
ROUTE = ((1, 0), (3, 0), (0, 1), (2, 0), (1, 1), (3, 1), (2, 1), (0, 0))
MESH = pl.DeviceIdType.MESH
BF = jnp.bfloat16
F32 = jnp.float32


def tables():
    k = np.arange(WIN)
    angle = (k[:, None] * k[None, :] % WIN) * (2.0 * math.pi / WIN)
    cos, sin = np.cos(angle), np.sin(angle)
    f = np.where(k < WIN // 2, k, k - WIN)
    h = np.exp(-1j * math.pi / (PROP_DIV * WIN) * (f * f % (2 * PROP_DIV * WIN)))
    dft = cos - 1j * sin
    q = (np.conj(dft) * h[None, :]) @ dft / WIN
    qr, qi = q.real, q.imag
    out = np.stack(
        [
            np.block([[cos, -sin], [sin, cos]]) / 16,
            np.block([[cos, sin], [-sin, cos]]) / 16,
            np.block([[qr, qi], [-qi, qr]]),
            np.block([[qr, -qi], [qi, qr]]),
        ]
    )
    return out.astype(np.float32).astype(BF)


def dot(a, b):
    return jnp.dot(a, b, preferred_element_type=F32)


def beside(re, im):
    return jnp.concatenate([re.astype(BF), im.astype(BF)], axis=1)


def stacked(re, im):
    return jnp.concatenate([re.astype(BF), im.astype(BF)], axis=0)


def right_left(re, im, right, left):
    mid = dot(beside(re, im), right).astype(BF)
    out = dot(left, jnp.concatenate([mid[:, :WIN], mid[:, WIN:]], axis=0))
    return out[:WIN], out[WIN:]


def left_right(re, im, left, right):
    mid = dot(left, stacked(re, im)).astype(BF)
    out = dot(jnp.concatenate([mid[:WIN], mid[WIN:]], axis=1), right)
    return out[:, :WIN], out[:, WIN:]


def iota(shape, axis):
    return lax.broadcasted_iota(jnp.int32, shape, axis)


def kernel(
    counts, offs_in, probe, obj, measured, tabs_in, out,
    offs, other_offs, obj_v, tabs, t_all, t_send, probe_v, meas, rolled, amps, grad, pieces, places, acc, z_send, z_recv,
    load_sem, own_sem, probe_sem, meas_sem, t_sem, t_out_sem, out_sem, place_sem, place_out_sem,
    piece_sem, piece_out_sem, z_sem, z_out_sem,
):
    pos, d, c = lax.axis_index("pos"), lax.axis_index("depth"), lax.axis_index("det")
    z, q = pos // PLANE, pos % PLANE
    y, x = q // 2, q % 2 * 2 + d
    cls = q * 2 + c
    other = z * PLANE + (q ^ 1)
    own = 2 * (2 * d + c)
    across = 2 * (2 * (1 - d) + c)
    beside_slot = 2 * (2 * d + 1 - c)

    own_offs = pltpu.make_async_copy(offs_in, offs, own_sem.at[3])
    own_offs.start()
    load_obj = []
    for cb in range(BANDS):
        column = obj.at[:, :, :, pl.ds(cb * WIN, WIN)]
        load_obj.append(pltpu.make_async_copy(column, obj_v.at[cb], load_sem.at[cb]))
        load_obj[-1].start()
    load_tabs = pltpu.make_async_copy(tabs_in, tabs, load_sem.at[BANDS])
    load_tabs.start()
    own_probe = pltpu.make_async_copy(probe, probe_v.at[c], own_sem.at[0])
    own_probe.start()
    own_meas = pltpu.make_async_copy(measured.at[pl.ds(own, 2)], meas.at[c], own_sem.at[1])
    own_meas.start()

    barrier = pltpu.get_barrier_semaphore()
    for k in range(1, 2 * CLS):
        pl.semaphore_signal(
            barrier, inc=1,
            device_id=(z * PLANE + (q ^ (k // 4)), d ^ (k // 2 % 2), c ^ (k % 2)),
            device_id_type=MESH,
        )
    for k in range(1, BANDS):
        pl.semaphore_signal(
            barrier, inc=1, device_id=((z + k) % BANDS * PLANE + q, d, c), device_id_type=MESH
        )

    own_offs.wait()
    slot_of = iota((CAP, 128), 0)
    for axis in range(2):
        spread = jnp.zeros((CAP, 128), jnp.int32)
        for s in range(CAP):
            spread = jnp.where(slot_of == s, offs[axis, s], spread)
        places[q, axis] = spread
    acc[...] = jnp.zeros_like(acc)
    pl.semaphore_wait(barrier, 2 * CLS - 1 + BANDS - 1)

    def place_copy(k):
        return pltpu.make_async_remote_copy(
            src_ref=places.at[q], dst_ref=places.at[q], send_sem=place_out_sem.at[k],
            recv_sem=place_sem.at[q], device_id=(z * PLANE + (q ^ k), d, c),
            device_id_type=MESH,
        )

    def places_of(g):
        return pltpu.make_async_copy(places.at[g], places.at[g], place_sem.at[g])

    place_copy(1).start()

    probe_copy = pltpu.make_async_remote_copy(
        src_ref=probe, dst_ref=probe_v.at[c], send_sem=out_sem.at[0], recv_sem=probe_sem,
        device_id=(pos, d, 1 - c), device_id_type=MESH,
    )
    probe_copy.start()
    meas_copy = pltpu.make_async_remote_copy(
        src_ref=measured.at[pl.ds(beside_slot, 2)], dst_ref=meas.at[c], send_sem=out_sem.at[1],
        recv_sem=meas_sem, device_id=(pos, d, 1 - c), device_id_type=MESH,
    )
    meas_copy.start()

    for column in load_obj:
        column.wait()

    row_of, col_of = iota((WIN, WIN), 0), iota((WIN, WIN), 1)

    half_row = iota((HALF, WIN), 0)
    half_col = iota((HALF, WIN), 1)

    def cut(r, col, half, plane):
        rows = pl.ds(half * HALF, HALF)
        band = jnp.minimum(r >> 8, BANDS - 2)
        block = jnp.minimum(col >> 8, BANDS - 2)
        late = half_col >= col - block * WIN
        top = jnp.where(
            late, obj_v[block, plane, band, rows], obj_v[block + 1, plane, band, rows]
        )
        low = jnp.where(
            late, obj_v[block, plane, band + 1, rows], obj_v[block + 1, plane, band + 1, rows]
        )
        return jnp.where(half_row >= r - band * WIN - half * HALF, top, low).astype(BF)

    def t_copy(i, half):
        there = pos + half * (other - pos)
        return pltpu.make_async_remote_copy(
            src_ref=t_send.at[i, half], dst_ref=t_all.at[d, i, half],
            send_sem=t_out_sem.at[i, half], recv_sem=t_sem.at[i, half],
            device_id=(there, 1 - d, c), device_id_type=MESH,
        )

    places_of(q ^ 1).wait()
    fetch = pltpu.make_async_copy(places.at[q ^ 1], other_offs, own_sem.at[2])
    fetch.start()
    fetch.wait()

    def send_half(n, carry):
        i, half = n // 2, (n + c) % 2
        r = jnp.where(half == 1, other_offs[0, across + i, 0], offs[0, across + i])
        col = jnp.where(half == 1, other_offs[1, across + i, 0], offs[1, across + i])
        for plane in range(2):
            t_send[i, half, plane] = cut(r, col, half, plane)
        t_copy(i, half).start()
        return carry

    def cut_own(i):
        for half in range(2):
            for plane in range(2):
                t_all[d, i, half, plane] = cut(
                    offs[0, own + i], offs[1, own + i], half, plane
                )

    lax.fori_loop(0, 2, send_half, 0)

    def window(s, i):
        return [
            jnp.concatenate([t_all[s, i, 0, p], t_all[s, i, 1, p]], axis=0).astype(F32)
            for p in range(2)
        ]

    def prepare(i):
        cut_own(i)
        flat = jnp.concatenate(
            [jnp.concatenate([probe_v[0, p], probe_v[1, p]], axis=0) for p in range(2)], axis=1
        )
        r, col = offs[0, own + i], offs[1, own + i]
        down = jnp.where(col_of == ((row_of - r) & (WIN - 1)), 1.0, 0.0).astype(BF)
        over = jnp.where(row_of == ((col_of - col) & (WIN - 1)), 1.0, 0.0).astype(BF)
        moved = dot(down, flat).astype(BF)
        moved = dot(jnp.concatenate([moved[:, :WIN], moved[:, WIN:]], axis=0), over)
        rolled[i, 0], rolled[i, 1] = moved[:WIN].astype(BF), moved[WIN:].astype(BF)
        amps[i] = jnp.concatenate([meas[0, i], meas[1, i]], axis=0).T

    own_probe.wait()
    own_meas.wait()
    probe_copy.wait_recv()
    meas_copy.wait_recv()
    prepare(0)
    lax.fori_loop(2, 4, send_half, 0)
    prepare(1)
    for k in range(2, PLANE):
        place_copy(k).start()
    load_tabs.wait()

    def send_pieces(i, s):
        odd = (s + d) % 2
        for dy, far in ROUTE:
            yy = (y + dy * (1 + 2 * c)) % 4
            xx = (x + odd + 2 * ((far + c * odd) % 2)) % 4
            for cc in range(2):
                if (dy, far, cc) == (0, 0, 0):
                    continue
                core = c ^ cc
                pltpu.make_async_remote_copy(
                    src_ref=grad.at[i, s, (yy * 2 + xx // 2) * 2 + core],
                    dst_ref=pieces.at[i, q, 2 * d + c],
                    send_sem=piece_out_sem.at[i, s], recv_sem=piece_sem.at[i, q],
                    device_id=(z * PLANE + yy * 2 + xx // 2, s, core), device_id_type=MESH,
                ).start()

    def send_here(i):
        xx = (x + 1 + 2 * c) % 4
        pltpu.make_async_remote_copy(
            src_ref=grad.at[i, 1 - d, (y * 2 + xx // 2) * 2 + c],
            dst_ref=pieces.at[i, q, 2 * d + c],
            send_sem=piece_out_sem.at[i, 0], recv_sem=piece_sem.at[i, q],
            device_id=(z * PLANE + y * 2 + xx // 2, 1 - d, c), device_id_type=MESH,
        ).start()
        pltpu.make_async_copy(
            grad.at[i, d, cls], pieces.at[i, q, 2 * d + c], piece_sem.at[i, q]
        ).start()

    def load(ref, i):
        return ref[i, 0].astype(F32), ref[i, 1].astype(F32)

    def rounded(pair):
        return pair[0].astype(BF).astype(F32), pair[1].astype(BF).astype(F32)

    def await_windows(i):
        for half in range(2):
            t_copy(i, half).wait_recv()

    def first_wave(i):
        pl.when(d == 1)(lambda: await_windows(i))
        (pr, pi), (tr, ti) = load(rolled, i), window(0, i)
        return rounded(
            right_left(pr * tr - pi * ti, pr * ti + pi * tr, tabs[2], tabs[3])
        )

    def far_field(i, wave):
        pl.when(d == 0)(lambda: await_windows(i))
        (wr, wi), (tr, ti) = wave, window(1, i)
        fr, fi = right_left(wr * tr - wi * ti, wr * ti + wi * tr, tabs[0], tabs[1])
        used = jnp.where(jnp.full((1, WIN), own + i, jnp.int32) < counts[0], 1.0, 0.0)
        scale = used * (1.0 - amps[i] * lax.rsqrt(jnp.maximum(fr * fr + fi * fi, 1.0)))
        return fr * scale, fi * scale

    def descent(residual):
        return rounded(left_right(residual[0], residual[1], tabs[0], tabs[1]))

    def put(i, s, wave, desc):
        (wr, wi), (dr, di) = wave, desc
        grad[i, s, :, 0] = (wr * dr + wi * di).astype(BF).reshape(CLS, 16, WIN)
        grad[i, s, :, 1] = (wr * di - wi * dr).astype(BF).reshape(CLS, 16, WIN)

    def first_descent(i, desc):
        (dr, di), (tr, ti) = desc, window(1, i)
        return rounded(
            right_left(tr * dr + ti * di, tr * di - ti * dr, tabs[3], tabs[2])
        )

    wave_a = first_wave(0)
    desc_a = descent(far_field(0, wave_a))
    put(0, 1, wave_a, desc_a)
    send_pieces(0, 1)
    wave_b = first_wave(1)
    desc_a = first_descent(0, desc_a)
    put(0, 0, load(rolled, 0), desc_a)
    send_pieces(0, 0)
    send_here(0)
    desc_b = descent(far_field(1, wave_b))
    put(1, 1, wave_b, desc_b)
    send_pieces(1, 1)
    put(1, 0, load(rolled, 1), first_descent(1, desc_b))
    send_pieces(1, 0)
    send_here(1)

    row16 = iota((2, 8, WIN), 0) * 8 + iota((2, 8, WIN), 1) + cls * 16
    col8 = iota((8, WIN), 1)

    def add_group(i, g):
        pltpu.make_async_copy(pieces.at[i, g], pieces.at[i, g], piece_sem.at[i, g]).wait()
        rows, cols = places[g, 0], places[g, 1]
        r0 = jnp.minimum(rows >> 8, BANDS - 2)
        c0 = jnp.minimum(cols >> 8, BANDS - 2)
        rm, cm = rows - r0 * WIN, cols - c0 * WIN

        def wide(x, k):
            one = jnp.broadcast_to(x[2 * k + i : 2 * k + i + 1], (8, 128))
            return jnp.concatenate([one, one], axis=1)

        band = [wide(r0, k) + jnp.where(row16 < wide(rm, k), 1, 0) for k in range(4)]
        block = [wide(c0, k) + jnp.where(col8 < wide(cm, k), 1, 0) for k in range(4)]
        for p in range(2):
            piece = [pieces[i, g, k, p].astype(F32).reshape(2, 8, WIN) for k in range(4)]
            for zb in range(BANDS):
                part = [jnp.where(b == zb, x, 0.0) for b, x in zip(band, piece)]
                for cb in range(BANDS):
                    total = acc[zb, p, :, :, cb * WIN : (cb + 1) * WIN]
                    for b, x in zip(block, part):
                        total += jnp.where(b == cb, x, 0.0)
                    acc[zb, p, :, :, cb * WIN : (cb + 1) * WIN] = total

    def add_first(k, carry):
        g = q ^ k ^ (k // 4 * 2)

        @pl.when(k > 1)
        def _():
            places_of(g).wait()

        add_group(0, g)
        return carry

    def add_second(k, carry):
        add_group(1, q ^ k ^ (k // 4 * 2))
        return carry

    lax.fori_loop(0, PLANE, add_first, 0)
    lax.fori_loop(0, PLANE, add_second, 0)

    z_send[...] = acc[...].reshape(BANDS, 2, 16, 1024).astype(BF)

    def z_copy(k):
        there = (z + k) % BANDS
        return pltpu.make_async_remote_copy(
            src_ref=z_send.at[there], dst_ref=z_recv.at[k], send_sem=z_out_sem.at[k],
            recv_sem=z_sem.at[k], device_id=(there * PLANE + q, d, c), device_id_type=MESH,
        )

    for k in (1 + 2 * c, 3 - 2 * c, 2):
        z_copy(k).start()
    total = acc[z].reshape(2, 16, 1024)
    for k in (1, 3, 2):
        z_copy(k).wait_recv()
        total += z_recv[k].astype(F32)
    out[...] = total

    for k in range(1, BANDS):
        z_copy(k).wait_send()
    probe_copy.wait_send()
    meas_copy.wait_send()
    for i in range(2):
        for half in range(2):
            t_copy(i, half).wait_send()
    for k in range(1, PLANE):
        place_copy(k).wait_send()
    for i in range(2):
        for s, count in ((0, CLS), (1, CLS - 1)):
            sent = grad.at[i, s, pl.ds(0, count)]
            pltpu.make_async_copy(sent, sent, piece_out_sem.at[i, s]).wait()


def per_device(offsets, counts, probe_wave, object_slices, measured):
    smem = pl.BlockSpec(memory_space=pltpu.SMEM)
    anywhere = pl.BlockSpec(memory_space=pl.ANY)
    dma = pltpu.SemaphoreType.DMA
    planes = object_slices.reshape(2, BANDS, WIN, BANDS * WIN)
    operands = (offsets.T, probe_wave, planes, measured, jnp.asarray(tables()))
    grad = pl.pallas_call(
        kernel,
        out_shape=pltpu.VMEM((2, 16, 1024), F32),
        in_specs=[smem] + [anywhere] * 5,
        out_specs=pl.BlockSpec(memory_space=pltpu.VMEM),
        scratch_shapes=[
            pltpu.SMEM((2, CAP), jnp.int32),
            pltpu.SMEM((2, CAP, 128), jnp.int32),
            pltpu.VMEM((BANDS, 2, BANDS, WIN, WIN), F32),
            pltpu.VMEM((4, 2 * WIN, 2 * WIN), BF),
            pltpu.VMEM((2, 2, 2, 2, HALF, WIN), BF),
            pltpu.VMEM((2, 2, 2, HALF, WIN), BF),
            pltpu.VMEM((2, 2, WIN // 2, WIN), BF),
            pltpu.VMEM((2, 2, WIN // 2, WIN), F32),
            pltpu.VMEM((2, 2, WIN, WIN), BF),
            pltpu.VMEM((2, WIN, WIN), F32),
            pltpu.VMEM((2, 2, CLS, 2, 16, WIN), BF),
            pltpu.VMEM((2, PLANE, CAP // 2, 2, 16, WIN), BF),
            pltpu.VMEM((PLANE, 2, CAP, 128), jnp.int32),
            pltpu.VMEM((BANDS, 2, 2, 8, 1024), F32),
            pltpu.VMEM((BANDS, 2, 16, 1024), BF),
            pltpu.VMEM((BANDS, 2, 16, 1024), BF),
            dma((BANDS + 1,)),
            dma((4,)),
            dma,
            dma,
            dma((2, 2)),
            dma((2, 2)),
            dma((2,)),
            dma((PLANE,)),
            dma((PLANE,)),
            dma((2, PLANE)),
            dma((2, 2)),
            dma((BANDS,)),
            dma((BANDS,)),
        ],
        compiler_params=pltpu.CompilerParams(
            collective_id=0, has_side_effects=True, vmem_limit_bytes=40 * 2**20
        ),
        cost_estimate=pl.CostEstimate(
            flops=2 * 16 * 2**27, bytes_accessed=12 * 2**20, transcendentals=0
        ),
    )(counts, *(pltpu.with_memory_space_constraint(a, pltpu.HBM) for a in operands))
    return grad[None]


def solution(mesh):
    in_specs = (
        P("pos", None),
        P("pos"),
        P(None, "det", None),
        P("depth", None, None, None),
        P("pos", "det", None),
    )
    out_specs = P("depth", None, ("pos", "det"), None)
    return jax.shard_map(
        per_device, mesh=mesh, in_specs=in_specs, out_specs=out_specs, check_vma=False
    )
```

```python
import math

import jax
import jax.numpy as jnp
import numpy as np
from jax import lax
from jax.experimental import pallas as pl
from jax.experimental.pallas import tpu as pltpu
from jax.sharding import PartitionSpec as P

PROP_DIV = 2
WIN = 256
HALF = WIN // 2
BANDS = 4
PLANE = 8
CAP = 8
CLS = 16
ROUTE = ((2, 1), (2, 0), (0, 1), (1, 1), (3, 1), (1, 0), (3, 0), (0, 0))
MESH = pl.DeviceIdType.MESH
BF = jnp.bfloat16
F32 = jnp.float32


def tables():
    k = np.arange(WIN)
    angle = (k[:, None] * k[None, :] % WIN) * (2.0 * math.pi / WIN)
    cos, sin = np.cos(angle), np.sin(angle)
    f = np.where(k < WIN // 2, k, k - WIN)
    h = np.exp(-1j * math.pi / (PROP_DIV * WIN) * (f * f % (2 * PROP_DIV * WIN)))
    dft = cos - 1j * sin
    q = (np.conj(dft) * h[None, :]) @ dft / WIN
    qr, qi = q.real, q.imag
    out = np.stack(
        [
            np.block([[cos, -sin], [sin, cos]]) / 16,
            np.block([[cos, sin], [-sin, cos]]) / 16,
            np.block([[qr, qi], [-qi, qr]]),
            np.block([[qr, -qi], [qi, qr]]),
        ]
    )
    return out.astype(np.float32).astype(BF)


def dot(a, b):
    return jnp.dot(a, b, preferred_element_type=F32)


def beside(re, im):
    return jnp.concatenate([re.astype(BF), im.astype(BF)], axis=1)


def stacked(re, im):
    return jnp.concatenate([re.astype(BF), im.astype(BF)], axis=0)


def right_left(re, im, right, left):
    mid = dot(beside(re, im), right).astype(BF)
    out = dot(left, jnp.concatenate([mid[:, :WIN], mid[:, WIN:]], axis=0))
    return out[:WIN], out[WIN:]


def left_right(re, im, left, right):
    mid = dot(left, stacked(re, im)).astype(BF)
    out = dot(jnp.concatenate([mid[:WIN], mid[WIN:]], axis=1), right)
    return out[:, :WIN], out[:, WIN:]


def iota(shape, axis):
    return lax.broadcasted_iota(jnp.int32, shape, axis)


def kernel(
    counts, offs_in, probe, obj, measured, tabs_in, out,
    offs, other_offs, obj_v, tabs, t_all, t_send, probe_v, meas, rolled, amps, grad, pieces, places, acc, z_send, z_recv,
    load_sem, own_sem, probe_sem, meas_sem, t_sem, t_out_sem, out_sem, place_sem, place_out_sem,
    piece_sem, piece_out_sem, z_sem, z_out_sem,
):
    pos, d, c = lax.axis_index("pos"), lax.axis_index("depth"), lax.axis_index("det")
    z, q = pos // PLANE, pos % PLANE
    y, x = q // 2, q % 2 * 2 + d
    cls = q * 2 + c
    other = z * PLANE + (q ^ 1)
    own = 2 * (2 * d + c)
    across = 2 * (2 * (1 - d) + c)
    beside_slot = 2 * (2 * d + 1 - c)

    own_offs = pltpu.make_async_copy(offs_in, offs, own_sem.at[3])
    own_offs.start()
    load_obj = []
    for cb in range(BANDS):
        column = obj.at[:, :, :, pl.ds(cb * WIN, WIN)]
        load_obj.append(pltpu.make_async_copy(column, obj_v.at[cb], load_sem.at[cb]))
        load_obj[-1].start()
    load_tabs = pltpu.make_async_copy(tabs_in, tabs, load_sem.at[BANDS])
    load_tabs.start()
    own_probe = pltpu.make_async_copy(probe, probe_v.at[c], own_sem.at[0])
    own_probe.start()
    own_meas = pltpu.make_async_copy(measured.at[pl.ds(own, 2)], meas.at[c], own_sem.at[1])
    own_meas.start()

    barrier = pltpu.get_barrier_semaphore()
    for k in range(1, 2 * CLS):
        pl.semaphore_signal(
            barrier, inc=1,
            device_id=(z * PLANE + (q ^ (k // 4)), d ^ (k // 2 % 2), c ^ (k % 2)),
            device_id_type=MESH,
        )
    for k in range(1, BANDS):
        pl.semaphore_signal(
            barrier, inc=1, device_id=((z + k) % BANDS * PLANE + q, d, c), device_id_type=MESH
        )

    own_offs.wait()
    slot_of = iota((CAP, 128), 0)
    for axis in range(2):
        spread = jnp.zeros((CAP, 128), jnp.int32)
        for s in range(CAP):
            spread = jnp.where(slot_of == s, offs[axis, s], spread)
        places[q, axis] = spread
    acc[...] = jnp.zeros_like(acc)
    pl.semaphore_wait(barrier, 2 * CLS - 1 + BANDS - 1)

    def place_copy(k):
        return pltpu.make_async_remote_copy(
            src_ref=places.at[q], dst_ref=places.at[q], send_sem=place_out_sem.at[k],
            recv_sem=place_sem.at[q], device_id=(z * PLANE + (q ^ k), d, c),
            device_id_type=MESH,
        )

    def places_of(g):
        return pltpu.make_async_copy(places.at[g], places.at[g], place_sem.at[g])

    place_copy(1).start()

    probe_copy = pltpu.make_async_remote_copy(
        src_ref=probe, dst_ref=probe_v.at[c], send_sem=out_sem.at[0], recv_sem=probe_sem,
        device_id=(pos, d, 1 - c), device_id_type=MESH,
    )
    probe_copy.start()
    meas_copy = pltpu.make_async_remote_copy(
        src_ref=measured.at[pl.ds(beside_slot, 2)], dst_ref=meas.at[c], send_sem=out_sem.at[1],
        recv_sem=meas_sem, device_id=(pos, d, 1 - c), device_id_type=MESH,
    )
    meas_copy.start()

    for column in load_obj:
        column.wait()

    row_of, col_of = iota((WIN, WIN), 0), iota((WIN, WIN), 1)

    half_row = iota((HALF, WIN), 0)
    half_col = iota((HALF, WIN), 1)

    def cut(r, col, half, plane):
        rows = pl.ds(half * HALF, HALF)
        band = jnp.minimum(r >> 8, BANDS - 2)
        block = jnp.minimum(col >> 8, BANDS - 2)
        late = half_col >= col - block * WIN
        top = jnp.where(
            late, obj_v[block, plane, band, rows], obj_v[block + 1, plane, band, rows]
        )
        low = jnp.where(
            late, obj_v[block, plane, band + 1, rows], obj_v[block + 1, plane, band + 1, rows]
        )
        return jnp.where(half_row >= r - band * WIN - half * HALF, top, low).astype(BF)

    def t_copy(i, half):
        there = pos + half * (other - pos)
        return pltpu.make_async_remote_copy(
            src_ref=t_send.at[i, half], dst_ref=t_all.at[d, i, half],
            send_sem=t_out_sem.at[i, half], recv_sem=t_sem.at[i, half],
            device_id=(there, 1 - d, c), device_id_type=MESH,
        )

    places_of(q ^ 1).wait()
    fetch = pltpu.make_async_copy(places.at[q ^ 1], other_offs, own_sem.at[2])
    fetch.start()
    fetch.wait()

    def send_half(n, carry):
        i, half = n // 2, (n + c) % 2
        r = jnp.where(half == 1, other_offs[0, across + i, 0], offs[0, across + i])
        col = jnp.where(half == 1, other_offs[1, across + i, 0], offs[1, across + i])
        for plane in range(2):
            t_send[i, half, plane] = cut(r, col, half, plane)
        t_copy(i, half).start()
        return carry

    lax.fori_loop(0, 4, send_half, 0)
    for k in range(2, PLANE):
        place_copy(k).start()

    def cut_own(i, carry):
        for half in range(2):
            for plane in range(2):
                t_all[d, i, half, plane] = cut(
                    offs[0, own + i], offs[1, own + i], half, plane
                )
        return carry

    lax.fori_loop(0, 2, cut_own, 0)

    def window(s, i):
        return [
            jnp.concatenate([t_all[s, i, 0, p], t_all[s, i, 1, p]], axis=0).astype(F32)
            for p in range(2)
        ]

    own_probe.wait()
    own_meas.wait()
    probe_copy.wait_recv()
    meas_copy.wait_recv()

    flat = jnp.concatenate(
        [jnp.concatenate([probe_v[0, p], probe_v[1, p]], axis=0) for p in range(2)], axis=1
    )
    for i in range(2):
        r, col = offs[0, own + i], offs[1, own + i]
        down = jnp.where(col_of == ((row_of - r) & (WIN - 1)), 1.0, 0.0).astype(BF)
        over = jnp.where(row_of == ((col_of - col) & (WIN - 1)), 1.0, 0.0).astype(BF)
        moved = dot(down, flat).astype(BF)
        moved = dot(jnp.concatenate([moved[:, :WIN], moved[:, WIN:]], axis=0), over)
        rolled[i, 0], rolled[i, 1] = moved[:WIN].astype(BF), moved[WIN:].astype(BF)
        amps[i] = jnp.concatenate([meas[0, i], meas[1, i]], axis=0).T
    load_tabs.wait()

    def send_pieces(i, s):
        odd = (s + d) % 2
        for dy, far in ROUTE:
            yy = (y + dy * (1 + 2 * c)) % 4
            xx = (x + odd + 2 * ((far + c * odd) % 2)) % 4
            for cc in range(2):
                if (dy, far, cc) == (0, 0, 0):
                    continue
                core = c ^ cc
                pltpu.make_async_remote_copy(
                    src_ref=grad.at[i, s, (yy * 2 + xx // 2) * 2 + core],
                    dst_ref=pieces.at[i, q, 2 * d + c],
                    send_sem=piece_out_sem.at[i, s], recv_sem=piece_sem.at[i, q],
                    device_id=(z * PLANE + yy * 2 + xx // 2, s, core), device_id_type=MESH,
                ).start()

    def send_here(i):
        xx = (x + 1 + 2 * c) % 4
        pltpu.make_async_remote_copy(
            src_ref=grad.at[i, 1 - d, (y * 2 + xx // 2) * 2 + c],
            dst_ref=pieces.at[i, q, 2 * d + c],
            send_sem=piece_out_sem.at[i, 0], recv_sem=piece_sem.at[i, q],
            device_id=(z * PLANE + y * 2 + xx // 2, 1 - d, c), device_id_type=MESH,
        ).start()
        pltpu.make_async_copy(
            grad.at[i, d, cls], pieces.at[i, q, 2 * d + c], piece_sem.at[i, q]
        ).start()

    def load(ref, i):
        return ref[i, 0].astype(F32), ref[i, 1].astype(F32)

    def rounded(pair):
        return pair[0].astype(BF).astype(F32), pair[1].astype(BF).astype(F32)

    def first_wave(i):
        for half in range(2):
            t_copy(i, half).wait_recv()
        (pr, pi), (tr, ti) = load(rolled, i), window(0, i)
        return rounded(
            right_left(pr * tr - pi * ti, pr * ti + pi * tr, tabs[2], tabs[3])
        )

    def far_field(i, wave):
        (wr, wi), (tr, ti) = wave, window(1, i)
        fr, fi = right_left(wr * tr - wi * ti, wr * ti + wi * tr, tabs[0], tabs[1])
        used = jnp.where(jnp.full((1, WIN), own + i, jnp.int32) < counts[0], 1.0, 0.0)
        scale = used * (1.0 - amps[i] * lax.rsqrt(jnp.maximum(fr * fr + fi * fi, 1.0)))
        return fr * scale, fi * scale

    def descent(residual):
        return rounded(left_right(residual[0], residual[1], tabs[0], tabs[1]))

    def put(i, s, wave, desc):
        (wr, wi), (dr, di) = wave, desc
        grad[i, s, :, 0] = (wr * dr + wi * di).astype(BF).reshape(CLS, 16, WIN)
        grad[i, s, :, 1] = (wr * di - wi * dr).astype(BF).reshape(CLS, 16, WIN)

    def first_descent(i, desc):
        (dr, di), (tr, ti) = desc, window(1, i)
        return rounded(
            right_left(tr * dr + ti * di, tr * di - ti * dr, tabs[3], tabs[2])
        )

    wave_a = first_wave(0)
    desc_a = descent(far_field(0, wave_a))
    put(0, 1, wave_a, desc_a)
    send_pieces(0, 1)
    wave_b = first_wave(1)
    desc_a = first_descent(0, desc_a)
    put(0, 0, load(rolled, 0), desc_a)
    send_pieces(0, 0)
    send_here(0)
    desc_b = descent(far_field(1, wave_b))
    put(1, 1, wave_b, desc_b)
    send_pieces(1, 1)
    put(1, 0, load(rolled, 1), first_descent(1, desc_b))
    send_pieces(1, 0)
    send_here(1)

    row16 = iota((2, 8, WIN), 0) * 8 + iota((2, 8, WIN), 1) + cls * 16
    col8 = iota((8, WIN), 1)

    def add_group(i, g):
        pltpu.make_async_copy(pieces.at[i, g], pieces.at[i, g], piece_sem.at[i, g]).wait()
        rows, cols = places[g, 0], places[g, 1]
        r0 = jnp.minimum(rows >> 8, BANDS - 2)
        c0 = jnp.minimum(cols >> 8, BANDS - 2)
        rm, cm = rows - r0 * WIN, cols - c0 * WIN

        def wide(x, k):
            one = jnp.broadcast_to(x[2 * k + i : 2 * k + i + 1], (8, 128))
            return jnp.concatenate([one, one], axis=1)

        band = [wide(r0, k) + jnp.where(row16 < wide(rm, k), 1, 0) for k in range(4)]
        block = [wide(c0, k) + jnp.where(col8 < wide(cm, k), 1, 0) for k in range(4)]
        for p in range(2):
            piece = [pieces[i, g, k, p].astype(F32).reshape(2, 8, WIN) for k in range(4)]
            for zb in range(BANDS):
                part = [jnp.where(b == zb, x, 0.0) for b, x in zip(band, piece)]
                for cb in range(BANDS):
                    total = acc[zb, p, :, :, cb * WIN : (cb + 1) * WIN]
                    for b, x in zip(block, part):
                        total += jnp.where(b == cb, x, 0.0)
                    acc[zb, p, :, :, cb * WIN : (cb + 1) * WIN] = total

    def add_first(k, carry):
        g = q ^ k ^ (k // 4 * 2)

        @pl.when(k > 1)
        def _():
            places_of(g).wait()

        add_group(0, g)
        return carry

    def add_second(k, carry):
        add_group(1, q ^ k ^ (k // 4 * 2))
        return carry

    lax.fori_loop(0, PLANE, add_first, 0)
    lax.fori_loop(0, PLANE, add_second, 0)

    z_send[...] = acc[...].reshape(BANDS, 2, 16, 1024).astype(BF)

    def z_copy(k):
        there = (z + k) % BANDS
        return pltpu.make_async_remote_copy(
            src_ref=z_send.at[there], dst_ref=z_recv.at[k], send_sem=z_out_sem.at[k],
            recv_sem=z_sem.at[k], device_id=(there * PLANE + q, d, c), device_id_type=MESH,
        )

    for k in (1 + 2 * c, 3 - 2 * c, 2):
        z_copy(k).start()
    total = acc[z].reshape(2, 16, 1024)
    for k in (1, 3, 2):
        z_copy(k).wait_recv()
        total += z_recv[k].astype(F32)
    out[...] = total

    for k in range(1, BANDS):
        z_copy(k).wait_send()
    probe_copy.wait_send()
    meas_copy.wait_send()
    for i in range(2):
        for half in range(2):
            t_copy(i, half).wait_send()
    for k in range(1, PLANE):
        place_copy(k).wait_send()
    for i in range(2):
        for s, count in ((0, CLS), (1, CLS - 1)):
            sent = grad.at[i, s, pl.ds(0, count)]
            pltpu.make_async_copy(sent, sent, piece_out_sem.at[i, s]).wait()


def per_device(offsets, counts, probe_wave, object_slices, measured):
    smem = pl.BlockSpec(memory_space=pltpu.SMEM)
    anywhere = pl.BlockSpec(memory_space=pl.ANY)
    dma = pltpu.SemaphoreType.DMA
    planes = object_slices.reshape(2, BANDS, WIN, BANDS * WIN)
    operands = (offsets.T, probe_wave, planes, measured, jnp.asarray(tables()))
    grad = pl.pallas_call(
        kernel,
        out_shape=pltpu.VMEM((2, 16, 1024), F32),
        in_specs=[smem] + [anywhere] * 5,
        out_specs=pl.BlockSpec(memory_space=pltpu.VMEM),
        scratch_shapes=[
            pltpu.SMEM((2, CAP), jnp.int32),
            pltpu.SMEM((2, CAP, 128), jnp.int32),
            pltpu.VMEM((BANDS, 2, BANDS, WIN, WIN), F32),
            pltpu.VMEM((4, 2 * WIN, 2 * WIN), BF),
            pltpu.VMEM((2, 2, 2, 2, HALF, WIN), BF),
            pltpu.VMEM((2, 2, 2, HALF, WIN), BF),
            pltpu.VMEM((2, 2, WIN // 2, WIN), BF),
            pltpu.VMEM((2, 2, WIN // 2, WIN), F32),
            pltpu.VMEM((2, 2, WIN, WIN), BF),
            pltpu.VMEM((2, WIN, WIN), F32),
            pltpu.VMEM((2, 2, CLS, 2, 16, WIN), BF),
            pltpu.VMEM((2, PLANE, CAP // 2, 2, 16, WIN), BF),
            pltpu.VMEM((PLANE, 2, CAP, 128), jnp.int32),
            pltpu.VMEM((BANDS, 2, 2, 8, 1024), F32),
            pltpu.VMEM((BANDS, 2, 16, 1024), BF),
            pltpu.VMEM((BANDS, 2, 16, 1024), BF),
            dma((BANDS + 1,)),
            dma((4,)),
            dma,
            dma,
            dma((2, 2)),
            dma((2, 2)),
            dma((2,)),
            dma((PLANE,)),
            dma((PLANE,)),
            dma((2, PLANE)),
            dma((2, 2)),
            dma((BANDS,)),
            dma((BANDS,)),
        ],
        compiler_params=pltpu.CompilerParams(
            collective_id=0, has_side_effects=True, vmem_limit_bytes=40 * 2**20
        ),
        cost_estimate=pl.CostEstimate(
            flops=2 * 16 * 2**27, bytes_accessed=12 * 2**20, transcendentals=0
        ),
    )(counts, *(pltpu.with_memory_space_constraint(a, pltpu.HBM) for a in operands))
    return grad[None]


def solution(mesh):
    in_specs = (
        P("pos", None),
        P("pos"),
        P(None, "det", None),
        P("depth", None, None, None),
        P("pos", "det", None),
    )
    out_specs = P("depth", None, ("pos", "det"), None)
    return jax.shard_map(
        per_device, mesh=mesh, in_specs=in_specs, out_specs=out_specs, check_vma=False
    )
```

```python
import math

import jax
import jax.numpy as jnp
import numpy as np
from jax import lax
from jax.experimental import pallas as pl
from jax.experimental.pallas import tpu as pltpu
from jax.sharding import PartitionSpec as P

PROP_DIV = 2
WIN = 256
HALF = WIN // 2
BANDS = 4
PLANE = 8
CAP = 8
CLS = 16
ROUTE = ((1, 0), (3, 0), (0, 1), (2, 0), (1, 1), (3, 1), (2, 1), (0, 0))
MESH = pl.DeviceIdType.MESH
BF = jnp.bfloat16
F32 = jnp.float32


def tables():
    k = np.arange(WIN)
    angle = (k[:, None] * k[None, :] % WIN) * (2.0 * math.pi / WIN)
    cos, sin = np.cos(angle), np.sin(angle)
    f = np.where(k < WIN // 2, k, k - WIN)
    h = np.exp(-1j * math.pi / (PROP_DIV * WIN) * (f * f % (2 * PROP_DIV * WIN)))
    dft = cos - 1j * sin
    q = (np.conj(dft) * h[None, :]) @ dft / WIN
    qr, qi = q.real, q.imag
    out = np.stack(
        [
            np.block([[cos, -sin], [sin, cos]]) / 16,
            np.block([[cos, sin], [-sin, cos]]) / 16,
            np.block([[qr, qi], [-qi, qr]]),
            np.block([[qr, -qi], [qi, qr]]),
        ]
    )
    return out.astype(np.float32).astype(BF)


def dot(a, b):
    return jnp.dot(a, b, preferred_element_type=F32)


def beside(re, im):
    return jnp.concatenate([re.astype(BF), im.astype(BF)], axis=1)


def stacked(re, im):
    return jnp.concatenate([re.astype(BF), im.astype(BF)], axis=0)


def right_left(re, im, right, left):
    mid = dot(beside(re, im), right).astype(BF)
    out = dot(left, jnp.concatenate([mid[:, :WIN], mid[:, WIN:]], axis=0))
    return out[:WIN], out[WIN:]


def left_right(re, im, left, right):
    mid = dot(left, stacked(re, im)).astype(BF)
    out = dot(jnp.concatenate([mid[:WIN], mid[WIN:]], axis=1), right)
    return out[:, :WIN], out[:, WIN:]


def iota(shape, axis):
    return lax.broadcasted_iota(jnp.int32, shape, axis)


def kernel(
    counts, offs_in, probe, obj, measured, tabs_in, out,
    offs, other_offs, obj_v, tabs, t_all, t_send, probe_v, meas, rolled, amps, grad, pieces, places, acc, z_send, z_recv,
    load_sem, own_sem, probe_sem, meas_sem, t_sem, t_out_sem, out_sem, place_sem, place_out_sem,
    swap_sem, swap_out_sem, piece_sem, piece_out_sem, z_sem, z_out_sem,
):
    pos, d, c = lax.axis_index("pos"), lax.axis_index("depth"), lax.axis_index("det")
    z, q = pos // PLANE, pos % PLANE
    y, x = q // 2, q % 2 * 2 + d
    cls = q * 2 + c
    other = z * PLANE + (q ^ 1)
    own = 2 * (2 * d + c)
    across = 2 * (2 * (1 - d) + c)
    beside_slot = 2 * (2 * d + 1 - c)

    own_offs = pltpu.make_async_copy(offs_in, offs, own_sem.at[3])
    own_offs.start()
    load_obj = []
    for cb in range(BANDS):
        column = obj.at[:, :, :, pl.ds(cb * WIN, WIN)]
        load_obj.append(pltpu.make_async_copy(column, obj_v.at[cb], load_sem.at[cb]))
        load_obj[-1].start()
    load_tabs = pltpu.make_async_copy(tabs_in, tabs, load_sem.at[BANDS])
    load_tabs.start()
    own_probe = pltpu.make_async_copy(probe, probe_v.at[c], own_sem.at[0])
    own_probe.start()
    own_meas = pltpu.make_async_copy(measured.at[pl.ds(own, 2)], meas.at[c], own_sem.at[1])
    own_meas.start()

    barrier = pltpu.get_barrier_semaphore()
    pl.semaphore_signal(barrier, inc=1, device_id=(pos, d, 1 - c), device_id_type=MESH)
    for k in range(1, CLS):
        pl.semaphore_signal(
            barrier, inc=1, device_id=(z * PLANE + (q ^ (k // 2)), d ^ (k % 2), c),
            device_id_type=MESH,
        )
    for k in range(1, BANDS):
        pl.semaphore_signal(
            barrier, inc=1, device_id=((z + k) % BANDS * PLANE + q, d, c), device_id_type=MESH
        )

    own_offs.wait()
    slot_of = iota((CAP, 128), 0)
    for axis in range(2):
        spread = jnp.zeros((CAP, 128), jnp.int32)
        for s in range(CAP):
            spread = jnp.where(slot_of == s, offs[axis, s], spread)
        places[q, axis] = spread
    acc[...] = jnp.zeros_like(acc)
    pl.semaphore_wait(barrier, 1 + CLS - 1 + BANDS - 1)

    def place_copy(k):
        return pltpu.make_async_remote_copy(
            src_ref=places.at[q], dst_ref=places.at[q], send_sem=place_out_sem.at[k],
            recv_sem=place_sem.at[q], device_id=(z * PLANE + (q ^ k), d, c),
            device_id_type=MESH,
        )

    def places_of(g):
        return pltpu.make_async_copy(places.at[g], places.at[g], place_sem.at[g])

    place_copy(1).start()

    probe_copy = pltpu.make_async_remote_copy(
        src_ref=probe, dst_ref=probe_v.at[c], send_sem=out_sem.at[0], recv_sem=probe_sem,
        device_id=(pos, d, 1 - c), device_id_type=MESH,
    )
    probe_copy.start()
    meas_copy = pltpu.make_async_remote_copy(
        src_ref=measured.at[pl.ds(beside_slot, 2)], dst_ref=meas.at[c], send_sem=out_sem.at[1],
        recv_sem=meas_sem, device_id=(pos, d, 1 - c), device_id_type=MESH,
    )
    meas_copy.start()

    for column in load_obj:
        column.wait()

    row_of, col_of = iota((WIN, WIN), 0), iota((WIN, WIN), 1)

    half_row = iota((HALF, WIN), 0)
    half_col = iota((HALF, WIN), 1)

    def cut(r, col, half, plane):
        rows = pl.ds(half * HALF, HALF)
        band = jnp.minimum(r >> 8, BANDS - 2)
        block = jnp.minimum(col >> 8, BANDS - 2)
        late = half_col >= col - block * WIN
        top = jnp.where(
            late, obj_v[block, plane, band, rows], obj_v[block + 1, plane, band, rows]
        )
        low = jnp.where(
            late, obj_v[block, plane, band + 1, rows], obj_v[block + 1, plane, band + 1, rows]
        )
        return jnp.where(half_row >= r - band * WIN - half * HALF, top, low).astype(BF)

    def t_copy(i, half):
        there = pos + half * (other - pos)
        return pltpu.make_async_remote_copy(
            src_ref=t_send.at[i, half], dst_ref=t_all.at[d, i, half],
            send_sem=t_out_sem.at[i, half], recv_sem=t_sem.at[i, half],
            device_id=(there, 1 - d, c), device_id_type=MESH,
        )

    places_of(q ^ 1).wait()
    fetch = pltpu.make_async_copy(places.at[q ^ 1], other_offs, own_sem.at[2])
    fetch.start()
    fetch.wait()

    def send_half(n, carry):
        i, half = n // 2, (n + c) % 2
        r = jnp.where(half == 1, other_offs[0, across + i, 0], offs[0, across + i])
        col = jnp.where(half == 1, other_offs[1, across + i, 0], offs[1, across + i])
        for plane in range(2):
            t_send[i, half, plane] = cut(r, col, half, plane)
        t_copy(i, half).start()
        return carry

    lax.fori_loop(0, 4, send_half, 0)
    for k in range(2, PLANE):
        place_copy(k).start()

    def cut_own(i, carry):
        for half in range(2):
            for plane in range(2):
                t_all[d, i, half, plane] = cut(
                    offs[0, own + i], offs[1, own + i], half, plane
                )
        return carry

    lax.fori_loop(0, 2, cut_own, 0)

    def window(s, i):
        return [
            jnp.concatenate([t_all[s, i, 0, p], t_all[s, i, 1, p]], axis=0).astype(F32)
            for p in range(2)
        ]

    own_probe.wait()
    own_meas.wait()
    probe_copy.wait_recv()
    meas_copy.wait_recv()

    flat = jnp.concatenate(
        [jnp.concatenate([probe_v[0, p], probe_v[1, p]], axis=0) for p in range(2)], axis=1
    )
    for i in range(2):
        r, col = offs[0, own + i], offs[1, own + i]
        down = jnp.where(col_of == ((row_of - r) & (WIN - 1)), 1.0, 0.0).astype(BF)
        over = jnp.where(row_of == ((col_of - col) & (WIN - 1)), 1.0, 0.0).astype(BF)
        moved = dot(down, flat).astype(BF)
        moved = dot(jnp.concatenate([moved[:, :WIN], moved[:, WIN:]], axis=0), over)
        rolled[i, 0], rolled[i, 1] = moved[:WIN].astype(BF), moved[WIN:].astype(BF)
        amps[i] = jnp.concatenate([meas[0, i], meas[1, i]], axis=0).T
    load_tabs.wait()

    def swap(i, s):
        part = grad.at[i, s, 1 - c, :, c]
        return pltpu.make_async_remote_copy(
            src_ref=part, dst_ref=part, send_sem=swap_out_sem.at[i, s], recv_sem=swap_sem.at[i, s],
            device_id=(pos, d, 1 - c), device_id_type=MESH,
        )

    def piece_copy(i, s, yy, xx, out_sem):
        return pltpu.make_async_remote_copy(
            src_ref=grad.at[i, s, c, yy * 2 + xx // 2], dst_ref=pieces.at[i, q, d],
            send_sem=out_sem, recv_sem=piece_sem.at[i, q],
            device_id=(z * PLANE + yy * 2 + xx // 2, s, c), device_id_type=MESH,
        )

    def send_pieces(i, s):
        swap(i, s).wait_recv()
        odd = (s + d) % 2
        for dy, far in ROUTE[:-1]:
            yy = (y + dy * (1 + 2 * c)) % 4
            xx = (x + odd + 2 * ((far + c * odd) % 2)) % 4
            piece_copy(i, s, yy, xx, piece_out_sem.at[i, s]).start()

    def send_here(i):
        piece_copy(i, 1 - d, y, (x + 1 + 2 * c) % 4, piece_out_sem.at[i, 0]).start()
        pltpu.make_async_copy(
            grad.at[i, d, c, q], pieces.at[i, q, d], piece_sem.at[i, q]
        ).start()

    def load(ref, i):
        return ref[i, 0].astype(F32), ref[i, 1].astype(F32)

    def rounded(pair):
        return pair[0].astype(BF).astype(F32), pair[1].astype(BF).astype(F32)

    def first_wave(i):
        for half in range(2):
            t_copy(i, half).wait_recv()
        (pr, pi), (tr, ti) = load(rolled, i), window(0, i)
        return rounded(
            right_left(pr * tr - pi * ti, pr * ti + pi * tr, tabs[2], tabs[3])
        )

    def far_field(i, wave):
        (wr, wi), (tr, ti) = wave, window(1, i)
        fr, fi = right_left(wr * tr - wi * ti, wr * ti + wi * tr, tabs[0], tabs[1])
        used = jnp.where(jnp.full((1, WIN), own + i, jnp.int32) < counts[0], 1.0, 0.0)
        scale = used * (1.0 - amps[i] * lax.rsqrt(jnp.maximum(fr * fr + fi * fi, 1.0)))
        return fr * scale, fi * scale

    def descent(residual):
        return rounded(left_right(residual[0], residual[1], tabs[0], tabs[1]))

    def put(i, s, wave, desc):
        (wr, wi), (dr, di) = wave, desc
        re = (wr * dr + wi * di).astype(BF).reshape(PLANE, 2, 16, WIN)
        im = (wr * di - wi * dr).astype(BF).reshape(PLANE, 2, 16, WIN)
        for core in range(2):
            grad[i, s, core, :, c, 0] = re[:, core]
            grad[i, s, core, :, c, 1] = im[:, core]
        swap(i, s).start()

    def first_descent(i, desc):
        (dr, di), (tr, ti) = desc, window(1, i)
        return rounded(
            right_left(tr * dr + ti * di, tr * di - ti * dr, tabs[3], tabs[2])
        )

    wave_a = first_wave(0)
    desc_a = descent(far_field(0, wave_a))
    put(0, 1, wave_a, desc_a)
    put(0, 0, load(rolled, 0), first_descent(0, desc_a))
    send_pieces(0, 1)
    wave_b = first_wave(1)
    send_pieces(0, 0)
    send_here(0)
    desc_b = descent(far_field(1, wave_b))
    put(1, 1, wave_b, desc_b)
    put(1, 0, load(rolled, 1), first_descent(1, desc_b))
    send_pieces(1, 1)
    send_pieces(1, 0)
    send_here(1)

    row16 = iota((2, 8, WIN), 0) * 8 + iota((2, 8, WIN), 1) + cls * 16
    col8 = iota((8, WIN), 1)

    def add_group(i, g):
        pltpu.make_async_copy(pieces.at[i, g], pieces.at[i, g], piece_sem.at[i, g]).wait()
        rows, cols = places[g, 0], places[g, 1]
        r0 = jnp.minimum(rows >> 8, BANDS - 2)
        c0 = jnp.minimum(cols >> 8, BANDS - 2)
        rm, cm = rows - r0 * WIN, cols - c0 * WIN

        def wide(x, k):
            one = jnp.broadcast_to(x[2 * k + i : 2 * k + i + 1], (8, 128))
            return jnp.concatenate([one, one], axis=1)

        band = [wide(r0, k) + jnp.where(row16 < wide(rm, k), 1, 0) for k in range(4)]
        block = [wide(c0, k) + jnp.where(col8 < wide(cm, k), 1, 0) for k in range(4)]
        for p in range(2):
            piece = [pieces[i, g, k // 2, k % 2, p].astype(F32).reshape(2, 8, WIN) for k in range(4)]
            for zb in range(BANDS):
                part = [jnp.where(b == zb, x, 0.0) for b, x in zip(band, piece)]
                for cb in range(BANDS):
                    total = acc[zb, p, :, :, cb * WIN : (cb + 1) * WIN]
                    for b, x in zip(block, part):
                        total += jnp.where(b == cb, x, 0.0)
                    acc[zb, p, :, :, cb * WIN : (cb + 1) * WIN] = total

    def add_first(k, carry):
        g = q ^ k ^ (k // 4 * 2)

        @pl.when(k > 1)
        def _():
            places_of(g).wait()

        add_group(0, g)
        return carry

    def add_second(k, carry):
        add_group(1, q ^ k ^ (k // 4 * 2))
        return carry

    lax.fori_loop(0, PLANE, add_first, 0)
    lax.fori_loop(0, PLANE, add_second, 0)

    z_send[...] = acc[...].reshape(BANDS, 2, 16, 1024).astype(BF)

    def z_copy(k):
        there = (z + k) % BANDS
        return pltpu.make_async_remote_copy(
            src_ref=z_send.at[there], dst_ref=z_recv.at[k], send_sem=z_out_sem.at[k],
            recv_sem=z_sem.at[k], device_id=(there * PLANE + q, d, c), device_id_type=MESH,
        )

    for k in (1 + 2 * c, 3 - 2 * c, 2):
        z_copy(k).start()
    total = acc[z].reshape(2, 16, 1024)
    for k in (1, 3, 2):
        z_copy(k).wait_recv()
        total += z_recv[k].astype(F32)
    out[...] = total

    for k in range(1, BANDS):
        z_copy(k).wait_send()
    probe_copy.wait_send()
    meas_copy.wait_send()
    for i in range(2):
        for half in range(2):
            t_copy(i, half).wait_send()
    for k in range(1, PLANE):
        place_copy(k).wait_send()
    for i in range(2):
        for s, count in ((0, PLANE), (1, PLANE - 1)):
            swap(i, s).wait_send()
            sent = grad.at[i, s, 0, pl.ds(0, count)]
            pltpu.make_async_copy(sent, sent, piece_out_sem.at[i, s]).wait()


def per_device(offsets, counts, probe_wave, object_slices, measured):
    smem = pl.BlockSpec(memory_space=pltpu.SMEM)
    anywhere = pl.BlockSpec(memory_space=pl.ANY)
    dma = pltpu.SemaphoreType.DMA
    planes = object_slices.reshape(2, BANDS, WIN, BANDS * WIN)
    operands = (offsets.T, probe_wave, planes, measured, jnp.asarray(tables()))
    grad = pl.pallas_call(
        kernel,
        out_shape=pltpu.VMEM((2, 16, 1024), F32),
        in_specs=[smem] + [anywhere] * 5,
        out_specs=pl.BlockSpec(memory_space=pltpu.VMEM),
        scratch_shapes=[
            pltpu.SMEM((2, CAP), jnp.int32),
            pltpu.SMEM((2, CAP, 128), jnp.int32),
            pltpu.VMEM((BANDS, 2, BANDS, WIN, WIN), F32),
            pltpu.VMEM((4, 2 * WIN, 2 * WIN), BF),
            pltpu.VMEM((2, 2, 2, 2, HALF, WIN), BF),
            pltpu.VMEM((2, 2, 2, HALF, WIN), BF),
            pltpu.VMEM((2, 2, WIN // 2, WIN), BF),
            pltpu.VMEM((2, 2, WIN // 2, WIN), F32),
            pltpu.VMEM((2, 2, WIN, WIN), BF),
            pltpu.VMEM((2, WIN, WIN), F32),
            pltpu.VMEM((2, 2, 2, PLANE, 2, 2, 16, WIN), BF),
            pltpu.VMEM((2, PLANE, 2, 2, 2, 16, WIN), BF),
            pltpu.VMEM((PLANE, 2, CAP, 128), jnp.int32),
            pltpu.VMEM((BANDS, 2, 2, 8, 1024), F32),
            pltpu.VMEM((BANDS, 2, 16, 1024), BF),
            pltpu.VMEM((BANDS, 2, 16, 1024), BF),
            dma((BANDS + 1,)),
            dma((4,)),
            dma,
            dma,
            dma((2, 2)),
            dma((2, 2)),
            dma((2,)),
            dma((PLANE,)),
            dma((PLANE,)),
            dma((2, 2)),
            dma((2, 2)),
            dma((2, PLANE)),
            dma((2, 2)),
            dma((BANDS,)),
            dma((BANDS,)),
        ],
        compiler_params=pltpu.CompilerParams(
            collective_id=0, has_side_effects=True, vmem_limit_bytes=40 * 2**20
        ),
        cost_estimate=pl.CostEstimate(
            flops=2 * 16 * 2**27, bytes_accessed=12 * 2**20, transcendentals=0
        ),
    )(counts, *(pltpu.with_memory_space_constraint(a, pltpu.HBM) for a in operands))
    return grad[None]


def solution(mesh):
    in_specs = (
        P("pos", None),
        P("pos"),
        P(None, "det", None),
        P("depth", None, None, None),
        P("pos", "det", None),
    )
    out_specs = P("depth", None, ("pos", "det"), None)
    return jax.shard_map(
        per_device, mesh=mesh, in_specs=in_specs, out_specs=out_specs, check_vma=False
    )
```

```python
import math

import jax
import jax.numpy as jnp
import numpy as np
from jax import lax
from jax.experimental import pallas as pl
from jax.experimental.pallas import tpu as pltpu
from jax.sharding import PartitionSpec as P

PROP_DIV = 2
WIN = 256
HALF = WIN // 2
BANDS = 4
PLANE = 8
CAP = 8
CLS = 16
ROUTE = ((1, 0), (3, 0), (0, 1), (2, 0), (1, 1), (3, 1), (2, 1), (0, 0))
MESH = pl.DeviceIdType.MESH
BF = jnp.bfloat16
F32 = jnp.float32


def tables():
    k = np.arange(WIN)
    angle = (k[:, None] * k[None, :] % WIN) * (2.0 * math.pi / WIN)
    cos, sin = np.cos(angle), np.sin(angle)
    f = np.where(k < WIN // 2, k, k - WIN)
    h = np.exp(-1j * math.pi / (PROP_DIV * WIN) * (f * f % (2 * PROP_DIV * WIN)))
    dft = cos - 1j * sin
    q = (np.conj(dft) * h[None, :]) @ dft / WIN
    qr, qi = q.real, q.imag
    out = np.stack(
        [
            np.block([[cos, -sin], [sin, cos]]) / 16,
            np.block([[cos, sin], [-sin, cos]]) / 16,
            np.block([[qr, qi], [-qi, qr]]),
            np.block([[qr, -qi], [qi, qr]]),
        ]
    )
    return out.astype(np.float32).astype(BF)


def dot(a, b):
    return jnp.dot(a, b, preferred_element_type=F32)


def beside(re, im):
    return jnp.concatenate([re.astype(BF), im.astype(BF)], axis=1)


def stacked(re, im):
    return jnp.concatenate([re.astype(BF), im.astype(BF)], axis=0)


def right_left(re, im, right, left):
    mid = dot(beside(re, im), right).astype(BF)
    out = dot(left, jnp.concatenate([mid[:, :WIN], mid[:, WIN:]], axis=0))
    return out[:WIN], out[WIN:]


def left_right(re, im, left, right):
    mid = dot(left, stacked(re, im)).astype(BF)
    out = dot(jnp.concatenate([mid[:WIN], mid[WIN:]], axis=1), right)
    return out[:, :WIN], out[:, WIN:]


def iota(shape, axis):
    return lax.broadcasted_iota(jnp.int32, shape, axis)


def kernel(
    counts, offs_in, probe, obj, measured, tabs_in, out,
    offs, other_offs, obj_v, tabs, t_all, t_send, probe_v, meas, rolled, amps, grad, pieces, places, acc, z_send, z_recv,
    load_sem, own_sem, probe_sem, meas_sem, t_sem, t_out_sem, out_sem, place_sem, place_out_sem,
    piece_sem, piece_out_sem, z_sem, z_out_sem,
):
    pos, d, c = lax.axis_index("pos"), lax.axis_index("depth"), lax.axis_index("det")
    z, q = pos // PLANE, pos % PLANE
    y, x = q // 2, q % 2 * 2 + d
    cls = q * 2 + c
    other = z * PLANE + (q ^ 1)
    own = 2 * (2 * d + c)
    across = 2 * (2 * (1 - d) + c)
    beside_slot = 2 * (2 * d + 1 - c)

    own_offs = pltpu.make_async_copy(offs_in, offs, own_sem.at[3])
    own_offs.start()
    load_obj = []
    for cb in range(BANDS):
        column = obj.at[:, :, :, pl.ds(cb * WIN, WIN)]
        load_obj.append(pltpu.make_async_copy(column, obj_v.at[cb], load_sem.at[cb]))
        load_obj[-1].start()
    barrier = pltpu.get_barrier_semaphore()
    for k in range(1, 2 * CLS):
        pl.semaphore_signal(
            barrier, inc=1,
            device_id=(z * PLANE + (q ^ (k // 4)), d ^ (k // 2 % 2), c ^ (k % 2)),
            device_id_type=MESH,
        )
    for k in range(1, BANDS):
        pl.semaphore_signal(
            barrier, inc=1, device_id=((z + k) % BANDS * PLANE + q, d, c), device_id_type=MESH
        )

    load_tabs = pltpu.make_async_copy(tabs_in, tabs, load_sem.at[BANDS])
    load_tabs.start()
    own_probe = pltpu.make_async_copy(probe, probe_v.at[c], own_sem.at[0])
    own_probe.start()
    own_meas = pltpu.make_async_copy(measured.at[pl.ds(own, 2)], meas.at[c], own_sem.at[1])
    own_meas.start()

    own_offs.wait()
    slot_of = iota((CAP, 128), 0)
    for axis in range(2):
        spread = jnp.zeros((CAP, 128), jnp.int32)
        for s in range(CAP):
            spread = jnp.where(slot_of == s, offs[axis, s], spread)
        places[q, axis] = spread
    acc[...] = jnp.zeros_like(acc)
    pl.semaphore_wait(barrier, 2 * CLS - 1 + BANDS - 1)

    def place_copy(k):
        return pltpu.make_async_remote_copy(
            src_ref=places.at[q], dst_ref=places.at[q], send_sem=place_out_sem.at[k],
            recv_sem=place_sem.at[q], device_id=(z * PLANE + (q ^ k), d, c),
            device_id_type=MESH,
        )

    def places_of(g):
        return pltpu.make_async_copy(places.at[g], places.at[g], place_sem.at[g])

    offs_copy = pltpu.make_async_remote_copy(
        src_ref=offs, dst_ref=other_offs, send_sem=place_out_sem.at[0], recv_sem=own_sem.at[2],
        device_id=(other, d, c), device_id_type=MESH,
    )
    offs_copy.start()

    probe_copy = pltpu.make_async_remote_copy(
        src_ref=probe, dst_ref=probe_v.at[c], send_sem=out_sem.at[0], recv_sem=probe_sem,
        device_id=(pos, d, 1 - c), device_id_type=MESH,
    )
    probe_copy.start()
    meas_copy = pltpu.make_async_remote_copy(
        src_ref=measured.at[pl.ds(beside_slot, 2)], dst_ref=meas.at[c], send_sem=out_sem.at[1],
        recv_sem=meas_sem, device_id=(pos, d, 1 - c), device_id_type=MESH,
    )
    meas_copy.start()

    for column in load_obj:
        column.wait()

    row_of, col_of = iota((WIN, WIN), 0), iota((WIN, WIN), 1)

    half_row = iota((HALF, WIN), 0)
    half_col = iota((HALF, WIN), 1)

    def cut(r, col, half, plane):
        rows = pl.ds(half * HALF, HALF)
        band = jnp.minimum(r >> 8, BANDS - 2)
        block = jnp.minimum(col >> 8, BANDS - 2)
        late = half_col >= col - block * WIN
        top = jnp.where(
            late, obj_v[block, plane, band, rows], obj_v[block + 1, plane, band, rows]
        )
        low = jnp.where(
            late, obj_v[block, plane, band + 1, rows], obj_v[block + 1, plane, band + 1, rows]
        )
        return jnp.where(half_row >= r - band * WIN - half * HALF, top, low).astype(BF)

    def t_copy(i, half):
        there = pos + half * (other - pos)
        return pltpu.make_async_remote_copy(
            src_ref=t_send.at[i, half], dst_ref=t_all.at[d, i, half],
            send_sem=t_out_sem.at[i, half], recv_sem=t_sem.at[i, half],
            device_id=(there, 1 - d, c), device_id_type=MESH,
        )

    def send_near(i):
        for plane in range(2):
            t_send[i, 0, plane] = cut(offs[0, across + i], offs[1, across + i], 0, plane)
        t_copy(i, 0).start()

    def send_far(i):
        for plane in range(2):
            t_send[i, 1, plane] = cut(
                other_offs[0, across + i], other_offs[1, across + i], 1, plane
            )
        t_copy(i, 1).start()

    send_near(0)
    offs_copy.wait_recv()
    send_far(0)
    send_near(1)
    send_far(1)
    for k in range(1, PLANE):
        place_copy(k).start()

    def cut_own(i, carry):
        for half in range(2):
            for plane in range(2):
                t_all[d, i, half, plane] = cut(
                    offs[0, own + i], offs[1, own + i], half, plane
                )
        return carry

    lax.fori_loop(0, 2, cut_own, 0)

    def window(s, i):
        return [
            jnp.concatenate([t_all[s, i, 0, p], t_all[s, i, 1, p]], axis=0).astype(F32)
            for p in range(2)
        ]

    own_probe.wait()
    own_meas.wait()
    probe_copy.wait_recv()
    meas_copy.wait_recv()

    flat = jnp.concatenate(
        [jnp.concatenate([probe_v[0, p], probe_v[1, p]], axis=0) for p in range(2)], axis=1
    )
    for i in range(2):
        r, col = offs[0, own + i], offs[1, own + i]
        down = jnp.where(col_of == ((row_of - r) & (WIN - 1)), 1.0, 0.0).astype(BF)
        over = jnp.where(row_of == ((col_of - col) & (WIN - 1)), 1.0, 0.0).astype(BF)
        moved = dot(down, flat).astype(BF)
        moved = dot(jnp.concatenate([moved[:, :WIN], moved[:, WIN:]], axis=0), over)
        rolled[i, 0], rolled[i, 1] = moved[:WIN].astype(BF), moved[WIN:].astype(BF)
        amps[i] = jnp.concatenate([meas[0, i], meas[1, i]], axis=0).T
    load_tabs.wait()

    def send_pieces(i, s):
        odd = (s + d) % 2
        for dy, far in ROUTE:
            yy = (y + dy * (1 + 2 * c)) % 4
            xx = (x + odd + 2 * ((far + c * odd) % 2)) % 4
            for cc in range(2):
                if (dy, far, cc) == (0, 0, 0):
                    continue
                core = c ^ cc
                pltpu.make_async_remote_copy(
                    src_ref=grad.at[i, s, (yy * 2 + xx // 2) * 2 + core],
                    dst_ref=pieces.at[i, q, 2 * d + c],
                    send_sem=piece_out_sem.at[i, s], recv_sem=piece_sem.at[i, q],
                    device_id=(z * PLANE + yy * 2 + xx // 2, s, core), device_id_type=MESH,
                ).start()

    def send_here(i):
        xx = (x + 1 + 2 * c) % 4
        pltpu.make_async_remote_copy(
            src_ref=grad.at[i, 1 - d, (y * 2 + xx // 2) * 2 + c],
            dst_ref=pieces.at[i, q, 2 * d + c],
            send_sem=piece_out_sem.at[i, 0], recv_sem=piece_sem.at[i, q],
            device_id=(z * PLANE + y * 2 + xx // 2, 1 - d, c), device_id_type=MESH,
        ).start()
        pltpu.make_async_copy(
            grad.at[i, d, cls], pieces.at[i, q, 2 * d + c], piece_sem.at[i, q]
        ).start()

    def load(ref, i):
        return ref[i, 0].astype(F32), ref[i, 1].astype(F32)

    def rounded(pair):
        return pair[0].astype(BF).astype(F32), pair[1].astype(BF).astype(F32)

    def first_wave(i):
        for half in range(2):
            t_copy(i, half).wait_recv()
        (pr, pi), (tr, ti) = load(rolled, i), window(0, i)
        return rounded(
            right_left(pr * tr - pi * ti, pr * ti + pi * tr, tabs[2], tabs[3])
        )

    def far_field(i, wave):
        (wr, wi), (tr, ti) = wave, window(1, i)
        fr, fi = right_left(wr * tr - wi * ti, wr * ti + wi * tr, tabs[0], tabs[1])
        used = jnp.where(jnp.full((1, WIN), own + i, jnp.int32) < counts[0], 1.0, 0.0)
        scale = used * (1.0 - amps[i] * lax.rsqrt(jnp.maximum(fr * fr + fi * fi, 1.0)))
        return fr * scale, fi * scale

    def descent(residual):
        return rounded(left_right(residual[0], residual[1], tabs[0], tabs[1]))

    def put(i, s, wave, desc):
        (wr, wi), (dr, di) = wave, desc
        grad[i, s, :, 0] = (wr * dr + wi * di).astype(BF).reshape(CLS, 16, WIN)
        grad[i, s, :, 1] = (wr * di - wi * dr).astype(BF).reshape(CLS, 16, WIN)

    def first_descent(i, desc):
        (dr, di), (tr, ti) = desc, window(1, i)
        return rounded(
            right_left(tr * dr + ti * di, tr * di - ti * dr, tabs[3], tabs[2])
        )

    wave_a = first_wave(0)
    desc_a = descent(far_field(0, wave_a))
    put(0, 1, wave_a, desc_a)
    send_pieces(0, 1)
    wave_b = first_wave(1)
    desc_a = first_descent(0, desc_a)
    put(0, 0, load(rolled, 0), desc_a)
    send_pieces(0, 0)
    send_here(0)
    desc_b = descent(far_field(1, wave_b))
    put(1, 1, wave_b, desc_b)
    send_pieces(1, 1)
    put(1, 0, load(rolled, 1), first_descent(1, desc_b))
    send_pieces(1, 0)
    send_here(1)

    row16 = iota((2, 8, WIN), 0) * 8 + iota((2, 8, WIN), 1) + cls * 16
    col8 = iota((8, WIN), 1)

    def add_group(i, g):
        pltpu.make_async_copy(pieces.at[i, g], pieces.at[i, g], piece_sem.at[i, g]).wait()
        rows, cols = places[g, 0], places[g, 1]
        r0 = jnp.minimum(rows >> 8, BANDS - 2)
        c0 = jnp.minimum(cols >> 8, BANDS - 2)
        rm, cm = rows - r0 * WIN, cols - c0 * WIN

        def wide(x, k):
            one = jnp.broadcast_to(x[2 * k + i : 2 * k + i + 1], (8, 128))
            return jnp.concatenate([one, one], axis=1)

        band = [wide(r0, k) + jnp.where(row16 < wide(rm, k), 1, 0) for k in range(4)]
        block = [wide(c0, k) + jnp.where(col8 < wide(cm, k), 1, 0) for k in range(4)]
        for p in range(2):
            piece = [pieces[i, g, k, p].astype(F32).reshape(2, 8, WIN) for k in range(4)]
            for zb in range(BANDS):
                part = [jnp.where(b == zb, x, 0.0) for b, x in zip(band, piece)]
                for cb in range(BANDS):
                    total = acc[zb, p, :, :, cb * WIN : (cb + 1) * WIN]
                    for b, x in zip(block, part):
                        total += jnp.where(b == cb, x, 0.0)
                    acc[zb, p, :, :, cb * WIN : (cb + 1) * WIN] = total

    def add_first(k, carry):
        g = q ^ k ^ (k // 4 * 2)

        @pl.when(k > 0)
        def _():
            places_of(g).wait()

        add_group(0, g)
        return carry

    def add_second(k, carry):
        add_group(1, q ^ k ^ (k // 4 * 2))
        return carry

    lax.fori_loop(0, PLANE, add_first, 0)
    lax.fori_loop(0, PLANE, add_second, 0)

    z_send[...] = acc[...].reshape(BANDS, 2, 16, 1024).astype(BF)

    def z_copy(k):
        there = (z + k) % BANDS
        return pltpu.make_async_remote_copy(
            src_ref=z_send.at[there], dst_ref=z_recv.at[k], send_sem=z_out_sem.at[k],
            recv_sem=z_sem.at[k], device_id=(there * PLANE + q, d, c), device_id_type=MESH,
        )

    for k in (1 + 2 * c, 3 - 2 * c, 2):
        z_copy(k).start()
    total = acc[z].reshape(2, 16, 1024)
    for k in (1, 3, 2):
        z_copy(k).wait_recv()
        total += z_recv[k].astype(F32)
    out[...] = total

    for k in range(1, BANDS):
        z_copy(k).wait_send()
    offs_copy.wait_send()
    probe_copy.wait_send()
    meas_copy.wait_send()
    for i in range(2):
        for half in range(2):
            t_copy(i, half).wait_send()
    for k in range(1, PLANE):
        place_copy(k).wait_send()
    for i in range(2):
        for s, count in ((0, CLS), (1, CLS - 1)):
            sent = grad.at[i, s, pl.ds(0, count)]
            pltpu.make_async_copy(sent, sent, piece_out_sem.at[i, s]).wait()


def per_device(offsets, counts, probe_wave, object_slices, measured):
    smem = pl.BlockSpec(memory_space=pltpu.SMEM)
    anywhere = pl.BlockSpec(memory_space=pl.ANY)
    dma = pltpu.SemaphoreType.DMA
    planes = object_slices.reshape(2, BANDS, WIN, BANDS * WIN)
    operands = (offsets.T, probe_wave, planes, measured, jnp.asarray(tables()))
    grad = pl.pallas_call(
        kernel,
        out_shape=pltpu.VMEM((2, 16, 1024), F32),
        in_specs=[smem] + [anywhere] * 5,
        out_specs=pl.BlockSpec(memory_space=pltpu.VMEM),
        scratch_shapes=[
            pltpu.SMEM((2, CAP), jnp.int32),
            pltpu.SMEM((2, CAP), jnp.int32),
            pltpu.VMEM((BANDS, 2, BANDS, WIN, WIN), F32),
            pltpu.VMEM((4, 2 * WIN, 2 * WIN), BF),
            pltpu.VMEM((2, 2, 2, 2, HALF, WIN), BF),
            pltpu.VMEM((2, 2, 2, HALF, WIN), BF),
            pltpu.VMEM((2, 2, WIN // 2, WIN), BF),
            pltpu.VMEM((2, 2, WIN // 2, WIN), F32),
            pltpu.VMEM((2, 2, WIN, WIN), BF),
            pltpu.VMEM((2, WIN, WIN), F32),
            pltpu.VMEM((2, 2, CLS, 2, 16, WIN), BF),
            pltpu.VMEM((2, PLANE, CAP // 2, 2, 16, WIN), BF),
            pltpu.VMEM((PLANE, 2, CAP, 128), jnp.int32),
            pltpu.VMEM((BANDS, 2, 2, 8, 1024), F32),
            pltpu.VMEM((BANDS, 2, 16, 1024), BF),
            pltpu.VMEM((BANDS, 2, 16, 1024), BF),
            dma((BANDS + 1,)),
            dma((4,)),
            dma,
            dma,
            dma((2, 2)),
            dma((2, 2)),
            dma((2,)),
            dma((PLANE,)),
            dma((PLANE,)),
            dma((2, PLANE)),
            dma((2, 2)),
            dma((BANDS,)),
            dma((BANDS,)),
        ],
        compiler_params=pltpu.CompilerParams(
            collective_id=0, has_side_effects=True, vmem_limit_bytes=40 * 2**20
        ),
        cost_estimate=pl.CostEstimate(
            flops=2 * 16 * 2**27, bytes_accessed=12 * 2**20, transcendentals=0
        ),
    )(counts, *(pltpu.with_memory_space_constraint(a, pltpu.HBM) for a in operands))
    return grad[None]


def solution(mesh):
    in_specs = (
        P("pos", None),
        P("pos"),
        P(None, "det", None),
        P("depth", None, None, None),
        P("pos", "det", None),
    )
    out_specs = P("depth", None, ("pos", "det"), None)
    return jax.shard_map(
        per_device, mesh=mesh, in_specs=in_specs, out_specs=out_specs, check_vma=False
    )
```

```python
import math

import jax
import jax.numpy as jnp
import numpy as np
from jax import lax
from jax.experimental import pallas as pl
from jax.experimental.pallas import tpu as pltpu
from jax.sharding import PartitionSpec as P

PROP_DIV = 2
WIN = 256
HALF = WIN // 2
NEAR = 160
PARTS = ((0, NEAR), (NEAR, WIN - NEAR))
BANDS = 4
PLANE = 8
CAP = 8
CLS = 16
ROUTE = ((1, 0), (3, 0), (0, 1), (2, 0), (1, 1), (3, 1), (2, 1), (0, 0))
MESH = pl.DeviceIdType.MESH
BF = jnp.bfloat16
F32 = jnp.float32


def tables():
    k = np.arange(WIN)
    angle = (k[:, None] * k[None, :] % WIN) * (2.0 * math.pi / WIN)
    cos, sin = np.cos(angle), np.sin(angle)
    f = np.where(k < WIN // 2, k, k - WIN)
    h = np.exp(-1j * math.pi / (PROP_DIV * WIN) * (f * f % (2 * PROP_DIV * WIN)))
    dft = cos - 1j * sin
    q = (np.conj(dft) * h[None, :]) @ dft / WIN
    qr, qi = q.real, q.imag
    out = np.stack(
        [
            np.block([[cos, -sin], [sin, cos]]) / 16,
            np.block([[cos, sin], [-sin, cos]]) / 16,
            np.block([[qr, qi], [-qi, qr]]),
            np.block([[qr, -qi], [qi, qr]]),
        ]
    )
    return out.astype(np.float32).astype(BF)


def dot(a, b):
    return jnp.dot(a, b, preferred_element_type=F32)


def beside(re, im):
    return jnp.concatenate([re.astype(BF), im.astype(BF)], axis=1)


def stacked(re, im):
    return jnp.concatenate([re.astype(BF), im.astype(BF)], axis=0)


def right_left(re, im, right, left):
    mid = dot(beside(re, im), right).astype(BF)
    out = dot(left, jnp.concatenate([mid[:, :WIN], mid[:, WIN:]], axis=0))
    return out[:WIN], out[WIN:]


def left_right(re, im, left, right):
    mid = dot(left, stacked(re, im)).astype(BF)
    out = dot(jnp.concatenate([mid[:WIN], mid[WIN:]], axis=1), right)
    return out[:, :WIN], out[:, WIN:]


def iota(shape, axis):
    return lax.broadcasted_iota(jnp.int32, shape, axis)


def kernel(
    counts, offs_in, probe, obj, measured, tabs_in, out,
    offs, other_offs, obj_v, tabs, t_all, t_send, probe_v, meas, rolled, amps, grad, pieces, places, acc, z_send, z_recv,
    load_sem, own_sem, probe_sem, meas_sem, t_sem, t_out_sem, out_sem, place_sem, place_out_sem,
    piece_sem, piece_out_sem, z_sem, z_out_sem,
):
    pos, d, c = lax.axis_index("pos"), lax.axis_index("depth"), lax.axis_index("det")
    z, q = pos // PLANE, pos % PLANE
    y, x = q // 2, q % 2 * 2 + d
    cls = q * 2 + c
    other = z * PLANE + (q ^ 1)
    own = 2 * (2 * d + c)
    across = 2 * (2 * (1 - d) + c)
    beside_slot = 2 * (2 * d + 1 - c)

    own_offs = pltpu.make_async_copy(offs_in, offs, own_sem.at[3])
    own_offs.start()
    load_obj = []
    for cb in range(BANDS):
        column = obj.at[:, :, :, pl.ds(cb * WIN, WIN)]
        load_obj.append(pltpu.make_async_copy(column, obj_v.at[cb], load_sem.at[cb]))
        load_obj[-1].start()
    barrier = pltpu.get_barrier_semaphore()
    for k in range(1, 2 * CLS):
        pl.semaphore_signal(
            barrier, inc=1,
            device_id=(z * PLANE + (q ^ (k // 4)), d ^ (k // 2 % 2), c ^ (k % 2)),
            device_id_type=MESH,
        )
    for k in range(1, BANDS):
        pl.semaphore_signal(
            barrier, inc=1, device_id=((z + k) % BANDS * PLANE + q, d, c), device_id_type=MESH
        )

    load_tabs = pltpu.make_async_copy(tabs_in, tabs, load_sem.at[BANDS])
    load_tabs.start()
    own_probe = pltpu.make_async_copy(probe, probe_v.at[c], own_sem.at[0])
    own_probe.start()
    own_meas = pltpu.make_async_copy(measured.at[pl.ds(own, 2)], meas.at[c], own_sem.at[1])
    own_meas.start()

    own_offs.wait()
    slot_of = iota((CAP, 128), 0)
    for axis in range(2):
        spread = jnp.zeros((CAP, 128), jnp.int32)
        for s in range(CAP):
            spread = jnp.where(slot_of == s, offs[axis, s], spread)
        places[q, axis] = spread
    acc[...] = jnp.zeros_like(acc)
    pl.semaphore_wait(barrier, 2 * CLS - 1 + BANDS - 1)

    def place_copy(k):
        return pltpu.make_async_remote_copy(
            src_ref=places.at[q], dst_ref=places.at[q], send_sem=place_out_sem.at[k],
            recv_sem=place_sem.at[q], device_id=(z * PLANE + (q ^ k), d, c),
            device_id_type=MESH,
        )

    def places_of(g):
        return pltpu.make_async_copy(places.at[g], places.at[g], place_sem.at[g])

    offs_copy = pltpu.make_async_remote_copy(
        src_ref=offs, dst_ref=other_offs, send_sem=place_out_sem.at[0], recv_sem=own_sem.at[2],
        device_id=(other, d, c), device_id_type=MESH,
    )
    offs_copy.start()

    probe_copy = pltpu.make_async_remote_copy(
        src_ref=probe, dst_ref=probe_v.at[c], send_sem=out_sem.at[0], recv_sem=probe_sem,
        device_id=(pos, d, 1 - c), device_id_type=MESH,
    )
    probe_copy.start()
    meas_copy = pltpu.make_async_remote_copy(
        src_ref=measured.at[pl.ds(beside_slot, 2)], dst_ref=meas.at[c], send_sem=out_sem.at[1],
        recv_sem=meas_sem, device_id=(pos, d, 1 - c), device_id_type=MESH,
    )
    meas_copy.start()

    for column in load_obj:
        column.wait()

    row_of, col_of = iota((WIN, WIN), 0), iota((WIN, WIN), 1)

    def cut(r, col, plane, first, count):
        rows = pl.ds(first, count)
        band = jnp.minimum(r >> 8, BANDS - 2)
        block = jnp.minimum(col >> 8, BANDS - 2)
        late = iota((count, WIN), 1) >= col - block * WIN
        top = jnp.where(
            late, obj_v[block, plane, band, rows], obj_v[block + 1, plane, band, rows]
        )
        low = jnp.where(
            late, obj_v[block, plane, band + 1, rows], obj_v[block + 1, plane, band + 1, rows]
        )
        return jnp.where(iota((count, WIN), 0) >= r - band * WIN - first, top, low).astype(BF)

    def t_copy(i, part):
        rows = pl.ds(*PARTS[part])
        return pltpu.make_async_remote_copy(
            src_ref=t_send.at[i, :, rows], dst_ref=t_all.at[d, i, :, rows],
            send_sem=t_out_sem.at[i, part], recv_sem=t_sem.at[i, part],
            device_id=(other if part else pos, 1 - d, c), device_id_type=MESH,
        )

    def send_part(i, part):
        places_in = other_offs if part else offs
        for plane in range(2):
            t_send[i, plane, pl.ds(*PARTS[part])] = cut(
                places_in[0, across + i], places_in[1, across + i], plane, *PARTS[part]
            )
        t_copy(i, part).start()

    send_part(0, 0)
    offs_copy.wait_recv()
    send_part(0, 1)
    send_part(1, 0)
    send_part(1, 1)

    def window(s, i):
        return [t_all[s, i, p].astype(F32) for p in range(2)]

    def prepare(i):
        for plane in range(2):
            t_all[d, i, plane] = cut(offs[0, own + i], offs[1, own + i], plane, 0, WIN)
        flat = jnp.concatenate(
            [jnp.concatenate([probe_v[0, p], probe_v[1, p]], axis=0) for p in range(2)], axis=1
        )
        r, col = offs[0, own + i], offs[1, own + i]
        down = jnp.where(col_of == ((row_of - r) & (WIN - 1)), 1.0, 0.0).astype(BF)
        over = jnp.where(row_of == ((col_of - col) & (WIN - 1)), 1.0, 0.0).astype(BF)
        moved = dot(down, flat).astype(BF)
        moved = dot(jnp.concatenate([moved[:, :WIN], moved[:, WIN:]], axis=0), over)
        rolled[i, 0], rolled[i, 1] = moved[:WIN].astype(BF), moved[WIN:].astype(BF)
        amps[i] = jnp.concatenate([meas[0, i], meas[1, i]], axis=0).T

    own_probe.wait()
    own_meas.wait()
    probe_copy.wait_recv()
    meas_copy.wait_recv()
    prepare(0)
    load_tabs.wait()

    def send_pieces(i, s):
        odd = (s + d) % 2
        for dy, far in ROUTE:
            yy = (y + dy * (1 + 2 * c)) % 4
            xx = (x + odd + 2 * ((far + c * odd) % 2)) % 4
            for cc in range(2):
                if (dy, far, cc) == (0, 0, 0):
                    continue
                core = c ^ cc
                pltpu.make_async_remote_copy(
                    src_ref=grad.at[i, s, (yy * 2 + xx // 2) * 2 + core],
                    dst_ref=pieces.at[i, q, 2 * d + c],
                    send_sem=piece_out_sem.at[i, s], recv_sem=piece_sem.at[i, q],
                    device_id=(z * PLANE + yy * 2 + xx // 2, s, core), device_id_type=MESH,
                ).start()

    def send_here(i):
        xx = (x + 1 + 2 * c) % 4
        pltpu.make_async_remote_copy(
            src_ref=grad.at[i, 1 - d, (y * 2 + xx // 2) * 2 + c],
            dst_ref=pieces.at[i, q, 2 * d + c],
            send_sem=piece_out_sem.at[i, 0], recv_sem=piece_sem.at[i, q],
            device_id=(z * PLANE + y * 2 + xx // 2, 1 - d, c), device_id_type=MESH,
        ).start()
        pltpu.make_async_copy(
            grad.at[i, d, cls], pieces.at[i, q, 2 * d + c], piece_sem.at[i, q]
        ).start()

    def load(ref, i):
        return ref[i, 0].astype(F32), ref[i, 1].astype(F32)

    def rounded(pair):
        return pair[0].astype(BF).astype(F32), pair[1].astype(BF).astype(F32)

    def first_wave(i):
        for half in range(2):
            t_copy(i, half).wait_recv()
        (pr, pi), (tr, ti) = load(rolled, i), window(0, i)
        return rounded(
            right_left(pr * tr - pi * ti, pr * ti + pi * tr, tabs[2], tabs[3])
        )

    def far_field(i, wave):
        (wr, wi), (tr, ti) = wave, window(1, i)
        fr, fi = right_left(wr * tr - wi * ti, wr * ti + wi * tr, tabs[0], tabs[1])
        used = jnp.where(jnp.full((1, WIN), own + i, jnp.int32) < counts[0], 1.0, 0.0)
        scale = used * (1.0 - amps[i] * lax.rsqrt(jnp.maximum(fr * fr + fi * fi, 1.0)))
        return fr * scale, fi * scale

    def descent(residual):
        return rounded(left_right(residual[0], residual[1], tabs[0], tabs[1]))

    def put(i, s, wave, desc):
        (wr, wi), (dr, di) = wave, desc
        grad[i, s, :, 0] = (wr * dr + wi * di).astype(BF).reshape(CLS, 16, WIN)
        grad[i, s, :, 1] = (wr * di - wi * dr).astype(BF).reshape(CLS, 16, WIN)

    def first_descent(i, desc):
        (dr, di), (tr, ti) = desc, window(1, i)
        return rounded(
            right_left(tr * dr + ti * di, tr * di - ti * dr, tabs[3], tabs[2])
        )

    wave_a = first_wave(0)
    desc_a = descent(far_field(0, wave_a))
    put(0, 1, wave_a, desc_a)
    send_pieces(0, 1)
    for k in range(1, PLANE):
        place_copy(k).start()
    prepare(1)
    wave_b = first_wave(1)
    desc_a = first_descent(0, desc_a)
    put(0, 0, load(rolled, 0), desc_a)
    send_pieces(0, 0)
    send_here(0)
    desc_b = descent(far_field(1, wave_b))
    put(1, 1, wave_b, desc_b)
    send_pieces(1, 1)
    put(1, 0, load(rolled, 1), first_descent(1, desc_b))
    send_pieces(1, 0)
    send_here(1)

    row16 = iota((2, 8, WIN), 0) * 8 + iota((2, 8, WIN), 1) + cls * 16
    col8 = iota((8, WIN), 1)

    def add_group(i, g):
        pltpu.make_async_copy(pieces.at[i, g], pieces.at[i, g], piece_sem.at[i, g]).wait()
        rows, cols = places[g, 0], places[g, 1]
        r0 = jnp.minimum(rows >> 8, BANDS - 2)
        c0 = jnp.minimum(cols >> 8, BANDS - 2)
        rm, cm = rows - r0 * WIN, cols - c0 * WIN

        def wide(x, k):
            one = jnp.broadcast_to(x[2 * k + i : 2 * k + i + 1], (8, 128))
            return jnp.concatenate([one, one], axis=1)

        band = [wide(r0, k) + jnp.where(row16 < wide(rm, k), 1, 0) for k in range(4)]
        block = [wide(c0, k) + jnp.where(col8 < wide(cm, k), 1, 0) for k in range(4)]
        for p in range(2):
            piece = [pieces[i, g, k, p].astype(F32).reshape(2, 8, WIN) for k in range(4)]
            for zb in range(BANDS):
                part = [jnp.where(b == zb, x, 0.0) for b, x in zip(band, piece)]
                for cb in range(BANDS):
                    total = acc[zb, p, :, :, cb * WIN : (cb + 1) * WIN]
                    for b, x in zip(block, part):
                        total += jnp.where(b == cb, x, 0.0)
                    acc[zb, p, :, :, cb * WIN : (cb + 1) * WIN] = total

    def add_first(k, carry):
        g = q ^ k ^ (k // 4 * 2)

        @pl.when(k > 0)
        def _():
            places_of(g).wait()

        add_group(0, g)
        return carry

    def add_second(k, carry):
        add_group(1, q ^ k ^ (k // 4 * 2))
        return carry

    lax.fori_loop(0, PLANE, add_first, 0)
    lax.fori_loop(0, PLANE, add_second, 0)

    z_send[...] = acc[...].reshape(BANDS, 2, 16, 1024).astype(BF)

    def z_copy(k):
        there = (z + k) % BANDS
        return pltpu.make_async_remote_copy(
            src_ref=z_send.at[there], dst_ref=z_recv.at[k], send_sem=z_out_sem.at[k],
            recv_sem=z_sem.at[k], device_id=(there * PLANE + q, d, c), device_id_type=MESH,
        )

    for k in (1 + 2 * c, 3 - 2 * c, 2):
        z_copy(k).start()
    total = acc[z].reshape(2, 16, 1024)
    for k in (1, 3, 2):
        z_copy(k).wait_recv()
        total += z_recv[k].astype(F32)
    out[...] = total

    for k in range(1, BANDS):
        z_copy(k).wait_send()
    offs_copy.wait_send()
    probe_copy.wait_send()
    meas_copy.wait_send()
    for i in range(2):
        for half in range(2):
            t_copy(i, half).wait_send()
    for k in range(1, PLANE):
        place_copy(k).wait_send()
    for i in range(2):
        for s, count in ((0, CLS), (1, CLS - 1)):
            sent = grad.at[i, s, pl.ds(0, count)]
            pltpu.make_async_copy(sent, sent, piece_out_sem.at[i, s]).wait()


def per_device(offsets, counts, probe_wave, object_slices, measured):
    smem = pl.BlockSpec(memory_space=pltpu.SMEM)
    anywhere = pl.BlockSpec(memory_space=pl.ANY)
    dma = pltpu.SemaphoreType.DMA
    planes = object_slices.reshape(2, BANDS, WIN, BANDS * WIN)
    operands = (offsets.T, probe_wave, planes, measured, jnp.asarray(tables()))
    grad = pl.pallas_call(
        kernel,
        out_shape=pltpu.VMEM((2, 16, 1024), F32),
        in_specs=[smem] + [anywhere] * 5,
        out_specs=pl.BlockSpec(memory_space=pltpu.VMEM),
        scratch_shapes=[
            pltpu.SMEM((2, CAP), jnp.int32),
            pltpu.SMEM((2, CAP), jnp.int32),
            pltpu.VMEM((BANDS, 2, BANDS, WIN, WIN), F32),
            pltpu.VMEM((4, 2 * WIN, 2 * WIN), BF),
            pltpu.VMEM((2, 2, 2, WIN, WIN), BF),
            pltpu.VMEM((2, 2, WIN, WIN), BF),
            pltpu.VMEM((2, 2, WIN // 2, WIN), BF),
            pltpu.VMEM((2, 2, WIN // 2, WIN), F32),
            pltpu.VMEM((2, 2, WIN, WIN), BF),
            pltpu.VMEM((2, WIN, WIN), F32),
            pltpu.VMEM((2, 2, CLS, 2, 16, WIN), BF),
            pltpu.VMEM((2, PLANE, CAP // 2, 2, 16, WIN), BF),
            pltpu.VMEM((PLANE, 2, CAP, 128), jnp.int32),
            pltpu.VMEM((BANDS, 2, 2, 8, 1024), F32),
            pltpu.VMEM((BANDS, 2, 16, 1024), BF),
            pltpu.VMEM((BANDS, 2, 16, 1024), BF),
            dma((BANDS + 1,)),
            dma((4,)),
            dma,
            dma,
            dma((2, 2)),
            dma((2, 2)),
            dma((2,)),
            dma((PLANE,)),
            dma((PLANE,)),
            dma((2, PLANE)),
            dma((2, 2)),
            dma((BANDS,)),
            dma((BANDS,)),
        ],
        compiler_params=pltpu.CompilerParams(
            collective_id=0, has_side_effects=True, vmem_limit_bytes=40 * 2**20
        ),
        cost_estimate=pl.CostEstimate(
            flops=2 * 16 * 2**27, bytes_accessed=12 * 2**20, transcendentals=0
        ),
    )(counts, *(pltpu.with_memory_space_constraint(a, pltpu.HBM) for a in operands))
    return grad[None]


def solution(mesh):
    in_specs = (
        P("pos", None),
        P("pos"),
        P(None, "det", None),
        P("depth", None, None, None),
        P("pos", "det", None),
    )
    out_specs = P("depth", None, ("pos", "det"), None)
    return jax.shard_map(
        per_device, mesh=mesh, in_specs=in_specs, out_specs=out_specs, check_vma=False
    )
```

```python
import math

import jax
import jax.numpy as jnp
import numpy as np
from jax import lax
from jax.experimental import pallas as pl
from jax.experimental.pallas import tpu as pltpu
from jax.sharding import PartitionSpec as P

PROP_DIV = 2
WIN = 256
HALF = WIN // 2
NEAR = 160
PARTS = ((0, NEAR), (NEAR, WIN - NEAR))
BANDS = 4
PLANE = 8
CAP = 8
CLS = 16
ROUTE = ((1, 0), (3, 0), (0, 1), (2, 0), (1, 1), (3, 1), (2, 1), (0, 0))
MESH = pl.DeviceIdType.MESH
BF = jnp.bfloat16
F32 = jnp.float32


def tables():
    k = np.arange(WIN)
    angle = (k[:, None] * k[None, :] % WIN) * (2.0 * math.pi / WIN)
    cos, sin = np.cos(angle), np.sin(angle)
    f = np.where(k < WIN // 2, k, k - WIN)
    h = np.exp(-1j * math.pi / (PROP_DIV * WIN) * (f * f % (2 * PROP_DIV * WIN)))
    dft = cos - 1j * sin
    q = (np.conj(dft) * h[None, :]) @ dft / WIN
    qr, qi = q.real, q.imag
    out = np.stack(
        [
            np.block([[cos, -sin], [sin, cos]]) / 16,
            np.block([[cos, sin], [-sin, cos]]) / 16,
            np.block([[qr, qi], [-qi, qr]]),
            np.block([[qr, -qi], [qi, qr]]),
        ]
    )
    return out.astype(np.float32).astype(BF)


def dot(a, b):
    return jnp.dot(a, b, preferred_element_type=F32)


def beside(re, im):
    return jnp.concatenate([re.astype(BF), im.astype(BF)], axis=1)


def stacked(re, im):
    return jnp.concatenate([re.astype(BF), im.astype(BF)], axis=0)


def right_left(re, im, right, left):
    mid = dot(beside(re, im), right).astype(BF)
    out = dot(left, jnp.concatenate([mid[:, :WIN], mid[:, WIN:]], axis=0))
    return out[:WIN], out[WIN:]


def left_right(re, im, left, right):
    mid = dot(left, stacked(re, im)).astype(BF)
    out = dot(jnp.concatenate([mid[:WIN], mid[WIN:]], axis=1), right)
    return out[:, :WIN], out[:, WIN:]


def iota(shape, axis):
    return lax.broadcasted_iota(jnp.int32, shape, axis)


def kernel(
    counts, offs_in, probe, obj, measured, tabs_in, out,
    offs, other_offs, obj_v, tabs, t_all, t_send, probe_v, meas, rolled, amps, grad, pieces, places, acc, z_send, z_recv,
    load_sem, own_sem, probe_sem, meas_sem, t_sem, t_out_sem, out_sem, place_sem, place_out_sem,
    piece_sem, piece_out_sem, z_sem, z_out_sem,
):
    pos, d, c = lax.axis_index("pos"), lax.axis_index("depth"), lax.axis_index("det")
    z, q = pos // PLANE, pos % PLANE
    y, x = q // 2, q % 2 * 2 + d
    cls = q * 2 + c
    other = z * PLANE + (q ^ 1)
    own = 2 * (2 * d + c)
    across = 2 * (2 * (1 - d) + c)
    beside_slot = 2 * (2 * d + 1 - c)

    own_offs = pltpu.make_async_copy(offs_in, offs, own_sem.at[3])
    own_offs.start()
    load_obj = []
    for cb in range(BANDS):
        column = obj.at[:, :, :, pl.ds(cb * WIN, WIN)]
        load_obj.append(pltpu.make_async_copy(column, obj_v.at[cb], load_sem.at[cb]))
        load_obj[-1].start()
    barrier = pltpu.get_barrier_semaphore()
    for k in range(1, 2 * CLS):
        pl.semaphore_signal(
            barrier, inc=1,
            device_id=(z * PLANE + (q ^ (k // 4)), d ^ (k // 2 % 2), c ^ (k % 2)),
            device_id_type=MESH,
        )
    for k in range(1, BANDS):
        pl.semaphore_signal(
            barrier, inc=1, device_id=((z + k) % BANDS * PLANE + q, d, c), device_id_type=MESH
        )

    load_tabs = pltpu.make_async_copy(tabs_in, tabs, load_sem.at[BANDS])
    load_tabs.start()
    own_probe = pltpu.make_async_copy(probe, probe_v.at[c], own_sem.at[0])
    own_probe.start()
    own_meas = pltpu.make_async_copy(measured.at[pl.ds(own, 2)], meas.at[c], own_sem.at[1])
    own_meas.start()

    own_offs.wait()
    slot_of = iota((CAP, 128), 0)
    for axis in range(2):
        spread = jnp.zeros((CAP, 128), jnp.int32)
        for s in range(CAP):
            spread = jnp.where(slot_of == s, offs[axis, s], spread)
        places[q, axis] = spread
    acc[...] = jnp.zeros_like(acc)
    pl.semaphore_wait(barrier, 2 * CLS - 1 + BANDS - 1)

    def place_copy(k):
        return pltpu.make_async_remote_copy(
            src_ref=places.at[q], dst_ref=places.at[q], send_sem=place_out_sem.at[k],
            recv_sem=place_sem.at[q], device_id=(z * PLANE + (q ^ k), d, c),
            device_id_type=MESH,
        )

    def places_of(g):
        return pltpu.make_async_copy(places.at[g], places.at[g], place_sem.at[g])

    offs_copy = pltpu.make_async_remote_copy(
        src_ref=offs, dst_ref=other_offs, send_sem=place_out_sem.at[0], recv_sem=own_sem.at[2],
        device_id=(other, d, c), device_id_type=MESH,
    )
    offs_copy.start()

    probe_copy = pltpu.make_async_remote_copy(
        src_ref=probe, dst_ref=probe_v.at[c], send_sem=out_sem.at[0], recv_sem=probe_sem,
        device_id=(pos, d, 1 - c), device_id_type=MESH,
    )
    probe_copy.start()
    meas_copy = pltpu.make_async_remote_copy(
        src_ref=measured.at[pl.ds(beside_slot, 2)], dst_ref=meas.at[c], send_sem=out_sem.at[1],
        recv_sem=meas_sem, device_id=(pos, d, 1 - c), device_id_type=MESH,
    )
    meas_copy.start()

    for column in load_obj:
        column.wait()

    row_of, col_of = iota((WIN, WIN), 0), iota((WIN, WIN), 1)

    def cut(r, col, plane, first, count):
        rows = pl.ds(first, count)
        band = jnp.minimum(r >> 8, BANDS - 2)
        block = jnp.minimum(col >> 8, BANDS - 2)
        late = iota((count, WIN), 1) >= col - block * WIN
        top = jnp.where(
            late, obj_v[block, plane, band, rows], obj_v[block + 1, plane, band, rows]
        )
        low = jnp.where(
            late, obj_v[block, plane, band + 1, rows], obj_v[block + 1, plane, band + 1, rows]
        )
        return jnp.where(iota((count, WIN), 0) >= r - band * WIN - first, top, low).astype(BF)

    def t_copy(i, part):
        rows = pl.ds(*PARTS[part])
        return pltpu.make_async_remote_copy(
            src_ref=t_send.at[i, :, rows], dst_ref=t_all.at[d, i, :, rows],
            send_sem=t_out_sem.at[i, part], recv_sem=t_sem.at[i, part],
            device_id=(other if part else pos, 1 - d, c), device_id_type=MESH,
        )

    def send_part(i, part):
        places_in = other_offs if part else offs
        for plane in range(2):
            t_send[i, plane, pl.ds(*PARTS[part])] = cut(
                places_in[0, across + i], places_in[1, across + i], plane, *PARTS[part]
            )
        t_copy(i, part).start()

    send_part(0, 0)
    offs_copy.wait_recv()
    send_part(0, 1)
    send_part(1, 0)
    send_part(1, 1)

    def window(s, i):
        return [t_all[s, i, p].astype(F32) for p in range(2)]

    def prepare(i):
        for plane in range(2):
            t_all[d, i, plane] = cut(offs[0, own + i], offs[1, own + i], plane, 0, WIN)
        flat = jnp.concatenate(
            [jnp.concatenate([probe_v[0, p], probe_v[1, p]], axis=0) for p in range(2)], axis=1
        )
        r, col = offs[0, own + i], offs[1, own + i]
        down = jnp.where(col_of == ((row_of - r) & (WIN - 1)), 1.0, 0.0).astype(BF)
        over = jnp.where(row_of == ((col_of - col) & (WIN - 1)), 1.0, 0.0).astype(BF)
        moved = dot(down, flat).astype(BF)
        moved = dot(jnp.concatenate([moved[:, :WIN], moved[:, WIN:]], axis=0), over)
        rolled[i, 0], rolled[i, 1] = moved[:WIN].astype(BF), moved[WIN:].astype(BF)
        amps[i] = jnp.concatenate([meas[0, i], meas[1, i]], axis=0).T

    own_probe.wait()
    own_meas.wait()
    probe_copy.wait_recv()
    meas_copy.wait_recv()
    prepare(0)
    prepare(1)
    for k in range(1, PLANE):
        place_copy(k).start()
    load_tabs.wait()

    def send_pieces(i, s):
        odd = (s + d) % 2
        for dy, far in ROUTE:
            yy = (y + dy * (1 + 2 * c)) % 4
            xx = (x + odd + 2 * ((far + c * odd) % 2)) % 4
            for cc in range(2):
                if (dy, far, cc) == (0, 0, 0):
                    continue
                core = c ^ cc
                pltpu.make_async_remote_copy(
                    src_ref=grad.at[i, s, (yy * 2 + xx // 2) * 2 + core],
                    dst_ref=pieces.at[i, q, 2 * d + c],
                    send_sem=piece_out_sem.at[i, s], recv_sem=piece_sem.at[i, q],
                    device_id=(z * PLANE + yy * 2 + xx // 2, s, core), device_id_type=MESH,
                ).start()

    def send_here(i):
        xx = (x + 1 + 2 * c) % 4
        pltpu.make_async_remote_copy(
            src_ref=grad.at[i, 1 - d, (y * 2 + xx // 2) * 2 + c],
            dst_ref=pieces.at[i, q, 2 * d + c],
            send_sem=piece_out_sem.at[i, 0], recv_sem=piece_sem.at[i, q],
            device_id=(z * PLANE + y * 2 + xx // 2, 1 - d, c), device_id_type=MESH,
        ).start()
        pltpu.make_async_copy(
            grad.at[i, d, cls], pieces.at[i, q, 2 * d + c], piece_sem.at[i, q]
        ).start()

    def load(ref, i):
        return ref[i, 0].astype(F32), ref[i, 1].astype(F32)

    def rounded(pair):
        return pair[0].astype(BF).astype(F32), pair[1].astype(BF).astype(F32)

    def first_wave(i):
        for half in range(2):
            t_copy(i, half).wait_recv()
        (pr, pi), (tr, ti) = load(rolled, i), window(0, i)
        return rounded(
            right_left(pr * tr - pi * ti, pr * ti + pi * tr, tabs[2], tabs[3])
        )

    def far_field(i, wave):
        (wr, wi), (tr, ti) = wave, window(1, i)
        fr, fi = right_left(wr * tr - wi * ti, wr * ti + wi * tr, tabs[0], tabs[1])
        used = jnp.where(jnp.full((1, WIN), own + i, jnp.int32) < counts[0], 1.0, 0.0)
        scale = used * (1.0 - amps[i] * lax.rsqrt(jnp.maximum(fr * fr + fi * fi, 1.0)))
        return fr * scale, fi * scale

    def descent(residual):
        return rounded(left_right(residual[0], residual[1], tabs[0], tabs[1]))

    def put(i, s, wave, desc):
        (wr, wi), (dr, di) = wave, desc
        grad[i, s, :, 0] = (wr * dr + wi * di).astype(BF).reshape(CLS, 16, WIN)
        grad[i, s, :, 1] = (wr * di - wi * dr).astype(BF).reshape(CLS, 16, WIN)

    def first_descent(i, desc):
        (dr, di), (tr, ti) = desc, window(1, i)
        return rounded(
            right_left(tr * dr + ti * di, tr * di - ti * dr, tabs[3], tabs[2])
        )

    wave_a = first_wave(0)
    desc_a = descent(far_field(0, wave_a))
    put(0, 1, wave_a, desc_a)
    send_pieces(0, 1)
    wave_b = first_wave(1)
    desc_a = first_descent(0, desc_a)
    put(0, 0, load(rolled, 0), desc_a)
    send_pieces(0, 0)
    send_here(0)
    desc_b = descent(far_field(1, wave_b))
    put(1, 1, wave_b, desc_b)
    put(1, 0, load(rolled, 1), first_descent(1, desc_b))
    send_pieces(1, 0)
    send_here(1)
    send_pieces(1, 1)

    row16 = iota((2, 8, WIN), 0) * 8 + iota((2, 8, WIN), 1) + cls * 16
    col8 = iota((8, WIN), 1)

    def add_group(i, g):
        pltpu.make_async_copy(pieces.at[i, g], pieces.at[i, g], piece_sem.at[i, g]).wait()
        rows, cols = places[g, 0], places[g, 1]
        r0 = jnp.minimum(rows >> 8, BANDS - 2)
        c0 = jnp.minimum(cols >> 8, BANDS - 2)
        rm, cm = rows - r0 * WIN, cols - c0 * WIN

        def wide(x, k):
            one = jnp.broadcast_to(x[2 * k + i : 2 * k + i + 1], (8, 128))
            return jnp.concatenate([one, one], axis=1)

        band = [wide(r0, k) + jnp.where(row16 < wide(rm, k), 1, 0) for k in range(4)]
        block = [wide(c0, k) + jnp.where(col8 < wide(cm, k), 1, 0) for k in range(4)]
        for p in range(2):
            piece = [pieces[i, g, k, p].astype(F32).reshape(2, 8, WIN) for k in range(4)]
            for zb in range(BANDS):
                part = [jnp.where(b == zb, x, 0.0) for b, x in zip(band, piece)]
                for cb in range(BANDS):
                    total = acc[zb, p, :, :, cb * WIN : (cb + 1) * WIN]
                    for b, x in zip(block, part):
                        total += jnp.where(b == cb, x, 0.0)
                    acc[zb, p, :, :, cb * WIN : (cb + 1) * WIN] = total

    def add_first(k, carry):
        g = q ^ k ^ (k // 4 * 2)

        @pl.when(k > 0)
        def _():
            places_of(g).wait()

        add_group(0, g)
        return carry

    def add_second(k, carry):
        add_group(1, q ^ k ^ (k // 4 * 2))
        return carry

    lax.fori_loop(0, PLANE, add_first, 0)
    lax.fori_loop(0, PLANE, add_second, 0)

    z_send[...] = acc[...].reshape(BANDS, 2, 16, 1024).astype(BF)

    def z_copy(k):
        there = (z + k) % BANDS
        return pltpu.make_async_remote_copy(
            src_ref=z_send.at[there], dst_ref=z_recv.at[k], send_sem=z_out_sem.at[k],
            recv_sem=z_sem.at[k], device_id=(there * PLANE + q, d, c), device_id_type=MESH,
        )

    for k in (1 + 2 * c, 3 - 2 * c, 2):
        z_copy(k).start()
    total = acc[z].reshape(2, 16, 1024)
    for k in (1, 3, 2):
        z_copy(k).wait_recv()
        total += z_recv[k].astype(F32)
    out[...] = total

    for k in range(1, BANDS):
        z_copy(k).wait_send()
    offs_copy.wait_send()
    probe_copy.wait_send()
    meas_copy.wait_send()
    for i in range(2):
        for half in range(2):
            t_copy(i, half).wait_send()
    for k in range(1, PLANE):
        place_copy(k).wait_send()
    for i in range(2):
        for s, count in ((0, CLS), (1, CLS - 1)):
            sent = grad.at[i, s, pl.ds(0, count)]
            pltpu.make_async_copy(sent, sent, piece_out_sem.at[i, s]).wait()


def per_device(offsets, counts, probe_wave, object_slices, measured):
    smem = pl.BlockSpec(memory_space=pltpu.SMEM)
    anywhere = pl.BlockSpec(memory_space=pl.ANY)
    dma = pltpu.SemaphoreType.DMA
    planes = object_slices.reshape(2, BANDS, WIN, BANDS * WIN)
    operands = (offsets.T, probe_wave, planes, measured, jnp.asarray(tables()))
    grad = pl.pallas_call(
        kernel,
        out_shape=pltpu.VMEM((2, 16, 1024), F32),
        in_specs=[smem] + [anywhere] * 5,
        out_specs=pl.BlockSpec(memory_space=pltpu.VMEM),
        scratch_shapes=[
            pltpu.SMEM((2, CAP), jnp.int32),
            pltpu.SMEM((2, CAP), jnp.int32),
            pltpu.VMEM((BANDS, 2, BANDS, WIN, WIN), F32),
            pltpu.VMEM((4, 2 * WIN, 2 * WIN), BF),
            pltpu.VMEM((2, 2, 2, WIN, WIN), BF),
            pltpu.VMEM((2, 2, WIN, WIN), BF),
            pltpu.VMEM((2, 2, WIN // 2, WIN), BF),
            pltpu.VMEM((2, 2, WIN // 2, WIN), F32),
            pltpu.VMEM((2, 2, WIN, WIN), BF),
            pltpu.VMEM((2, WIN, WIN), F32),
            pltpu.VMEM((2, 2, CLS, 2, 16, WIN), BF),
            pltpu.VMEM((2, PLANE, CAP // 2, 2, 16, WIN), BF),
            pltpu.VMEM((PLANE, 2, CAP, 128), jnp.int32),
            pltpu.VMEM((BANDS, 2, 2, 8, 1024), F32),
            pltpu.VMEM((BANDS, 2, 16, 1024), BF),
            pltpu.VMEM((BANDS, 2, 16, 1024), BF),
            dma((BANDS + 1,)),
            dma((4,)),
            dma,
            dma,
            dma((2, 2)),
            dma((2, 2)),
            dma((2,)),
            dma((PLANE,)),
            dma((PLANE,)),
            dma((2, PLANE)),
            dma((2, 2)),
            dma((BANDS,)),
            dma((BANDS,)),
        ],
        compiler_params=pltpu.CompilerParams(
            collective_id=0, has_side_effects=True, vmem_limit_bytes=40 * 2**20
        ),
        cost_estimate=pl.CostEstimate(
            flops=2 * 16 * 2**27, bytes_accessed=12 * 2**20, transcendentals=0
        ),
    )(counts, *(pltpu.with_memory_space_constraint(a, pltpu.HBM) for a in operands))
    return grad[None]


def solution(mesh):
    in_specs = (
        P("pos", None),
        P("pos"),
        P(None, "det", None),
        P("depth", None, None, None),
        P("pos", "det", None),
    )
    out_specs = P("depth", None, ("pos", "det"), None)
    return jax.shard_map(
        per_device, mesh=mesh, in_specs=in_specs, out_specs=out_specs, check_vma=False
    )
```

```python
import math

import jax
import jax.numpy as jnp
import numpy as np
from jax import lax
from jax.experimental import pallas as pl
from jax.experimental.pallas import tpu as pltpu
from jax.sharding import PartitionSpec as P

PROP_DIV = 2
WIN = 256
HALF = WIN // 2
BANDS = 4
PLANE = 8
CAP = 8
CLS = 16
ROUTE = ((1, 0), (3, 0), (0, 1), (2, 0), (1, 1), (3, 1), (2, 1), (0, 0))
MESH = pl.DeviceIdType.MESH
BF = jnp.bfloat16
F32 = jnp.float32


def tables():
    k = np.arange(WIN)
    angle = (k[:, None] * k[None, :] % WIN) * (2.0 * math.pi / WIN)
    cos, sin = np.cos(angle), np.sin(angle)
    f = np.where(k < WIN // 2, k, k - WIN)
    h = np.exp(-1j * math.pi / (PROP_DIV * WIN) * (f * f % (2 * PROP_DIV * WIN)))
    dft = cos - 1j * sin
    q = (np.conj(dft) * h[None, :]) @ dft / WIN
    qr, qi = q.real, q.imag
    out = np.stack(
        [
            np.block([[cos, -sin], [sin, cos]]) / 16,
            np.block([[cos, sin], [-sin, cos]]) / 16,
            np.block([[qr, qi], [-qi, qr]]),
            np.block([[qr, -qi], [qi, qr]]),
        ]
    )
    return out.astype(np.float32).astype(BF)


def dot(a, b):
    return jnp.dot(a, b, preferred_element_type=F32)


def beside(re, im):
    return jnp.concatenate([re.astype(BF), im.astype(BF)], axis=1)


def stacked(re, im):
    return jnp.concatenate([re.astype(BF), im.astype(BF)], axis=0)


def right_left(re, im, right, left):
    mid = dot(beside(re, im), right).astype(BF)
    out = dot(left, jnp.concatenate([mid[:, :WIN], mid[:, WIN:]], axis=0))
    return out[:WIN], out[WIN:]


def left_right(re, im, left, right):
    mid = dot(left, stacked(re, im)).astype(BF)
    out = dot(jnp.concatenate([mid[:WIN], mid[WIN:]], axis=1), right)
    return out[:, :WIN], out[:, WIN:]


def iota(shape, axis):
    return lax.broadcasted_iota(jnp.int32, shape, axis)


def kernel(
    counts, offs_in, probe, obj, measured, tabs_in, out,
    offs, other_offs, obj_v, tabs, t_all, t_send, probe_v, meas, rolled, amps, grad, pieces, places, acc, z_send, z_recv,
    load_sem, own_sem, probe_sem, meas_sem, t_sem, t_out_sem, out_sem, place_sem, place_out_sem,
    piece_sem, piece_out_sem, z_sem, z_out_sem,
):
    pos, d, c = lax.axis_index("pos"), lax.axis_index("depth"), lax.axis_index("det")
    z, q = pos // PLANE, pos % PLANE
    y, x = q // 2, q % 2 * 2 + d
    first_of_plane = z * PLANE
    cls = q * 2 + c
    other = z * PLANE + (q ^ 1)
    own = 2 * (2 * d + c)
    across = 2 * (2 * (1 - d) + c)
    beside_slot = 2 * (2 * d + 1 - c)

    own_offs = pltpu.make_async_copy(offs_in, offs, own_sem.at[3])
    own_offs.start()
    load_obj = []
    for cb in range(BANDS):
        column = obj.at[:, :, :, pl.ds(cb * WIN, WIN)]
        load_obj.append(pltpu.make_async_copy(column, obj_v.at[cb], load_sem.at[cb]))
        load_obj[-1].start()
    barrier = pltpu.get_barrier_semaphore()
    for k in range(1, 2 * CLS):
        pl.semaphore_signal(
            barrier, inc=1,
            device_id=(z * PLANE + (q ^ (k // 4)), d ^ (k // 2 % 2), c ^ (k % 2)),
            device_id_type=MESH,
        )
    for k in range(1, BANDS):
        pl.semaphore_signal(
            barrier, inc=1, device_id=((z + k) % BANDS * PLANE + q, d, c), device_id_type=MESH
        )

    load_tabs = pltpu.make_async_copy(tabs_in, tabs, load_sem.at[BANDS])
    load_tabs.start()
    own_probe = pltpu.make_async_copy(probe, probe_v.at[c], own_sem.at[0])
    own_probe.start()
    own_meas = pltpu.make_async_copy(measured.at[pl.ds(own, 2)], meas.at[c], own_sem.at[1])
    own_meas.start()

    own_offs.wait()
    slot_of = iota((CAP, 128), 0)
    for axis in range(2):
        spread = jnp.zeros((CAP, 128), jnp.int32)
        for s in range(CAP):
            spread = jnp.where(slot_of == s, offs[axis, s], spread)
        places[q, axis] = spread
    acc[...] = jnp.zeros_like(acc)
    pl.semaphore_wait(barrier, 2 * CLS - 1 + BANDS - 1)

    def place_copy(k):
        return pltpu.make_async_remote_copy(
            src_ref=places.at[q], dst_ref=places.at[q], send_sem=place_out_sem.at[k],
            recv_sem=place_sem.at[q], device_id=(z * PLANE + (q ^ k), d, c),
            device_id_type=MESH,
        )

    def places_of(g):
        return pltpu.make_async_copy(places.at[g], places.at[g], place_sem.at[g])

    offs_copy = pltpu.make_async_remote_copy(
        src_ref=offs, dst_ref=other_offs, send_sem=place_out_sem.at[0], recv_sem=own_sem.at[2],
        device_id=(other, d, c), device_id_type=MESH,
    )
    offs_copy.start()

    probe_copy = pltpu.make_async_remote_copy(
        src_ref=probe, dst_ref=probe_v.at[c], send_sem=out_sem.at[0], recv_sem=probe_sem,
        device_id=(pos, d, 1 - c), device_id_type=MESH,
    )
    probe_copy.start()
    meas_copy = pltpu.make_async_remote_copy(
        src_ref=measured.at[pl.ds(beside_slot, 2)], dst_ref=meas.at[c], send_sem=out_sem.at[1],
        recv_sem=meas_sem, device_id=(pos, d, 1 - c), device_id_type=MESH,
    )
    meas_copy.start()

    for column in load_obj:
        column.wait()

    row_of, col_of = iota((WIN, WIN), 0), iota((WIN, WIN), 1)

    half_row = iota((HALF, WIN), 0)
    half_col = iota((HALF, WIN), 1)

    def cut(r, col, half, plane):
        rows = pl.ds(half * HALF, HALF)
        band = jnp.minimum(r >> 8, BANDS - 2)
        block = jnp.minimum(col >> 8, BANDS - 2)
        late = half_col >= col - block * WIN
        top = jnp.where(
            late, obj_v[block, plane, band, rows], obj_v[block + 1, plane, band, rows]
        )
        low = jnp.where(
            late, obj_v[block, plane, band + 1, rows], obj_v[block + 1, plane, band + 1, rows]
        )
        return jnp.where(half_row >= r - band * WIN - half * HALF, top, low).astype(BF)

    def t_copy(i, half):
        there = pos + half * (other - pos)
        return pltpu.make_async_remote_copy(
            src_ref=t_send.at[i, half], dst_ref=t_all.at[d, i, half],
            send_sem=t_out_sem.at[i, half], recv_sem=t_sem.at[i, half],
            device_id=(there, 1 - d, c), device_id_type=MESH,
        )

    def send_near(i):
        for plane in range(2):
            t_send[i, 0, plane] = cut(offs[0, across + i], offs[1, across + i], 0, plane)
        t_copy(i, 0).start()

    def send_far(i):
        for plane in range(2):
            t_send[i, 1, plane] = cut(
                other_offs[0, across + i], other_offs[1, across + i], 1, plane
            )
        t_copy(i, 1).start()

    send_near(0)
    offs_copy.wait_recv()
    send_far(0)
    send_near(1)
    send_far(1)
    for k in range(1, PLANE):
        place_copy(k).start()

    def cut_own(i, carry):
        for half in range(2):
            for plane in range(2):
                t_all[d, i, half, plane] = cut(
                    offs[0, own + i], offs[1, own + i], half, plane
                )
        return carry

    lax.fori_loop(0, 2, cut_own, 0)

    def window(s, i):
        return [
            jnp.concatenate([t_all[s, i, 0, p], t_all[s, i, 1, p]], axis=0).astype(F32)
            for p in range(2)
        ]

    own_probe.wait()
    own_meas.wait()
    probe_copy.wait_recv()
    meas_copy.wait_recv()

    flat = jnp.concatenate(
        [jnp.concatenate([probe_v[0, p], probe_v[1, p]], axis=0) for p in range(2)], axis=1
    )
    for i in range(2):
        r, col = offs[0, own + i], offs[1, own + i]
        down = jnp.where(col_of == ((row_of - r) & (WIN - 1)), 1.0, 0.0).astype(BF)
        over = jnp.where(row_of == ((col_of - col) & (WIN - 1)), 1.0, 0.0).astype(BF)
        moved = dot(down, flat).astype(BF)
        moved = dot(jnp.concatenate([moved[:, :WIN], moved[:, WIN:]], axis=0), over)
        rolled[i, 0], rolled[i, 1] = moved[:WIN].astype(BF), moved[WIN:].astype(BF)
        amps[i] = jnp.concatenate([meas[0, i], meas[1, i]], axis=0).T
    load_tabs.wait()

    def send_pieces(i, s):
        odd = d ^ s
        flip = c & odd
        for dy, far in ROUTE:
            yy = (y + (dy if dy % 2 == 0 else dy + 2 * c)) & 3
            xh = ((x + odd + 2 * (far ^ flip)) & 3) >> 1
            group = yy * 2 + xh
            for cc in range(2):
                if (dy, far, cc) == (0, 0, 0):
                    continue
                core = c ^ cc
                pltpu.make_async_remote_copy(
                    src_ref=grad.at[i, s, group * 2 + core],
                    dst_ref=pieces.at[i, q, 2 * d + c],
                    send_sem=piece_out_sem.at[i, s], recv_sem=piece_sem.at[i, q],
                    device_id=(first_of_plane + group, s, core), device_id_type=MESH,
                ).start()

    def send_here(i):
        xx = (x + 1 + 2 * c) % 4
        pltpu.make_async_remote_copy(
            src_ref=grad.at[i, 1 - d, (y * 2 + xx // 2) * 2 + c],
            dst_ref=pieces.at[i, q, 2 * d + c],
            send_sem=piece_out_sem.at[i, 0], recv_sem=piece_sem.at[i, q],
            device_id=(z * PLANE + y * 2 + xx // 2, 1 - d, c), device_id_type=MESH,
        ).start()
        pltpu.make_async_copy(
            grad.at[i, d, cls], pieces.at[i, q, 2 * d + c], piece_sem.at[i, q]
        ).start()

    def load(ref, i):
        return ref[i, 0].astype(F32), ref[i, 1].astype(F32)

    def rounded(pair):
        return pair[0].astype(BF).astype(F32), pair[1].astype(BF).astype(F32)

    def first_wave(i):
        for half in range(2):
            t_copy(i, half).wait_recv()
        (pr, pi), (tr, ti) = load(rolled, i), window(0, i)
        return rounded(
            right_left(pr * tr - pi * ti, pr * ti + pi * tr, tabs[2], tabs[3])
        )

    def far_field(i, wave):
        (wr, wi), (tr, ti) = wave, window(1, i)
        fr, fi = right_left(wr * tr - wi * ti, wr * ti + wi * tr, tabs[0], tabs[1])
        used = jnp.where(jnp.full((1, WIN), own + i, jnp.int32) < counts[0], 1.0, 0.0)
        scale = used * (1.0 - amps[i] * lax.rsqrt(jnp.maximum(fr * fr + fi * fi, 1.0)))
        return fr * scale, fi * scale

    def descent(residual):
        return rounded(left_right(residual[0], residual[1], tabs[0], tabs[1]))

    def put(i, s, wave, desc):
        (wr, wi), (dr, di) = wave, desc
        grad[i, s, :, 0] = (wr * dr + wi * di).astype(BF).reshape(CLS, 16, WIN)
        grad[i, s, :, 1] = (wr * di - wi * dr).astype(BF).reshape(CLS, 16, WIN)

    def first_descent(i, desc):
        (dr, di), (tr, ti) = desc, window(1, i)
        return rounded(
            right_left(tr * dr + ti * di, tr * di - ti * dr, tabs[3], tabs[2])
        )

    wave_a = first_wave(0)
    desc_a = descent(far_field(0, wave_a))
    put(0, 1, wave_a, desc_a)
    send_pieces(0, 1)
    wave_b = first_wave(1)
    desc_a = first_descent(0, desc_a)
    put(0, 0, load(rolled, 0), desc_a)
    send_pieces(0, 0)
    send_here(0)
    desc_b = descent(far_field(1, wave_b))
    put(1, 1, wave_b, desc_b)
    send_pieces(1, 1)
    put(1, 0, load(rolled, 1), first_descent(1, desc_b))
    send_pieces(1, 0)
    send_here(1)

    row16 = iota((2, 8, WIN), 0) * 8 + iota((2, 8, WIN), 1) + cls * 16
    col8 = iota((8, WIN), 1)

    def add_group(i, g):
        pltpu.make_async_copy(pieces.at[i, g], pieces.at[i, g], piece_sem.at[i, g]).wait()
        rows, cols = places[g, 0], places[g, 1]
        r0 = jnp.minimum(rows >> 8, BANDS - 2)
        c0 = jnp.minimum(cols >> 8, BANDS - 2)
        rm, cm = rows - r0 * WIN, cols - c0 * WIN

        def wide(x, k):
            one = jnp.broadcast_to(x[2 * k + i : 2 * k + i + 1], (8, 128))
            return jnp.concatenate([one, one], axis=1)

        band = [wide(r0, k) + jnp.where(row16 < wide(rm, k), 1, 0) for k in range(4)]
        block = [wide(c0, k) + jnp.where(col8 < wide(cm, k), 1, 0) for k in range(4)]
        for p in range(2):
            piece = [pieces[i, g, k, p].astype(F32).reshape(2, 8, WIN) for k in range(4)]
            for zb in range(BANDS):
                part = [jnp.where(b == zb, x, 0.0) for b, x in zip(band, piece)]
                for cb in range(BANDS):
                    total = acc[zb, p, :, :, cb * WIN : (cb + 1) * WIN]
                    for b, x in zip(block, part):
                        total += jnp.where(b == cb, x, 0.0)
                    acc[zb, p, :, :, cb * WIN : (cb + 1) * WIN] = total

    def add_first(k, carry):
        g = q ^ k ^ (k // 4 * 2)

        @pl.when(k > 0)
        def _():
            places_of(g).wait()

        add_group(0, g)
        return carry

    def add_second(k, carry):
        add_group(1, q ^ k ^ (k // 4 * 2))
        return carry

    lax.fori_loop(0, PLANE, add_first, 0)
    lax.fori_loop(0, PLANE, add_second, 0)

    z_send[...] = acc[...].reshape(BANDS, 2, 16, 1024).astype(BF)

    def z_copy(k):
        there = (z + k) % BANDS
        return pltpu.make_async_remote_copy(
            src_ref=z_send.at[there], dst_ref=z_recv.at[k], send_sem=z_out_sem.at[k],
            recv_sem=z_sem.at[k], device_id=(there * PLANE + q, d, c), device_id_type=MESH,
        )

    for k in (1 + c, 2 - c, 3):
        z_copy(k).start()
    total = acc[z].reshape(2, 16, 1024)
    for k in (3, 2, 1):
        z_copy(k).wait_recv()
        total += z_recv[k].astype(F32)
    out[...] = total

    for k in range(1, BANDS):
        z_copy(k).wait_send()
    offs_copy.wait_send()
    probe_copy.wait_send()
    meas_copy.wait_send()
    for i in range(2):
        for half in range(2):
            t_copy(i, half).wait_send()
    for k in range(1, PLANE):
        place_copy(k).wait_send()
    for i in range(2):
        for s, count in ((0, CLS), (1, CLS - 1)):
            sent = grad.at[i, s, pl.ds(0, count)]
            pltpu.make_async_copy(sent, sent, piece_out_sem.at[i, s]).wait()


def per_device(offsets, counts, probe_wave, object_slices, measured):
    smem = pl.BlockSpec(memory_space=pltpu.SMEM)
    anywhere = pl.BlockSpec(memory_space=pl.ANY)
    dma = pltpu.SemaphoreType.DMA
    planes = object_slices.reshape(2, BANDS, WIN, BANDS * WIN)
    operands = (offsets.T, probe_wave, planes, measured, jnp.asarray(tables()))
    grad = pl.pallas_call(
        kernel,
        out_shape=pltpu.VMEM((2, 16, 1024), F32),
        in_specs=[smem] + [anywhere] * 5,
        out_specs=pl.BlockSpec(memory_space=pltpu.VMEM),
        scratch_shapes=[
            pltpu.SMEM((2, CAP), jnp.int32),
            pltpu.SMEM((2, CAP), jnp.int32),
            pltpu.VMEM((BANDS, 2, BANDS, WIN, WIN), F32),
            pltpu.VMEM((4, 2 * WIN, 2 * WIN), BF),
            pltpu.VMEM((2, 2, 2, 2, HALF, WIN), BF),
            pltpu.VMEM((2, 2, 2, HALF, WIN), BF),
            pltpu.VMEM((2, 2, WIN // 2, WIN), BF),
            pltpu.VMEM((2, 2, WIN // 2, WIN), F32),
            pltpu.VMEM((2, 2, WIN, WIN), BF),
            pltpu.VMEM((2, WIN, WIN), F32),
            pltpu.VMEM((2, 2, CLS, 2, 16, WIN), BF),
            pltpu.VMEM((2, PLANE, CAP // 2, 2, 16, WIN), BF),
            pltpu.VMEM((PLANE, 2, CAP, 128), jnp.int32),
            pltpu.VMEM((BANDS, 2, 2, 8, 1024), F32),
            pltpu.VMEM((BANDS, 2, 16, 1024), BF),
            pltpu.VMEM((BANDS, 2, 16, 1024), BF),
            dma((BANDS + 1,)),
            dma((4,)),
            dma,
            dma,
            dma((2, 2)),
            dma((2, 2)),
            dma((2,)),
            dma((PLANE,)),
            dma((PLANE,)),
            dma((2, PLANE)),
            dma((2, 2)),
            dma((BANDS,)),
            dma((BANDS,)),
        ],
        compiler_params=pltpu.CompilerParams(
            collective_id=0, has_side_effects=True, vmem_limit_bytes=40 * 2**20
        ),
        cost_estimate=pl.CostEstimate(
            flops=2 * 16 * 2**27, bytes_accessed=12 * 2**20, transcendentals=0
        ),
    )(counts, *(pltpu.with_memory_space_constraint(a, pltpu.HBM) for a in operands))
    return grad[None]


def solution(mesh):
    in_specs = (
        P("pos", None),
        P("pos"),
        P(None, "det", None),
        P("depth", None, None, None),
        P("pos", "det", None),
    )
    out_specs = P("depth", None, ("pos", "det"), None)
    return jax.shard_map(
        per_device, mesh=mesh, in_specs=in_specs, out_specs=out_specs, check_vma=False
    )
```

```python
import math

import jax
import jax.numpy as jnp
import numpy as np
from jax import lax
from jax.experimental import pallas as pl
from jax.experimental.pallas import tpu as pltpu
from jax.sharding import PartitionSpec as P

PROP_DIV = 2
WIN = 256
HALF = WIN // 2
NEAR = 160
PARTS = ((0, NEAR), (NEAR, WIN - NEAR))
BANDS = 4
PLANE = 8
CAP = 8
CLS = 16
ROUTE = ((1, 0), (3, 0), (0, 1), (2, 0), (1, 1), (3, 1), (2, 1), (0, 0))
MESH = pl.DeviceIdType.MESH
BF = jnp.bfloat16
F32 = jnp.float32


def tables():
    k = np.arange(WIN)
    angle = (k[:, None] * k[None, :] % WIN) * (2.0 * math.pi / WIN)
    cos, sin = np.cos(angle), np.sin(angle)
    f = np.where(k < WIN // 2, k, k - WIN)
    h = np.exp(-1j * math.pi / (PROP_DIV * WIN) * (f * f % (2 * PROP_DIV * WIN)))
    dft = cos - 1j * sin
    q = (np.conj(dft) * h[None, :]) @ dft / WIN
    qr, qi = q.real, q.imag
    out = np.stack(
        [
            np.block([[cos, -sin], [sin, cos]]) / 16,
            np.block([[cos, sin], [-sin, cos]]) / 16,
            np.block([[qr, qi], [-qi, qr]]),
            np.block([[qr, -qi], [qi, qr]]),
        ]
    )
    return out.astype(np.float32).astype(BF)


def dot(a, b):
    return jnp.dot(a, b, preferred_element_type=F32)


def beside(re, im):
    return jnp.concatenate([re.astype(BF), im.astype(BF)], axis=1)


def stacked(re, im):
    return jnp.concatenate([re.astype(BF), im.astype(BF)], axis=0)


def right_left(re, im, right, left):
    mid = dot(beside(re, im), right).astype(BF)
    out = dot(left, jnp.concatenate([mid[:, :WIN], mid[:, WIN:]], axis=0))
    return out[:WIN], out[WIN:]


def left_right(re, im, left, right):
    mid = dot(left, stacked(re, im)).astype(BF)
    out = dot(jnp.concatenate([mid[:WIN], mid[WIN:]], axis=1), right)
    return out[:, :WIN], out[:, WIN:]


def iota(shape, axis):
    return lax.broadcasted_iota(jnp.int32, shape, axis)


def kernel(
    counts, offs_in, probe, obj, measured, tabs_in, out,
    offs, other_offs, obj_v, tabs, t_all, t_send, probe_v, meas, rolled, amps, grad, pieces, places, acc, z_send, z_recv,
    load_sem, own_sem, probe_sem, meas_sem, t_sem, t_out_sem, out_sem, place_sem, place_out_sem,
    piece_sem, piece_out_sem, z_sem, z_out_sem,
):
    pos, d, c = lax.axis_index("pos"), lax.axis_index("depth"), lax.axis_index("det")
    z, q = pos // PLANE, pos % PLANE
    y, x = q // 2, q % 2 * 2 + d
    first_of_plane = z * PLANE
    cls = q * 2 + c
    other = z * PLANE + (q ^ 1)
    own = 2 * (2 * d + c)
    across = 2 * (2 * (1 - d) + c)
    beside_slot = 2 * (2 * d + 1 - c)

    own_offs = pltpu.make_async_copy(offs_in, offs, own_sem.at[3])
    own_offs.start()
    load_obj = []
    for cb in range(BANDS):
        column = obj.at[:, :, :, pl.ds(cb * WIN, WIN)]
        load_obj.append(pltpu.make_async_copy(column, obj_v.at[cb], load_sem.at[cb]))
        load_obj[-1].start()
    barrier = pltpu.get_barrier_semaphore()
    for k in range(1, 2 * CLS):
        pl.semaphore_signal(
            barrier, inc=1,
            device_id=(z * PLANE + (q ^ (k // 4)), d ^ (k // 2 % 2), c ^ (k % 2)),
            device_id_type=MESH,
        )
    for k in range(1, BANDS):
        pl.semaphore_signal(
            barrier, inc=1, device_id=((z + k) % BANDS * PLANE + q, d, c), device_id_type=MESH
        )

    load_tabs = pltpu.make_async_copy(tabs_in, tabs, load_sem.at[BANDS])
    load_tabs.start()
    own_probe = pltpu.make_async_copy(probe, probe_v.at[c], own_sem.at[0])
    own_probe.start()
    own_meas = pltpu.make_async_copy(measured.at[pl.ds(own, 2)], meas.at[c], own_sem.at[1])
    own_meas.start()

    own_offs.wait()
    slot_of = iota((CAP, 128), 0)
    for axis in range(2):
        spread = jnp.zeros((CAP, 128), jnp.int32)
        for s in range(CAP):
            spread = jnp.where(slot_of == s, offs[axis, s], spread)
        places[q, axis] = spread
    acc[...] = jnp.zeros_like(acc)
    pl.semaphore_wait(barrier, 2 * CLS - 1 + BANDS - 1)

    def place_copy(k):
        return pltpu.make_async_remote_copy(
            src_ref=places.at[q], dst_ref=places.at[q], send_sem=place_out_sem.at[k],
            recv_sem=place_sem.at[q], device_id=(z * PLANE + (q ^ k), d, c),
            device_id_type=MESH,
        )

    def places_of(g):
        return pltpu.make_async_copy(places.at[g], places.at[g], place_sem.at[g])

    offs_copy = pltpu.make_async_remote_copy(
        src_ref=offs, dst_ref=other_offs, send_sem=place_out_sem.at[0], recv_sem=own_sem.at[2],
        device_id=(other, d, c), device_id_type=MESH,
    )
    offs_copy.start()

    probe_copy = pltpu.make_async_remote_copy(
        src_ref=probe, dst_ref=probe_v.at[c], send_sem=out_sem.at[0], recv_sem=probe_sem,
        device_id=(pos, d, 1 - c), device_id_type=MESH,
    )
    probe_copy.start()
    meas_copy = pltpu.make_async_remote_copy(
        src_ref=measured.at[pl.ds(beside_slot, 2)], dst_ref=meas.at[c], send_sem=out_sem.at[1],
        recv_sem=meas_sem, device_id=(pos, d, 1 - c), device_id_type=MESH,
    )
    meas_copy.start()

    for column in load_obj:
        column.wait()

    row_of, col_of = iota((WIN, WIN), 0), iota((WIN, WIN), 1)

    def cut(r, col, plane, first, count):
        rows = pl.ds(first, count)
        band = jnp.minimum(r >> 8, BANDS - 2)
        block = jnp.minimum(col >> 8, BANDS - 2)
        late = iota((count, WIN), 1) >= col - block * WIN
        top = jnp.where(
            late, obj_v[block, plane, band, rows], obj_v[block + 1, plane, band, rows]
        )
        low = jnp.where(
            late, obj_v[block, plane, band + 1, rows], obj_v[block + 1, plane, band + 1, rows]
        )
        return jnp.where(iota((count, WIN), 0) >= r - band * WIN - first, top, low).astype(BF)

    def t_copy(i, part):
        rows = pl.ds(*PARTS[part])
        return pltpu.make_async_remote_copy(
            src_ref=t_send.at[i, :, rows], dst_ref=t_all.at[d, i, :, rows],
            send_sem=t_out_sem.at[i, part], recv_sem=t_sem.at[i, part],
            device_id=(other if part else pos, 1 - d, c), device_id_type=MESH,
        )

    def send_part(i, part):
        places_in = other_offs if part else offs
        for plane in range(2):
            t_send[i, plane, pl.ds(*PARTS[part])] = cut(
                places_in[0, across + i], places_in[1, across + i], plane, *PARTS[part]
            )
        t_copy(i, part).start()

    send_part(0, 0)
    offs_copy.wait_recv()
    send_part(0, 1)
    send_part(1, 0)
    send_part(1, 1)

    def window(s, i):
        return [t_all[s, i, p].astype(F32) for p in range(2)]

    def prepare(i):
        for plane in range(2):
            t_all[d, i, plane] = cut(offs[0, own + i], offs[1, own + i], plane, 0, WIN)
        flat = jnp.concatenate(
            [jnp.concatenate([probe_v[0, p], probe_v[1, p]], axis=0) for p in range(2)], axis=1
        )
        r, col = offs[0, own + i], offs[1, own + i]
        down = jnp.where(col_of == ((row_of - r) & (WIN - 1)), 1.0, 0.0).astype(BF)
        over = jnp.where(row_of == ((col_of - col) & (WIN - 1)), 1.0, 0.0).astype(BF)
        moved = dot(down, flat).astype(BF)
        moved = dot(jnp.concatenate([moved[:, :WIN], moved[:, WIN:]], axis=0), over)
        rolled[i, 0], rolled[i, 1] = moved[:WIN].astype(BF), moved[WIN:].astype(BF)
        amps[i] = jnp.concatenate([meas[0, i], meas[1, i]], axis=0).T

    own_probe.wait()
    own_meas.wait()
    probe_copy.wait_recv()
    meas_copy.wait_recv()
    prepare(0)
    for k in range(1, PLANE):
        place_copy(k).start()
    load_tabs.wait()

    def send_pieces(i, s):
        odd = d ^ s
        flip = c & odd
        for dy, far in ROUTE:
            yy = (y + (dy if dy % 2 == 0 else dy + 2 * c)) & 3
            xh = ((x + odd + 2 * (far ^ flip)) & 3) >> 1
            group = yy * 2 + xh
            for cc in range(2):
                if (dy, far, cc) == (0, 0, 0):
                    continue
                core = c ^ cc
                pltpu.make_async_remote_copy(
                    src_ref=grad.at[i, s, group * 2 + core],
                    dst_ref=pieces.at[i, q, 2 * d + c],
                    send_sem=piece_out_sem.at[i, s], recv_sem=piece_sem.at[i, q],
                    device_id=(first_of_plane + group, s, core), device_id_type=MESH,
                ).start()

    def send_here(i):
        xx = (x + 1 + 2 * c) % 4
        pltpu.make_async_remote_copy(
            src_ref=grad.at[i, 1 - d, (y * 2 + xx // 2) * 2 + c],
            dst_ref=pieces.at[i, q, 2 * d + c],
            send_sem=piece_out_sem.at[i, 0], recv_sem=piece_sem.at[i, q],
            device_id=(z * PLANE + y * 2 + xx // 2, 1 - d, c), device_id_type=MESH,
        ).start()
        pltpu.make_async_copy(
            grad.at[i, d, cls], pieces.at[i, q, 2 * d + c], piece_sem.at[i, q]
        ).start()

    def load(ref, i):
        return ref[i, 0].astype(F32), ref[i, 1].astype(F32)

    def rounded(pair):
        return pair[0].astype(BF).astype(F32), pair[1].astype(BF).astype(F32)

    def first_wave(i):
        for half in range(2):
            t_copy(i, half).wait_recv()
        (pr, pi), (tr, ti) = load(rolled, i), window(0, i)
        return rounded(
            right_left(pr * tr - pi * ti, pr * ti + pi * tr, tabs[2], tabs[3])
        )

    def far_field(i, wave):
        (wr, wi), (tr, ti) = wave, window(1, i)
        fr, fi = right_left(wr * tr - wi * ti, wr * ti + wi * tr, tabs[0], tabs[1])
        used = jnp.where(jnp.full((1, WIN), own + i, jnp.int32) < counts[0], 1.0, 0.0)
        scale = used * (1.0 - amps[i] * lax.rsqrt(jnp.maximum(fr * fr + fi * fi, 1.0)))
        return fr * scale, fi * scale

    def descent(residual):
        return rounded(left_right(residual[0], residual[1], tabs[0], tabs[1]))

    def put(i, s, wave, desc):
        (wr, wi), (dr, di) = wave, desc
        grad[i, s, :, 0] = (wr * dr + wi * di).astype(BF).reshape(CLS, 16, WIN)
        grad[i, s, :, 1] = (wr * di - wi * dr).astype(BF).reshape(CLS, 16, WIN)

    def first_descent(i, desc):
        (dr, di), (tr, ti) = desc, window(1, i)
        return rounded(
            right_left(tr * dr + ti * di, tr * di - ti * dr, tabs[3], tabs[2])
        )

    wave_a = first_wave(0)
    prepare(1)
    desc_a = descent(far_field(0, wave_a))
    put(0, 1, wave_a, desc_a)
    send_pieces(0, 1)
    wave_b = first_wave(1)
    desc_a = first_descent(0, desc_a)
    put(0, 0, load(rolled, 0), desc_a)
    send_pieces(0, 0)
    send_here(0)
    desc_b = descent(far_field(1, wave_b))
    put(1, 1, wave_b, desc_b)
    send_pieces(1, 1)
    put(1, 0, load(rolled, 1), first_descent(1, desc_b))
    send_pieces(1, 0)
    send_here(1)

    row16 = iota((2, 8, WIN), 0) * 8 + iota((2, 8, WIN), 1) + cls * 16
    col8 = iota((8, WIN), 1)

    def add_group(i, g):
        pltpu.make_async_copy(pieces.at[i, g], pieces.at[i, g], piece_sem.at[i, g]).wait()
        rows, cols = places[g, 0], places[g, 1]
        r0 = jnp.minimum(rows >> 8, BANDS - 2)
        c0 = jnp.minimum(cols >> 8, BANDS - 2)
        rm, cm = rows - r0 * WIN, cols - c0 * WIN

        def wide(x, k):
            one = jnp.broadcast_to(x[2 * k + i : 2 * k + i + 1], (8, 128))
            return jnp.concatenate([one, one], axis=1)

        band = [wide(r0, k) + jnp.where(row16 < wide(rm, k), 1, 0) for k in range(4)]
        block = [wide(c0, k) + jnp.where(col8 < wide(cm, k), 1, 0) for k in range(4)]
        for p in range(2):
            piece = [pieces[i, g, k, p].astype(F32).reshape(2, 8, WIN) for k in range(4)]
            for zb in range(BANDS):
                part = [jnp.where(b == zb, x, 0.0) for b, x in zip(band, piece)]
                for cb in range(BANDS):
                    total = acc[zb, p, :, :, cb * WIN : (cb + 1) * WIN]
                    for b, x in zip(block, part):
                        total += jnp.where(b == cb, x, 0.0)
                    acc[zb, p, :, :, cb * WIN : (cb + 1) * WIN] = total

    def add_first(k, carry):
        g = q ^ k ^ (k // 4 * 2)

        @pl.when(k > 0)
        def _():
            places_of(g).wait()

        add_group(0, g)
        return carry

    def add_second(k, carry):
        add_group(1, q ^ k ^ (k // 4 * 2))
        return carry

    lax.fori_loop(0, PLANE, add_first, 0)
    lax.fori_loop(0, PLANE, add_second, 0)

    z_send[...] = acc[...].reshape(BANDS, 2, 16, 1024).astype(BF)

    def z_copy(k):
        there = (z + k) % BANDS
        return pltpu.make_async_remote_copy(
            src_ref=z_send.at[there], dst_ref=z_recv.at[k], send_sem=z_out_sem.at[k],
            recv_sem=z_sem.at[k], device_id=(there * PLANE + q, d, c), device_id_type=MESH,
        )

    for k in (1 + c, 2 - c, 3):
        z_copy(k).start()
    total = acc[z].reshape(2, 16, 1024)
    for k in (3, 2, 1):
        z_copy(k).wait_recv()
        total += z_recv[k].astype(F32)
    out[...] = total

    for k in range(1, BANDS):
        z_copy(k).wait_send()
    offs_copy.wait_send()
    probe_copy.wait_send()
    meas_copy.wait_send()
    for i in range(2):
        for half in range(2):
            t_copy(i, half).wait_send()
    for k in range(1, PLANE):
        place_copy(k).wait_send()
    for i in range(2):
        for s, count in ((0, CLS), (1, CLS - 1)):
            sent = grad.at[i, s, pl.ds(0, count)]
            pltpu.make_async_copy(sent, sent, piece_out_sem.at[i, s]).wait()


def per_device(offsets, counts, probe_wave, object_slices, measured):
    smem = pl.BlockSpec(memory_space=pltpu.SMEM)
    anywhere = pl.BlockSpec(memory_space=pl.ANY)
    dma = pltpu.SemaphoreType.DMA
    planes = object_slices.reshape(2, BANDS, WIN, BANDS * WIN)
    operands = (offsets.T, probe_wave, planes, measured, jnp.asarray(tables()))
    grad = pl.pallas_call(
        kernel,
        out_shape=pltpu.VMEM((2, 16, 1024), F32),
        in_specs=[smem] + [anywhere] * 5,
        out_specs=pl.BlockSpec(memory_space=pltpu.VMEM),
        scratch_shapes=[
            pltpu.SMEM((2, CAP), jnp.int32),
            pltpu.SMEM((2, CAP), jnp.int32),
            pltpu.VMEM((BANDS, 2, BANDS, WIN, WIN), F32),
            pltpu.VMEM((4, 2 * WIN, 2 * WIN), BF),
            pltpu.VMEM((2, 2, 2, WIN, WIN), BF),
            pltpu.VMEM((2, 2, WIN, WIN), BF),
            pltpu.VMEM((2, 2, WIN // 2, WIN), BF),
            pltpu.VMEM((2, 2, WIN // 2, WIN), F32),
            pltpu.VMEM((2, 2, WIN, WIN), BF),
            pltpu.VMEM((2, WIN, WIN), F32),
            pltpu.VMEM((2, 2, CLS, 2, 16, WIN), BF),
            pltpu.VMEM((2, PLANE, CAP // 2, 2, 16, WIN), BF),
            pltpu.VMEM((PLANE, 2, CAP, 128), jnp.int32),
            pltpu.VMEM((BANDS, 2, 2, 8, 1024), F32),
            pltpu.VMEM((BANDS, 2, 16, 1024), BF),
            pltpu.VMEM((BANDS, 2, 16, 1024), BF),
            dma((BANDS + 1,)),
            dma((4,)),
            dma,
            dma,
            dma((2, 2)),
            dma((2, 2)),
            dma((2,)),
            dma((PLANE,)),
            dma((PLANE,)),
            dma((2, PLANE)),
            dma((2, 2)),
            dma((BANDS,)),
            dma((BANDS,)),
        ],
        compiler_params=pltpu.CompilerParams(
            collective_id=0, has_side_effects=True, vmem_limit_bytes=40 * 2**20
        ),
        cost_estimate=pl.CostEstimate(
            flops=2 * 16 * 2**27, bytes_accessed=12 * 2**20, transcendentals=0
        ),
    )(counts, *(pltpu.with_memory_space_constraint(a, pltpu.HBM) for a in operands))
    return grad[None]


def solution(mesh):
    in_specs = (
        P("pos", None),
        P("pos"),
        P(None, "det", None),
        P("depth", None, None, None),
        P("pos", "det", None),
    )
    out_specs = P("depth", None, ("pos", "det"), None)
    return jax.shard_map(
        per_device, mesh=mesh, in_specs=in_specs, out_specs=out_specs, check_vma=False
    )
```

```python
import math

import jax
import jax.numpy as jnp
import numpy as np
from jax import lax
from jax.experimental import pallas as pl
from jax.experimental.pallas import tpu as pltpu
from jax.sharding import PartitionSpec as P

PROP_DIV = 2
WIN = 256
HALF = WIN // 2
NEAR = 160
PARTS = ((0, NEAR), (NEAR, WIN - NEAR))
BANDS = 4
PLANE = 8
CAP = 8
CLS = 16
ROUTE = ((1, 0), (3, 0), (0, 1), (2, 0), (1, 1), (3, 1), (2, 1), (0, 0))
MESH = pl.DeviceIdType.MESH
BF = jnp.bfloat16
F32 = jnp.float32


def tables():
    k = np.arange(WIN)
    angle = (k[:, None] * k[None, :] % WIN) * (2.0 * math.pi / WIN)
    cos, sin = np.cos(angle), np.sin(angle)
    f = np.where(k < WIN // 2, k, k - WIN)
    h = np.exp(-1j * math.pi / (PROP_DIV * WIN) * (f * f % (2 * PROP_DIV * WIN)))
    dft = cos - 1j * sin
    q = (np.conj(dft) * h[None, :]) @ dft / WIN
    qr, qi = q.real, q.imag
    out = np.stack(
        [
            np.block([[cos, -sin], [sin, cos]]) / 16,
            np.block([[cos, sin], [-sin, cos]]) / 16,
            np.block([[qr, qi], [-qi, qr]]),
            np.block([[qr, -qi], [qi, qr]]),
        ]
    )
    return out.astype(np.float32).astype(BF)


def dot(a, b):
    return jnp.dot(a, b, preferred_element_type=F32)


def beside(re, im):
    return jnp.concatenate([re.astype(BF), im.astype(BF)], axis=1)


def stacked(re, im):
    return jnp.concatenate([re.astype(BF), im.astype(BF)], axis=0)


def right_left(re, im, right, left):
    mid = dot(beside(re, im), right).astype(BF)
    out = dot(left, jnp.concatenate([mid[:, :WIN], mid[:, WIN:]], axis=0))
    return out[:WIN], out[WIN:]


def left_right(re, im, left, right):
    mid = dot(left, stacked(re, im)).astype(BF)
    out = dot(jnp.concatenate([mid[:WIN], mid[WIN:]], axis=1), right)
    return out[:, :WIN], out[:, WIN:]


def iota(shape, axis):
    return lax.broadcasted_iota(jnp.int32, shape, axis)


def kernel(
    counts, offs_in, probe, obj, measured, tabs_in, out,
    offs, other_offs, obj_v, tabs, t_all, t_send, probe_v, meas, rolled, amps, grad, pieces, places, acc, z_send, z_recv,
    load_sem, own_sem, probe_sem, meas_sem, t_sem, t_out_sem, out_sem, place_sem, place_out_sem,
    piece_sem, piece_out_sem, z_sem, z_out_sem,
):
    pos, d, c = lax.axis_index("pos"), lax.axis_index("depth"), lax.axis_index("det")
    z, q = pos // PLANE, pos % PLANE
    y, x = q // 2, q % 2 * 2 + d
    first_of_plane = z * PLANE
    cls = q * 2 + c
    other = z * PLANE + (q ^ 1)
    own = 2 * (2 * d + c)
    across = 2 * (2 * (1 - d) + c)
    beside_slot = 2 * (2 * d + 1 - c)

    own_offs = pltpu.make_async_copy(offs_in, offs, own_sem.at[3])
    own_offs.start()
    load_obj = []
    for cb in range(BANDS):
        column = obj.at[:, :, :, pl.ds(cb * WIN, WIN)]
        load_obj.append(pltpu.make_async_copy(column, obj_v.at[cb], load_sem.at[cb]))
        load_obj[-1].start()
    barrier = pltpu.get_barrier_semaphore()
    for k in range(1, 2 * CLS):
        pl.semaphore_signal(
            barrier, inc=1,
            device_id=(z * PLANE + (q ^ (k // 4)), d ^ (k // 2 % 2), c ^ (k % 2)),
            device_id_type=MESH,
        )
    for k in range(1, BANDS):
        pl.semaphore_signal(
            barrier, inc=1, device_id=((z + k) % BANDS * PLANE + q, d, c), device_id_type=MESH
        )

    load_tabs = pltpu.make_async_copy(tabs_in, tabs, load_sem.at[BANDS])
    load_tabs.start()
    own_probe = pltpu.make_async_copy(probe, probe_v.at[c], own_sem.at[0])
    own_probe.start()
    own_meas = pltpu.make_async_copy(measured.at[pl.ds(own, 2)], meas.at[c], own_sem.at[1])
    own_meas.start()

    own_offs.wait()
    slot_of = iota((CAP, 128), 0)
    for axis in range(2):
        spread = jnp.zeros((CAP, 128), jnp.int32)
        for s in range(CAP):
            spread = jnp.where(slot_of == s, offs[axis, s], spread)
        places[q, axis] = spread
    acc[...] = jnp.zeros_like(acc)
    pl.semaphore_wait(barrier, 2 * CLS - 1 + BANDS - 1)

    def place_copy(k):
        return pltpu.make_async_remote_copy(
            src_ref=places.at[q], dst_ref=places.at[q], send_sem=place_out_sem.at[k],
            recv_sem=place_sem.at[q], device_id=(z * PLANE + (q ^ k), d, c),
            device_id_type=MESH,
        )

    def places_of(g):
        return pltpu.make_async_copy(places.at[g], places.at[g], place_sem.at[g])

    offs_copy = pltpu.make_async_remote_copy(
        src_ref=offs, dst_ref=other_offs, send_sem=place_out_sem.at[0], recv_sem=own_sem.at[2],
        device_id=(other, d, c), device_id_type=MESH,
    )
    offs_copy.start()

    probe_copy = pltpu.make_async_remote_copy(
        src_ref=probe, dst_ref=probe_v.at[c], send_sem=out_sem.at[0], recv_sem=probe_sem,
        device_id=(pos, d, 1 - c), device_id_type=MESH,
    )
    probe_copy.start()
    meas_copy = pltpu.make_async_remote_copy(
        src_ref=measured.at[pl.ds(beside_slot, 2)], dst_ref=meas.at[c], send_sem=out_sem.at[1],
        recv_sem=meas_sem, device_id=(pos, d, 1 - c), device_id_type=MESH,
    )
    meas_copy.start()

    for column in load_obj:
        column.wait()

    row_of, col_of = iota((WIN, WIN), 0), iota((WIN, WIN), 1)

    def cut(r, col, plane, first, count):
        rows = pl.ds(first, count)
        band = jnp.minimum(r >> 8, BANDS - 2)
        block = jnp.minimum(col >> 8, BANDS - 2)
        late = iota((count, WIN), 1) >= col - block * WIN
        top = jnp.where(
            late, obj_v[block, plane, band, rows], obj_v[block + 1, plane, band, rows]
        )
        low = jnp.where(
            late, obj_v[block, plane, band + 1, rows], obj_v[block + 1, plane, band + 1, rows]
        )
        return jnp.where(iota((count, WIN), 0) >= r - band * WIN - first, top, low).astype(BF)

    def t_copy(i, part):
        rows = pl.ds(*PARTS[part])
        return pltpu.make_async_remote_copy(
            src_ref=t_send.at[i, :, rows], dst_ref=t_all.at[d, i, :, rows],
            send_sem=t_out_sem.at[i, part], recv_sem=t_sem.at[i, part],
            device_id=(other if part else pos, 1 - d, c), device_id_type=MESH,
        )

    def send_part(i, part):
        places_in = other_offs if part else offs
        for plane in range(2):
            t_send[i, plane, pl.ds(*PARTS[part])] = cut(
                places_in[0, across + i], places_in[1, across + i], plane, *PARTS[part]
            )
        t_copy(i, part).start()

    send_part(0, 0)
    offs_copy.wait_recv()
    send_part(0, 1)
    send_part(1, 0)
    send_part(1, 1)

    def window(s, i):
        return [t_all[s, i, p].astype(F32) for p in range(2)]

    def prepare(i):
        for plane in range(2):
            t_all[d, i, plane] = cut(offs[0, own + i], offs[1, own + i], plane, 0, WIN)
        flat = jnp.concatenate(
            [jnp.concatenate([probe_v[0, p], probe_v[1, p]], axis=0) for p in range(2)], axis=1
        )
        r, col = offs[0, own + i], offs[1, own + i]
        down = jnp.where(col_of == ((row_of - r) & (WIN - 1)), 1.0, 0.0).astype(BF)
        over = jnp.where(row_of == ((col_of - col) & (WIN - 1)), 1.0, 0.0).astype(BF)
        moved = dot(down, flat).astype(BF)
        moved = dot(jnp.concatenate([moved[:, :WIN], moved[:, WIN:]], axis=0), over)
        rolled[i, 0], rolled[i, 1] = moved[:WIN].astype(BF), moved[WIN:].astype(BF)
        amps[i] = jnp.concatenate([meas[0, i], meas[1, i]], axis=0).T

    own_probe.wait()
    own_meas.wait()
    probe_copy.wait_recv()
    meas_copy.wait_recv()
    prepare(0)
    for k in range(1, PLANE):
        place_copy(k).start()
    load_tabs.wait()

    def send_pieces(i, s):
        odd = d ^ s
        flip = c & odd
        for dy, far in ROUTE:
            yy = (y + (dy if dy % 2 == 0 else dy + 2 * c)) & 3
            xh = ((x + odd + 2 * (far ^ flip)) & 3) >> 1
            group = yy * 2 + xh
            for cc in range(2):
                if (dy, far, cc) == (0, 0, 0):
                    continue
                core = c ^ cc
                pltpu.make_async_remote_copy(
                    src_ref=grad.at[i, s, group * 2 + core],
                    dst_ref=pieces.at[i, q, 2 * d + c],
                    send_sem=piece_out_sem.at[i, s], recv_sem=piece_sem.at[i, q],
                    device_id=(first_of_plane + group, s, core), device_id_type=MESH,
                ).start()

    def send_here(i):
        xx = (x + 1 + 2 * c) % 4
        pltpu.make_async_remote_copy(
            src_ref=grad.at[i, 1 - d, (y * 2 + xx // 2) * 2 + c],
            dst_ref=pieces.at[i, q, 2 * d + c],
            send_sem=piece_out_sem.at[i, 0], recv_sem=piece_sem.at[i, q],
            device_id=(z * PLANE + y * 2 + xx // 2, 1 - d, c), device_id_type=MESH,
        ).start()
        pltpu.make_async_copy(
            grad.at[i, d, cls], pieces.at[i, q, 2 * d + c], piece_sem.at[i, q]
        ).start()

    def load(ref, i):
        return ref[i, 0].astype(F32), ref[i, 1].astype(F32)

    def rounded(pair):
        return pair[0].astype(BF).astype(F32), pair[1].astype(BF).astype(F32)

    def first_wave(i):
        for half in range(2):
            t_copy(i, half).wait_recv()
        (pr, pi), (tr, ti) = load(rolled, i), window(0, i)
        return rounded(
            right_left(pr * tr - pi * ti, pr * ti + pi * tr, tabs[2], tabs[3])
        )

    def far_field(i, wave):
        (wr, wi), (tr, ti) = wave, window(1, i)
        fr, fi = right_left(wr * tr - wi * ti, wr * ti + wi * tr, tabs[0], tabs[1])
        used = jnp.where(jnp.full((1, WIN), own + i, jnp.int32) < counts[0], 1.0, 0.0)
        scale = used * (1.0 - amps[i] * lax.rsqrt(jnp.maximum(fr * fr + fi * fi, 1.0)))
        return fr * scale, fi * scale

    def descent(residual):
        return rounded(left_right(residual[0], residual[1], tabs[0], tabs[1]))

    def put(i, s, wave, desc):
        (wr, wi), (dr, di) = wave, desc
        grad[i, s, :, 0] = (wr * dr + wi * di).astype(BF).reshape(CLS, 16, WIN)
        grad[i, s, :, 1] = (wr * di - wi * dr).astype(BF).reshape(CLS, 16, WIN)

    def first_descent(i, desc):
        (dr, di), (tr, ti) = desc, window(1, i)
        return rounded(
            right_left(tr * dr + ti * di, tr * di - ti * dr, tabs[3], tabs[2])
        )

    wave_a = first_wave(0)
    prepare(1)
    desc_a = descent(far_field(0, wave_a))
    put(0, 1, wave_a, desc_a)
    send_pieces(0, 1)
    wave_b = first_wave(1)
    desc_a = first_descent(0, desc_a)
    put(0, 0, load(rolled, 0), desc_a)
    send_pieces(0, 0)
    send_here(0)
    desc_b = descent(far_field(1, wave_b))
    put(1, 1, wave_b, desc_b)
    put(1, 0, load(rolled, 1), first_descent(1, desc_b))
    send_pieces(1, 0)
    send_here(1)
    send_pieces(1, 1)

    row16 = iota((2, 8, WIN), 0) * 8 + iota((2, 8, WIN), 1) + cls * 16
    col8 = iota((8, WIN), 1)

    def add_group(i, g):
        pltpu.make_async_copy(pieces.at[i, g], pieces.at[i, g], piece_sem.at[i, g]).wait()
        rows, cols = places[g, 0], places[g, 1]
        r0 = jnp.minimum(rows >> 8, BANDS - 2)
        c0 = jnp.minimum(cols >> 8, BANDS - 2)
        rm, cm = rows - r0 * WIN, cols - c0 * WIN

        def wide(x, k):
            one = jnp.broadcast_to(x[2 * k + i : 2 * k + i + 1], (8, 128))
            return jnp.concatenate([one, one], axis=1)

        band = [wide(r0, k) + jnp.where(row16 < wide(rm, k), 1, 0) for k in range(4)]
        block = [wide(c0, k) + jnp.where(col8 < wide(cm, k), 1, 0) for k in range(4)]
        for p in range(2):
            piece = [pieces[i, g, k, p].astype(F32).reshape(2, 8, WIN) for k in range(4)]
            for zb in range(BANDS):
                part = [jnp.where(b == zb, x, 0.0) for b, x in zip(band, piece)]
                for cb in range(BANDS):
                    total = acc[zb, p, :, :, cb * WIN : (cb + 1) * WIN]
                    for b, x in zip(block, part):
                        total += jnp.where(b == cb, x, 0.0)
                    acc[zb, p, :, :, cb * WIN : (cb + 1) * WIN] = total

    def add_first(k, carry):
        g = q ^ k ^ (k // 4 * 2)

        @pl.when(k > 0)
        def _():
            places_of(g).wait()

        add_group(0, g)
        return carry

    def add_second(k, carry):
        add_group(1, q ^ k ^ (k // 4 * 2))
        return carry

    lax.fori_loop(0, PLANE, add_first, 0)
    lax.fori_loop(0, PLANE, add_second, 0)

    z_send[...] = acc[...].reshape(BANDS, 2, 16, 1024).astype(BF)

    def z_copy(k):
        there = (z + k) % BANDS
        return pltpu.make_async_remote_copy(
            src_ref=z_send.at[there], dst_ref=z_recv.at[k], send_sem=z_out_sem.at[k],
            recv_sem=z_sem.at[k], device_id=(there * PLANE + q, d, c), device_id_type=MESH,
        )

    for k in (1 + c, 2 - c, 3):
        z_copy(k).start()
    total = acc[z].reshape(2, 16, 1024)
    for k in (3, 2, 1):
        z_copy(k).wait_recv()
        total += z_recv[k].astype(F32)
    out[...] = total

    for k in range(1, BANDS):
        z_copy(k).wait_send()
    offs_copy.wait_send()
    probe_copy.wait_send()
    meas_copy.wait_send()
    for i in range(2):
        for half in range(2):
            t_copy(i, half).wait_send()
    for k in range(1, PLANE):
        place_copy(k).wait_send()
    for i in range(2):
        for s, count in ((0, CLS), (1, CLS - 1)):
            sent = grad.at[i, s, pl.ds(0, count)]
            pltpu.make_async_copy(sent, sent, piece_out_sem.at[i, s]).wait()


def per_device(offsets, counts, probe_wave, object_slices, measured):
    smem = pl.BlockSpec(memory_space=pltpu.SMEM)
    anywhere = pl.BlockSpec(memory_space=pl.ANY)
    dma = pltpu.SemaphoreType.DMA
    planes = object_slices.reshape(2, BANDS, WIN, BANDS * WIN)
    operands = (offsets.T, probe_wave, planes, measured, jnp.asarray(tables()))
    grad = pl.pallas_call(
        kernel,
        out_shape=pltpu.VMEM((2, 16, 1024), F32),
        in_specs=[smem] + [anywhere] * 5,
        out_specs=pl.BlockSpec(memory_space=pltpu.VMEM),
        scratch_shapes=[
            pltpu.SMEM((2, CAP), jnp.int32),
            pltpu.SMEM((2, CAP), jnp.int32),
            pltpu.VMEM((BANDS, 2, BANDS, WIN, WIN), F32),
            pltpu.VMEM((4, 2 * WIN, 2 * WIN), BF),
            pltpu.VMEM((2, 2, 2, WIN, WIN), BF),
            pltpu.VMEM((2, 2, WIN, WIN), BF),
            pltpu.VMEM((2, 2, WIN // 2, WIN), BF),
            pltpu.VMEM((2, 2, WIN // 2, WIN), F32),
            pltpu.VMEM((2, 2, WIN, WIN), BF),
            pltpu.VMEM((2, WIN, WIN), F32),
            pltpu.VMEM((2, 2, CLS, 2, 16, WIN), BF),
            pltpu.VMEM((2, PLANE, CAP // 2, 2, 16, WIN), BF),
            pltpu.VMEM((PLANE, 2, CAP, 128), jnp.int32),
            pltpu.VMEM((BANDS, 2, 2, 8, 1024), F32),
            pltpu.VMEM((BANDS, 2, 16, 1024), BF),
            pltpu.VMEM((BANDS, 2, 16, 1024), BF),
            dma((BANDS + 1,)),
            dma((4,)),
            dma,
            dma,
            dma((2, 2)),
            dma((2, 2)),
            dma((2,)),
            dma((PLANE,)),
            dma((PLANE,)),
            dma((2, PLANE)),
            dma((2, 2)),
            dma((BANDS,)),
            dma((BANDS,)),
        ],
        compiler_params=pltpu.CompilerParams(
            collective_id=0, has_side_effects=True, vmem_limit_bytes=40 * 2**20
        ),
        cost_estimate=pl.CostEstimate(
            flops=2 * 16 * 2**27, bytes_accessed=12 * 2**20, transcendentals=0
        ),
    )(counts, *(pltpu.with_memory_space_constraint(a, pltpu.HBM) for a in operands))
    return grad[None]


def solution(mesh):
    in_specs = (
        P("pos", None),
        P("pos"),
        P(None, "det", None),
        P("depth", None, None, None),
        P("pos", "det", None),
    )
    out_specs = P("depth", None, ("pos", "det"), None)
    return jax.shard_map(
        per_device, mesh=mesh, in_specs=in_specs, out_specs=out_specs, check_vma=False
    )
```

```python
import math

import jax
import jax.numpy as jnp
import numpy as np
from jax import lax
from jax.experimental import pallas as pl
from jax.experimental.pallas import tpu as pltpu
from jax.sharding import PartitionSpec as P

PROP_DIV = 2
WIN = 256
HALF = WIN // 2
NEAR = 160
PARTS = ((0, NEAR), (NEAR, WIN - NEAR))
BANDS = 4
PLANE = 8
CAP = 8
CLS = 16
ROUTE = ((1, 0), (3, 0), (0, 1), (2, 0), (1, 1), (3, 1), (2, 1), (0, 0))
MESH = pl.DeviceIdType.MESH
BF = jnp.bfloat16
F32 = jnp.float32


def tables():
    k = np.arange(WIN)
    angle = (k[:, None] * k[None, :] % WIN) * (2.0 * math.pi / WIN)
    cos, sin = np.cos(angle), np.sin(angle)
    f = np.where(k < WIN // 2, k, k - WIN)
    h = np.exp(-1j * math.pi / (PROP_DIV * WIN) * (f * f % (2 * PROP_DIV * WIN)))
    dft = cos - 1j * sin
    q = (np.conj(dft) * h[None, :]) @ dft / WIN
    qr, qi = q.real, q.imag
    out = np.stack(
        [
            np.block([[cos, -sin], [sin, cos]]) / 16,
            np.block([[cos, sin], [-sin, cos]]) / 16,
            np.block([[qr, qi], [-qi, qr]]),
            np.block([[qr, -qi], [qi, qr]]),
        ]
    )
    return out.astype(np.float32).astype(BF)


def dot(a, b):
    return jnp.dot(a, b, preferred_element_type=F32)


def beside(re, im):
    return jnp.concatenate([re.astype(BF), im.astype(BF)], axis=1)


def stacked(re, im):
    return jnp.concatenate([re.astype(BF), im.astype(BF)], axis=0)


def right_left(re, im, right, left):
    mid = dot(beside(re, im), right).astype(BF)
    out = dot(left, jnp.concatenate([mid[:, :WIN], mid[:, WIN:]], axis=0))
    return out[:WIN], out[WIN:]


def left_right(re, im, left, right):
    mid = dot(left, stacked(re, im)).astype(BF)
    out = dot(jnp.concatenate([mid[:WIN], mid[WIN:]], axis=1), right)
    return out[:, :WIN], out[:, WIN:]


def iota(shape, axis):
    return lax.broadcasted_iota(jnp.int32, shape, axis)


def kernel(
    counts, offs_in, probe, obj, measured, tabs_in, out,
    offs, other_offs, obj_v, tabs, t_all, t_send, probe_v, meas, rolled, amps, grad, pieces, places, acc, z_send, z_recv,
    load_sem, own_sem, probe_sem, meas_sem, t_sem, t_out_sem, out_sem, place_sem, place_out_sem,
    piece_sem, piece_out_sem, z_sem, z_out_sem,
):
    pos, d, c = lax.axis_index("pos"), lax.axis_index("depth"), lax.axis_index("det")
    z, q = pos // PLANE, pos % PLANE
    y, x = q // 2, q % 2 * 2 + d
    first_of_plane = z * PLANE
    cls = q * 2 + c
    other = z * PLANE + (q ^ 1)
    own = 2 * (2 * d + c)
    across = 2 * (2 * (1 - d) + c)
    beside_slot = 2 * (2 * d + 1 - c)

    barrier = pltpu.get_barrier_semaphore()
    for k in range(1, 2 * CLS):
        pl.semaphore_signal(
            barrier, inc=1,
            device_id=(z * PLANE + (q ^ (k // 4)), d ^ (k // 2 % 2), c ^ (k % 2)),
            device_id_type=MESH,
        )
    for k in range(1, BANDS):
        pl.semaphore_signal(
            barrier, inc=1, device_id=((z + k) % BANDS * PLANE + q, d, c), device_id_type=MESH
        )

    own_offs = pltpu.make_async_copy(offs_in, offs, own_sem.at[3])
    own_offs.start()
    load_obj = []
    for cb in range(BANDS):
        column = obj.at[:, :, :, pl.ds(cb * WIN, WIN)]
        load_obj.append(pltpu.make_async_copy(column, obj_v.at[cb], load_sem.at[cb]))
        load_obj[-1].start()
    load_tabs = pltpu.make_async_copy(tabs_in, tabs, load_sem.at[BANDS])
    load_tabs.start()
    own_probe = pltpu.make_async_copy(probe, probe_v.at[c], own_sem.at[0])
    own_probe.start()
    own_meas = pltpu.make_async_copy(measured.at[pl.ds(own, 2)], meas.at[c], own_sem.at[1])
    own_meas.start()

    own_offs.wait()
    slot_of = iota((CAP, 128), 0)
    for axis in range(2):
        spread = jnp.zeros((CAP, 128), jnp.int32)
        for s in range(CAP):
            spread = jnp.where(slot_of == s, offs[axis, s], spread)
        places[q, axis] = spread
    acc[...] = jnp.zeros_like(acc)
    pl.semaphore_wait(barrier, 2 * CLS - 1 + BANDS - 1)

    def place_copy(k):
        return pltpu.make_async_remote_copy(
            src_ref=places.at[q], dst_ref=places.at[q], send_sem=place_out_sem.at[k],
            recv_sem=place_sem.at[q], device_id=(z * PLANE + (q ^ k), d, c),
            device_id_type=MESH,
        )

    def places_of(g):
        return pltpu.make_async_copy(places.at[g], places.at[g], place_sem.at[g])

    offs_copy = pltpu.make_async_remote_copy(
        src_ref=offs, dst_ref=other_offs, send_sem=place_out_sem.at[0], recv_sem=own_sem.at[2],
        device_id=(other, d, c), device_id_type=MESH,
    )
    offs_copy.start()

    probe_copy = pltpu.make_async_remote_copy(
        src_ref=probe, dst_ref=probe_v.at[c], send_sem=out_sem.at[0], recv_sem=probe_sem,
        device_id=(pos, d, 1 - c), device_id_type=MESH,
    )
    probe_copy.start()
    meas_copy = pltpu.make_async_remote_copy(
        src_ref=measured.at[pl.ds(beside_slot, 2)], dst_ref=meas.at[c], send_sem=out_sem.at[1],
        recv_sem=meas_sem, device_id=(pos, d, 1 - c), device_id_type=MESH,
    )
    meas_copy.start()

    for column in load_obj:
        column.wait()

    row_of, col_of = iota((WIN, WIN), 0), iota((WIN, WIN), 1)

    def cut(r, col, plane, first, count):
        rows = pl.ds(first, count)
        band = jnp.minimum(r >> 8, BANDS - 2)
        block = jnp.minimum(col >> 8, BANDS - 2)
        late = iota((count, WIN), 1) >= col - block * WIN
        top = jnp.where(
            late, obj_v[block, plane, band, rows], obj_v[block + 1, plane, band, rows]
        )
        low = jnp.where(
            late, obj_v[block, plane, band + 1, rows], obj_v[block + 1, plane, band + 1, rows]
        )
        return jnp.where(iota((count, WIN), 0) >= r - band * WIN - first, top, low).astype(BF)

    def t_copy(i, part):
        rows = pl.ds(*PARTS[part])
        return pltpu.make_async_remote_copy(
            src_ref=t_send.at[i, :, rows], dst_ref=t_all.at[d, i, :, rows],
            send_sem=t_out_sem.at[i, part], recv_sem=t_sem.at[i, part],
            device_id=(other if part else pos, 1 - d, c), device_id_type=MESH,
        )

    def send_part(i, part):
        places_in = other_offs if part else offs
        for plane in range(2):
            t_send[i, plane, pl.ds(*PARTS[part])] = cut(
                places_in[0, across + i], places_in[1, across + i], plane, *PARTS[part]
            )
        t_copy(i, part).start()

    send_part(0, 0)
    offs_copy.wait_recv()
    send_part(0, 1)
    send_part(1, 0)
    send_part(1, 1)

    def window(s, i):
        return [t_all[s, i, p].astype(F32) for p in range(2)]

    def prepare(i):
        for plane in range(2):
            t_all[d, i, plane] = cut(offs[0, own + i], offs[1, own + i], plane, 0, WIN)
        flat = jnp.concatenate(
            [jnp.concatenate([probe_v[0, p], probe_v[1, p]], axis=0) for p in range(2)], axis=1
        )
        r, col = offs[0, own + i], offs[1, own + i]
        down = jnp.where(col_of == ((row_of - r) & (WIN - 1)), 1.0, 0.0).astype(BF)
        over = jnp.where(row_of == ((col_of - col) & (WIN - 1)), 1.0, 0.0).astype(BF)
        moved = dot(down, flat).astype(BF)
        moved = dot(jnp.concatenate([moved[:, :WIN], moved[:, WIN:]], axis=0), over)
        rolled[i, 0], rolled[i, 1] = moved[:WIN].astype(BF), moved[WIN:].astype(BF)
        amps[i] = jnp.concatenate([meas[0, i], meas[1, i]], axis=0).T

    own_probe.wait()
    own_meas.wait()
    probe_copy.wait_recv()
    meas_copy.wait_recv()
    prepare(0)
    for k in range(1, PLANE):
        place_copy(k).start()
    load_tabs.wait()

    def send_pieces(i, s):
        odd = d ^ s
        flip = c & odd
        for dy, far in ROUTE:
            yy = (y + (dy if dy % 2 == 0 else dy + 2 * c)) & 3
            xh = ((x + odd + 2 * (far ^ flip)) & 3) >> 1
            group = yy * 2 + xh
            for cc in range(2):
                if (dy, far, cc) == (0, 0, 0):
                    continue
                core = c ^ cc
                pltpu.make_async_remote_copy(
                    src_ref=grad.at[i, s, group * 2 + core],
                    dst_ref=pieces.at[i, q, 2 * d + c],
                    send_sem=piece_out_sem.at[i, s], recv_sem=piece_sem.at[i, q],
                    device_id=(first_of_plane + group, s, core), device_id_type=MESH,
                ).start()

    def send_here(i):
        xx = (x + 1 + 2 * c) % 4
        pltpu.make_async_remote_copy(
            src_ref=grad.at[i, 1 - d, (y * 2 + xx // 2) * 2 + c],
            dst_ref=pieces.at[i, q, 2 * d + c],
            send_sem=piece_out_sem.at[i, 0], recv_sem=piece_sem.at[i, q],
            device_id=(z * PLANE + y * 2 + xx // 2, 1 - d, c), device_id_type=MESH,
        ).start()
        pltpu.make_async_copy(
            grad.at[i, d, cls], pieces.at[i, q, 2 * d + c], piece_sem.at[i, q]
        ).start()

    def load(ref, i):
        return ref[i, 0].astype(F32), ref[i, 1].astype(F32)

    def rounded(pair):
        return pair[0].astype(BF).astype(F32), pair[1].astype(BF).astype(F32)

    def first_wave(i):
        for half in range(2):
            t_copy(i, half).wait_recv()
        (pr, pi), (tr, ti) = load(rolled, i), window(0, i)
        return rounded(
            right_left(pr * tr - pi * ti, pr * ti + pi * tr, tabs[2], tabs[3])
        )

    def far_field(i, wave):
        (wr, wi), (tr, ti) = wave, window(1, i)
        fr, fi = right_left(wr * tr - wi * ti, wr * ti + wi * tr, tabs[0], tabs[1])
        used = jnp.where(jnp.full((1, WIN), own + i, jnp.int32) < counts[0], 1.0, 0.0)
        scale = used * (1.0 - amps[i] * lax.rsqrt(jnp.maximum(fr * fr + fi * fi, 1.0)))
        return fr * scale, fi * scale

    def descent(residual):
        return rounded(left_right(residual[0], residual[1], tabs[0], tabs[1]))

    def put(i, s, wave, desc):
        (wr, wi), (dr, di) = wave, desc
        grad[i, s, :, 0] = (wr * dr + wi * di).astype(BF).reshape(CLS, 16, WIN)
        grad[i, s, :, 1] = (wr * di - wi * dr).astype(BF).reshape(CLS, 16, WIN)

    def first_descent(i, desc):
        (dr, di), (tr, ti) = desc, window(1, i)
        return rounded(
            right_left(tr * dr + ti * di, tr * di - ti * dr, tabs[3], tabs[2])
        )

    wave_a = first_wave(0)
    prepare(1)
    desc_a = descent(far_field(0, wave_a))
    put(0, 1, wave_a, desc_a)
    send_pieces(0, 1)
    wave_b = first_wave(1)
    desc_a = first_descent(0, desc_a)
    put(0, 0, load(rolled, 0), desc_a)
    send_pieces(0, 0)
    send_here(0)
    desc_b = descent(far_field(1, wave_b))
    put(1, 1, wave_b, desc_b)
    send_pieces(1, 1)
    put(1, 0, load(rolled, 1), first_descent(1, desc_b))
    send_pieces(1, 0)
    send_here(1)

    row16 = iota((2, 8, WIN), 0) * 8 + iota((2, 8, WIN), 1) + cls * 16
    col8 = iota((8, WIN), 1)

    def add_group(i, g):
        pltpu.make_async_copy(pieces.at[i, g], pieces.at[i, g], piece_sem.at[i, g]).wait()
        rows, cols = places[g, 0], places[g, 1]
        r0 = jnp.minimum(rows >> 8, BANDS - 2)
        c0 = jnp.minimum(cols >> 8, BANDS - 2)
        rm, cm = rows - r0 * WIN, cols - c0 * WIN

        def wide(x, k):
            one = jnp.broadcast_to(x[2 * k + i : 2 * k + i + 1], (8, 128))
            return jnp.concatenate([one, one], axis=1)

        band = [wide(r0, k) + jnp.where(row16 < wide(rm, k), 1, 0) for k in range(4)]
        block = [wide(c0, k) + jnp.where(col8 < wide(cm, k), 1, 0) for k in range(4)]
        for p in range(2):
            piece = [pieces[i, g, k, p].astype(F32).reshape(2, 8, WIN) for k in range(4)]
            for zb in range(BANDS):
                part = [jnp.where(b == zb, x, 0.0) for b, x in zip(band, piece)]
                for cb in range(BANDS):
                    total = acc[zb, p, :, :, cb * WIN : (cb + 1) * WIN]
                    for b, x in zip(block, part):
                        total += jnp.where(b == cb, x, 0.0)
                    acc[zb, p, :, :, cb * WIN : (cb + 1) * WIN] = total

    def add_first(k, carry):
        g = q ^ k ^ (k // 4 * 2)

        @pl.when(k > 0)
        def _():
            places_of(g).wait()

        add_group(0, g)
        return carry

    def add_second(k, carry):
        add_group(1, q ^ k ^ (k // 4 * 2))
        return carry

    lax.fori_loop(0, PLANE, add_first, 0)
    lax.fori_loop(0, PLANE, add_second, 0)

    def z_copy(k):
        there = (z + k) % BANDS
        return pltpu.make_async_remote_copy(
            src_ref=z_send.at[there], dst_ref=z_recv.at[k], send_sem=z_out_sem.at[k],
            recv_sem=z_sem.at[k], device_id=(there * PLANE + q, d, c), device_id_type=MESH,
        )

    for k in (1 + c, 2 - c, 3):
        z_send[(z + k) % BANDS] = acc[(z + k) % BANDS].reshape(2, 16, 1024).astype(BF)
        z_copy(k).start()
    total = acc[z].reshape(2, 16, 1024)
    for k in (3, 2, 1):
        z_copy(k).wait_recv()
        total += z_recv[k].astype(F32)
    out[...] = total

    for k in range(1, BANDS):
        z_copy(k).wait_send()
    offs_copy.wait_send()
    probe_copy.wait_send()
    meas_copy.wait_send()
    for i in range(2):
        for half in range(2):
            t_copy(i, half).wait_send()
    for k in range(1, PLANE):
        place_copy(k).wait_send()
    for i in range(2):
        for s, count in ((0, CLS), (1, CLS - 1)):
            sent = grad.at[i, s, pl.ds(0, count)]
            pltpu.make_async_copy(sent, sent, piece_out_sem.at[i, s]).wait()


def per_device(offsets, counts, probe_wave, object_slices, measured):
    smem = pl.BlockSpec(memory_space=pltpu.SMEM)
    anywhere = pl.BlockSpec(memory_space=pl.ANY)
    dma = pltpu.SemaphoreType.DMA
    planes = object_slices.reshape(2, BANDS, WIN, BANDS * WIN)
    operands = (offsets.T, probe_wave, planes, measured, jnp.asarray(tables()))
    grad = pl.pallas_call(
        kernel,
        out_shape=pltpu.VMEM((2, 16, 1024), F32),
        in_specs=[smem] + [anywhere] * 5,
        out_specs=pl.BlockSpec(memory_space=pltpu.VMEM),
        scratch_shapes=[
            pltpu.SMEM((2, CAP), jnp.int32),
            pltpu.SMEM((2, CAP), jnp.int32),
            pltpu.VMEM((BANDS, 2, BANDS, WIN, WIN), F32),
            pltpu.VMEM((4, 2 * WIN, 2 * WIN), BF),
            pltpu.VMEM((2, 2, 2, WIN, WIN), BF),
            pltpu.VMEM((2, 2, WIN, WIN), BF),
            pltpu.VMEM((2, 2, WIN // 2, WIN), BF),
            pltpu.VMEM((2, 2, WIN // 2, WIN), F32),
            pltpu.VMEM((2, 2, WIN, WIN), BF),
            pltpu.VMEM((2, WIN, WIN), F32),
            pltpu.VMEM((2, 2, CLS, 2, 16, WIN), BF),
            pltpu.VMEM((2, PLANE, CAP // 2, 2, 16, WIN), BF),
            pltpu.VMEM((PLANE, 2, CAP, 128), jnp.int32),
            pltpu.VMEM((BANDS, 2, 2, 8, 1024), F32),
            pltpu.VMEM((BANDS, 2, 16, 1024), BF),
            pltpu.VMEM((BANDS, 2, 16, 1024), BF),
            dma((BANDS + 1,)),
            dma((4,)),
            dma,
            dma,
            dma((2, 2)),
            dma((2, 2)),
            dma((2,)),
            dma((PLANE,)),
            dma((PLANE,)),
            dma((2, PLANE)),
            dma((2, 2)),
            dma((BANDS,)),
            dma((BANDS,)),
        ],
        compiler_params=pltpu.CompilerParams(
            collective_id=0, has_side_effects=True, vmem_limit_bytes=40 * 2**20
        ),
        cost_estimate=pl.CostEstimate(
            flops=2 * 16 * 2**27, bytes_accessed=12 * 2**20, transcendentals=0
        ),
    )(counts, *(pltpu.with_memory_space_constraint(a, pltpu.HBM) for a in operands))
    return grad[None]


def solution(mesh):
    in_specs = (
        P("pos", None),
        P("pos"),
        P(None, "det", None),
        P("depth", None, None, None),
        P("pos", "det", None),
    )
    out_specs = P("depth", None, ("pos", "det"), None)
    return jax.shard_map(
        per_device, mesh=mesh, in_specs=in_specs, out_specs=out_specs, check_vma=False
    )
```

```python
import math

import jax
import jax.numpy as jnp
import numpy as np
from jax import lax
from jax.experimental import pallas as pl
from jax.experimental.pallas import tpu as pltpu
from jax.sharding import PartitionSpec as P

PROP_DIV = 2
WIN = 256
HALF = WIN // 2
NEAR = 160
PARTS = ((0, NEAR), (NEAR, WIN - NEAR))
BANDS = 4
PLANE = 8
CAP = 8
CLS = 16
ROUTE = ((1, 0), (3, 0), (0, 1), (2, 0), (1, 1), (3, 1), (2, 1), (0, 0))
MESH = pl.DeviceIdType.MESH
BF = jnp.bfloat16
F32 = jnp.float32


def tables():
    k = np.arange(WIN)
    angle = (k[:, None] * k[None, :] % WIN) * (2.0 * math.pi / WIN)
    cos, sin = np.cos(angle), np.sin(angle)
    f = np.where(k < WIN // 2, k, k - WIN)
    h = np.exp(-1j * math.pi / (PROP_DIV * WIN) * (f * f % (2 * PROP_DIV * WIN)))
    dft = cos - 1j * sin
    q = (np.conj(dft) * h[None, :]) @ dft / WIN
    qr, qi = q.real, q.imag
    out = np.stack(
        [
            np.block([[cos, -sin], [sin, cos]]) / 16,
            np.block([[cos, sin], [-sin, cos]]) / 16,
            np.block([[qr, qi], [-qi, qr]]),
            np.block([[qr, -qi], [qi, qr]]),
        ]
    )
    return out.astype(np.float32).astype(BF)


def dot(a, b):
    return jnp.dot(a, b, preferred_element_type=F32)


def beside(re, im):
    return jnp.concatenate([re.astype(BF), im.astype(BF)], axis=1)


def stacked(re, im):
    return jnp.concatenate([re.astype(BF), im.astype(BF)], axis=0)


def right_left(re, im, right, left):
    mid = dot(beside(re, im), right).astype(BF)
    out = dot(left, jnp.concatenate([mid[:, :WIN], mid[:, WIN:]], axis=0))
    return out[:WIN], out[WIN:]


def left_right(re, im, left, right):
    mid = dot(left, stacked(re, im)).astype(BF)
    out = dot(jnp.concatenate([mid[:WIN], mid[WIN:]], axis=1), right)
    return out[:, :WIN], out[:, WIN:]


def iota(shape, axis):
    return lax.broadcasted_iota(jnp.int32, shape, axis)


def kernel(
    counts, offs_in, probe, obj, measured, tabs_in, out,
    offs, other_offs, obj_v, tabs, t_all, t_send, probe_v, meas, rolled, amps, grad, pieces, places, acc, z_send, z_recv,
    load_sem, own_sem, probe_sem, meas_sem, t_sem, t_out_sem, out_sem, place_sem, place_out_sem,
    piece_sem, piece_out_sem, z_sem, z_out_sem,
):
    pos, d, c = lax.axis_index("pos"), lax.axis_index("depth"), lax.axis_index("det")
    z, q = pos // PLANE, pos % PLANE
    y, x = q // 2, q % 2 * 2 + d
    first_of_plane = z * PLANE
    cls = q * 2 + c
    other = z * PLANE + (q ^ 1)
    own = 2 * (2 * d + c)
    across = 2 * (2 * (1 - d) + c)
    beside_slot = 2 * (2 * d + 1 - c)

    barrier = pltpu.get_barrier_semaphore()
    for k in range(1, 2 * CLS):
        pl.semaphore_signal(
            barrier, inc=1,
            device_id=(z * PLANE + (q ^ (k // 4)), d ^ (k // 2 % 2), c ^ (k % 2)),
            device_id_type=MESH,
        )
    for k in range(1, BANDS):
        pl.semaphore_signal(
            barrier, inc=1, device_id=((z + k) % BANDS * PLANE + q, d, c), device_id_type=MESH
        )

    own_offs = pltpu.make_async_copy(offs_in, offs, own_sem.at[3])
    own_offs.start()
    load_obj = []
    for cb in range(BANDS):
        column = obj.at[:, :, :, pl.ds(cb * WIN, WIN)]
        load_obj.append(pltpu.make_async_copy(column, obj_v.at[cb], load_sem.at[cb]))
        load_obj[-1].start()
    load_tabs = pltpu.make_async_copy(tabs_in, tabs, load_sem.at[BANDS])
    load_tabs.start()
    own_probe = pltpu.make_async_copy(probe, probe_v.at[c], own_sem.at[0])
    own_probe.start()
    own_meas = pltpu.make_async_copy(measured.at[pl.ds(own, 2)], meas.at[c], own_sem.at[1])
    own_meas.start()

    own_offs.wait()
    slot_of = iota((CAP, 128), 0)
    for axis in range(2):
        spread = jnp.zeros((CAP, 128), jnp.int32)
        for s in range(CAP):
            spread = jnp.where(slot_of == s, offs[axis, s], spread)
        places[q, axis] = spread
    acc[...] = jnp.zeros_like(acc)
    pl.semaphore_wait(barrier, 2 * CLS - 1 + BANDS - 1)

    def place_copy(k):
        return pltpu.make_async_remote_copy(
            src_ref=places.at[q], dst_ref=places.at[q], send_sem=place_out_sem.at[k],
            recv_sem=place_sem.at[q], device_id=(z * PLANE + (q ^ k), d, c),
            device_id_type=MESH,
        )

    def places_of(g):
        return pltpu.make_async_copy(places.at[g], places.at[g], place_sem.at[g])

    offs_copy = pltpu.make_async_remote_copy(
        src_ref=offs, dst_ref=other_offs, send_sem=place_out_sem.at[0], recv_sem=own_sem.at[2],
        device_id=(other, d, c), device_id_type=MESH,
    )
    offs_copy.start()

    probe_copy = pltpu.make_async_remote_copy(
        src_ref=probe, dst_ref=probe_v.at[c], send_sem=out_sem.at[0], recv_sem=probe_sem,
        device_id=(pos, d, 1 - c), device_id_type=MESH,
    )
    probe_copy.start()
    meas_copy = pltpu.make_async_remote_copy(
        src_ref=measured.at[pl.ds(beside_slot, 2)], dst_ref=meas.at[c], send_sem=out_sem.at[1],
        recv_sem=meas_sem, device_id=(pos, d, 1 - c), device_id_type=MESH,
    )
    meas_copy.start()

    for column in load_obj:
        column.wait()

    row_of, col_of = iota((WIN, WIN), 0), iota((WIN, WIN), 1)

    def cut(r, col, plane, first, count):
        rows = pl.ds(first, count)
        band = jnp.minimum(r >> 8, BANDS - 2)
        block = jnp.minimum(col >> 8, BANDS - 2)
        late = iota((count, WIN), 1) >= col - block * WIN
        top = jnp.where(
            late, obj_v[block, plane, band, rows], obj_v[block + 1, plane, band, rows]
        )
        low = jnp.where(
            late, obj_v[block, plane, band + 1, rows], obj_v[block + 1, plane, band + 1, rows]
        )
        return jnp.where(iota((count, WIN), 0) >= r - band * WIN - first, top, low).astype(BF)

    def t_copy(i, part):
        rows = pl.ds(*PARTS[part])
        return pltpu.make_async_remote_copy(
            src_ref=t_send.at[i, :, rows], dst_ref=t_all.at[d, i, :, rows],
            send_sem=t_out_sem.at[i, part], recv_sem=t_sem.at[i, part],
            device_id=(other if part else pos, 1 - d, c), device_id_type=MESH,
        )

    def send_part(i, part):
        places_in = other_offs if part else offs
        for plane in range(2):
            t_send[i, plane, pl.ds(*PARTS[part])] = cut(
                places_in[0, across + i], places_in[1, across + i], plane, *PARTS[part]
            )
        t_copy(i, part).start()

    send_part(0, 0)
    offs_copy.wait_recv()
    send_part(0, 1)
    send_part(1, 0)
    send_part(1, 1)

    def window(s, i):
        return [t_all[s, i, p].astype(F32) for p in range(2)]

    def prepare(i):
        for plane in range(2):
            t_all[d, i, plane] = cut(offs[0, own + i], offs[1, own + i], plane, 0, WIN)
        flat = jnp.concatenate(
            [jnp.concatenate([probe_v[0, p], probe_v[1, p]], axis=0) for p in range(2)], axis=1
        )
        r, col = offs[0, own + i], offs[1, own + i]
        down = jnp.where(col_of == ((row_of - r) & (WIN - 1)), 1.0, 0.0).astype(BF)
        over = jnp.where(row_of == ((col_of - col) & (WIN - 1)), 1.0, 0.0).astype(BF)
        moved = dot(down, flat).astype(BF)
        moved = dot(jnp.concatenate([moved[:, :WIN], moved[:, WIN:]], axis=0), over)
        rolled[i, 0], rolled[i, 1] = moved[:WIN].astype(BF), moved[WIN:].astype(BF)
        amps[i] = jnp.concatenate([meas[0, i], meas[1, i]], axis=0).T

    own_probe.wait()
    own_meas.wait()
    probe_copy.wait_recv()
    meas_copy.wait_recv()
    prepare(0)
    for k in range(1, PLANE):
        place_copy(k).start()
    load_tabs.wait()

    def send_pieces(i, s):
        odd = d ^ s
        flip = c & odd
        for dy, far in ROUTE:
            yy = (y + (dy if dy % 2 == 0 else dy + 2 * c)) & 3
            xh = ((x + odd + 2 * (far ^ flip)) & 3) >> 1
            group = yy * 2 + xh
            for cc in range(2):
                if (dy, far, cc) == (0, 0, 0):
                    continue
                core = c ^ cc
                pltpu.make_async_remote_copy(
                    src_ref=grad.at[i, s, group * 2 + core],
                    dst_ref=pieces.at[i, q, 2 * d + c],
                    send_sem=piece_out_sem.at[i, s], recv_sem=piece_sem.at[i, q],
                    device_id=(first_of_plane + group, s, core), device_id_type=MESH,
                ).start()

    def send_here(i):
        xx = (x + 1 + 2 * c) % 4
        pltpu.make_async_remote_copy(
            src_ref=grad.at[i, 1 - d, (y * 2 + xx // 2) * 2 + c],
            dst_ref=pieces.at[i, q, 2 * d + c],
            send_sem=piece_out_sem.at[i, 0], recv_sem=piece_sem.at[i, q],
            device_id=(z * PLANE + y * 2 + xx // 2, 1 - d, c), device_id_type=MESH,
        ).start()
        pltpu.make_async_copy(
            grad.at[i, d, cls], pieces.at[i, q, 2 * d + c], piece_sem.at[i, q]
        ).start()

    def load(ref, i):
        return ref[i, 0].astype(F32), ref[i, 1].astype(F32)

    def rounded(pair):
        return pair[0].astype(BF).astype(F32), pair[1].astype(BF).astype(F32)

    def first_wave(i):
        for half in range(2):
            t_copy(i, half).wait_recv()
        (pr, pi), (tr, ti) = load(rolled, i), window(0, i)
        return rounded(
            right_left(pr * tr - pi * ti, pr * ti + pi * tr, tabs[2], tabs[3])
        )

    def far_field(i, wave):
        (wr, wi), (tr, ti) = wave, window(1, i)
        fr, fi = right_left(wr * tr - wi * ti, wr * ti + wi * tr, tabs[0], tabs[1])
        used = jnp.where(jnp.full((1, WIN), own + i, jnp.int32) < counts[0], 1.0, 0.0)
        scale = used * (1.0 - amps[i] * lax.rsqrt(jnp.maximum(fr * fr + fi * fi, 1.0)))
        return fr * scale, fi * scale

    def descent(residual):
        return rounded(left_right(residual[0], residual[1], tabs[0], tabs[1]))

    def put(i, s, wave, desc):
        (wr, wi), (dr, di) = wave, desc
        grad[i, s, :, 0] = (wr * dr + wi * di).astype(BF).reshape(CLS, 16, WIN)
        grad[i, s, :, 1] = (wr * di - wi * dr).astype(BF).reshape(CLS, 16, WIN)

    def first_descent(i, desc):
        (dr, di), (tr, ti) = desc, window(1, i)
        return rounded(
            right_left(tr * dr + ti * di, tr * di - ti * dr, tabs[3], tabs[2])
        )

    wave_a = first_wave(0)
    prepare(1)
    desc_a = descent(far_field(0, wave_a))
    put(0, 1, wave_a, desc_a)
    send_pieces(0, 1)
    desc_a = first_descent(0, desc_a)
    put(0, 0, load(rolled, 0), desc_a)
    send_pieces(0, 0)
    send_here(0)
    wave_b = first_wave(1)
    desc_b = descent(far_field(1, wave_b))
    put(1, 1, wave_b, desc_b)
    send_pieces(1, 1)
    put(1, 0, load(rolled, 1), first_descent(1, desc_b))
    send_pieces(1, 0)
    send_here(1)

    row16 = iota((2, 8, WIN), 0) * 8 + iota((2, 8, WIN), 1) + cls * 16
    col8 = iota((8, WIN), 1)

    def add_group(i, g):
        pltpu.make_async_copy(pieces.at[i, g], pieces.at[i, g], piece_sem.at[i, g]).wait()
        rows, cols = places[g, 0], places[g, 1]
        r0 = jnp.minimum(rows >> 8, BANDS - 2)
        c0 = jnp.minimum(cols >> 8, BANDS - 2)
        rm, cm = rows - r0 * WIN, cols - c0 * WIN

        def wide(x, k):
            one = jnp.broadcast_to(x[2 * k + i : 2 * k + i + 1], (8, 128))
            return jnp.concatenate([one, one], axis=1)

        band = [wide(r0, k) + jnp.where(row16 < wide(rm, k), 1, 0) for k in range(4)]
        block = [wide(c0, k) + jnp.where(col8 < wide(cm, k), 1, 0) for k in range(4)]
        for p in range(2):
            piece = [pieces[i, g, k, p].astype(F32).reshape(2, 8, WIN) for k in range(4)]
            for zb in range(BANDS):
                part = [jnp.where(b == zb, x, 0.0) for b, x in zip(band, piece)]
                for cb in range(BANDS):
                    total = acc[zb, p, :, :, cb * WIN : (cb + 1) * WIN]
                    for b, x in zip(block, part):
                        total += jnp.where(b == cb, x, 0.0)
                    acc[zb, p, :, :, cb * WIN : (cb + 1) * WIN] = total

    def add_first(k, carry):
        g = q ^ k ^ (k // 4 * 2)

        @pl.when(k > 0)
        def _():
            places_of(g).wait()

        add_group(0, g)
        return carry

    def add_second(k, carry):
        add_group(1, q ^ k ^ (k // 4 * 2))
        return carry

    lax.fori_loop(0, PLANE, add_first, 0)
    lax.fori_loop(0, PLANE, add_second, 0)

    def z_copy(k):
        there = (z + k) % BANDS
        return pltpu.make_async_remote_copy(
            src_ref=z_send.at[there], dst_ref=z_recv.at[k], send_sem=z_out_sem.at[k],
            recv_sem=z_sem.at[k], device_id=(there * PLANE + q, d, c), device_id_type=MESH,
        )

    for k in (1 + c, 2 - c, 3):
        z_send[(z + k) % BANDS] = acc[(z + k) % BANDS].reshape(2, 16, 1024).astype(BF)
        z_copy(k).start()
    total = acc[z].reshape(2, 16, 1024)
    for k in (3, 2, 1):
        z_copy(k).wait_recv()
        total += z_recv[k].astype(F32)
    out[...] = total

    for k in range(1, BANDS):
        z_copy(k).wait_send()
    offs_copy.wait_send()
    probe_copy.wait_send()
    meas_copy.wait_send()
    for i in range(2):
        for half in range(2):
            t_copy(i, half).wait_send()
    for k in range(1, PLANE):
        place_copy(k).wait_send()
    for i in range(2):
        for s, count in ((0, CLS), (1, CLS - 1)):
            sent = grad.at[i, s, pl.ds(0, count)]
            pltpu.make_async_copy(sent, sent, piece_out_sem.at[i, s]).wait()


def per_device(offsets, counts, probe_wave, object_slices, measured):
    smem = pl.BlockSpec(memory_space=pltpu.SMEM)
    anywhere = pl.BlockSpec(memory_space=pl.ANY)
    dma = pltpu.SemaphoreType.DMA
    planes = object_slices.reshape(2, BANDS, WIN, BANDS * WIN)
    operands = (offsets.T, probe_wave, planes, measured, jnp.asarray(tables()))
    grad = pl.pallas_call(
        kernel,
        out_shape=pltpu.VMEM((2, 16, 1024), F32),
        in_specs=[smem] + [anywhere] * 5,
        out_specs=pl.BlockSpec(memory_space=pltpu.VMEM),
        scratch_shapes=[
            pltpu.SMEM((2, CAP), jnp.int32),
            pltpu.SMEM((2, CAP), jnp.int32),
            pltpu.VMEM((BANDS, 2, BANDS, WIN, WIN), F32),
            pltpu.VMEM((4, 2 * WIN, 2 * WIN), BF),
            pltpu.VMEM((2, 2, 2, WIN, WIN), BF),
            pltpu.VMEM((2, 2, WIN, WIN), BF),
            pltpu.VMEM((2, 2, WIN // 2, WIN), BF),
            pltpu.VMEM((2, 2, WIN // 2, WIN), F32),
            pltpu.VMEM((2, 2, WIN, WIN), BF),
            pltpu.VMEM((2, WIN, WIN), F32),
            pltpu.VMEM((2, 2, CLS, 2, 16, WIN), BF),
            pltpu.VMEM((2, PLANE, CAP // 2, 2, 16, WIN), BF),
            pltpu.VMEM((PLANE, 2, CAP, 128), jnp.int32),
            pltpu.VMEM((BANDS, 2, 2, 8, 1024), F32),
            pltpu.VMEM((BANDS, 2, 16, 1024), BF),
            pltpu.VMEM((BANDS, 2, 16, 1024), BF),
            dma((BANDS + 1,)),
            dma((4,)),
            dma,
            dma,
            dma((2, 2)),
            dma((2, 2)),
            dma((2,)),
            dma((PLANE,)),
            dma((PLANE,)),
            dma((2, PLANE)),
            dma((2, 2)),
            dma((BANDS,)),
            dma((BANDS,)),
        ],
        compiler_params=pltpu.CompilerParams(
            collective_id=0, has_side_effects=True, vmem_limit_bytes=40 * 2**20
        ),
        cost_estimate=pl.CostEstimate(
            flops=2 * 16 * 2**27, bytes_accessed=12 * 2**20, transcendentals=0
        ),
    )(counts, *(pltpu.with_memory_space_constraint(a, pltpu.HBM) for a in operands))
    return grad[None]


def solution(mesh):
    in_specs = (
        P("pos", None),
        P("pos"),
        P(None, "det", None),
        P("depth", None, None, None),
        P("pos", "det", None),
    )
    out_specs = P("depth", None, ("pos", "det"), None)
    return jax.shard_map(
        per_device, mesh=mesh, in_specs=in_specs, out_specs=out_specs, check_vma=False
    )
```

```python
import math

import jax
import jax.numpy as jnp
import numpy as np
from jax import lax
from jax.experimental import pallas as pl
from jax.experimental.pallas import tpu as pltpu
from jax.sharding import PartitionSpec as P

PROP_DIV = 2
WIN = 256
HALF = WIN // 2
NEAR = 160
PARTS = ((0, NEAR), (NEAR, WIN - NEAR))
BANDS = 4
PLANE = 8
CAP = 8
CLS = 16
ROUTE = ((1, 0), (3, 0), (0, 1), (2, 0), (1, 1), (3, 1), (2, 1), (0, 0))
MESH = pl.DeviceIdType.MESH
BF = jnp.bfloat16
F32 = jnp.float32


def tables():
    k = np.arange(WIN)
    angle = (k[:, None] * k[None, :] % WIN) * (2.0 * math.pi / WIN)
    cos, sin = np.cos(angle), np.sin(angle)
    f = np.where(k < WIN // 2, k, k - WIN)
    h = np.exp(-1j * math.pi / (PROP_DIV * WIN) * (f * f % (2 * PROP_DIV * WIN)))
    dft = cos - 1j * sin
    q = (np.conj(dft) * h[None, :]) @ dft / WIN
    qr, qi = q.real, q.imag
    out = np.stack(
        [
            np.block([[cos, -sin], [sin, cos]]) / 16,
            np.block([[cos, sin], [-sin, cos]]) / 16,
            np.block([[qr, qi], [-qi, qr]]),
            np.block([[qr, -qi], [qi, qr]]),
        ]
    )
    return out.astype(np.float32).astype(BF)


def dot(a, b):
    return jnp.dot(a, b, preferred_element_type=F32)


def beside(re, im):
    return jnp.concatenate([re.astype(BF), im.astype(BF)], axis=1)


def stacked(re, im):
    return jnp.concatenate([re.astype(BF), im.astype(BF)], axis=0)


def right_left(re, im, right, left):
    mid = dot(beside(re, im), right).astype(BF)
    out = dot(left, jnp.concatenate([mid[:, :WIN], mid[:, WIN:]], axis=0))
    return out[:WIN], out[WIN:]


def left_right(re, im, left, right):
    mid = dot(left, stacked(re, im)).astype(BF)
    out = dot(jnp.concatenate([mid[:WIN], mid[WIN:]], axis=1), right)
    return out[:, :WIN], out[:, WIN:]


def iota(shape, axis):
    return lax.broadcasted_iota(jnp.int32, shape, axis)


def kernel(
    counts, offs_in, probe, obj, measured, tabs_in, out,
    offs, other_offs, obj_v, tabs, t_all, t_send, probe_v, meas, rolled, amps, grad, pieces, places, acc, z_send, z_recv,
    load_sem, own_sem, probe_sem, meas_sem, t_sem, t_out_sem, out_sem, place_sem, place_out_sem,
    piece_sem, piece_out_sem, z_sem, z_out_sem,
):
    pos, d, c = lax.axis_index("pos"), lax.axis_index("depth"), lax.axis_index("det")
    z, q = pos // PLANE, pos % PLANE
    y, x = q // 2, q % 2 * 2 + d
    first_of_plane = z * PLANE
    cls = q * 2 + c
    other = z * PLANE + (q ^ 1)
    own = 2 * (2 * d + c)
    across = 2 * (2 * (1 - d) + c)
    beside_slot = 2 * (2 * d + 1 - c)

    barrier = pltpu.get_barrier_semaphore()
    for k in range(1, 2 * CLS):
        pl.semaphore_signal(
            barrier, inc=1,
            device_id=(z * PLANE + (q ^ (k // 4)), d ^ (k // 2 % 2), c ^ (k % 2)),
            device_id_type=MESH,
        )
    for k in range(1, BANDS):
        pl.semaphore_signal(
            barrier, inc=1, device_id=((z + k) % BANDS * PLANE + q, d, c), device_id_type=MESH
        )

    own_offs = pltpu.make_async_copy(offs_in, offs, own_sem.at[3])
    own_offs.start()
    load_obj = []
    for cb in range(BANDS):
        column = obj.at[:, :, :, pl.ds(cb * WIN, WIN)]
        load_obj.append(pltpu.make_async_copy(column, obj_v.at[cb], load_sem.at[cb]))
        load_obj[-1].start()
    load_tabs = pltpu.make_async_copy(tabs_in, tabs, load_sem.at[BANDS])
    load_tabs.start()
    own_probe = pltpu.make_async_copy(probe, probe_v.at[c], own_sem.at[0])
    own_probe.start()
    own_meas = pltpu.make_async_copy(measured.at[pl.ds(own, 2)], meas.at[c], own_sem.at[1])
    own_meas.start()

    own_offs.wait()
    slot_of = iota((CAP, 128), 0)
    for axis in range(2):
        spread = jnp.zeros((CAP, 128), jnp.int32)
        for s in range(CAP):
            spread = jnp.where(slot_of == s, offs[axis, s], spread)
        places[q, axis] = spread
    acc[...] = jnp.zeros_like(acc)
    pl.semaphore_wait(barrier, 2 * CLS - 1 + BANDS - 1)

    def place_copy(k):
        return pltpu.make_async_remote_copy(
            src_ref=places.at[q], dst_ref=places.at[q], send_sem=place_out_sem.at[k],
            recv_sem=place_sem.at[q], device_id=(z * PLANE + (q ^ k), d, c),
            device_id_type=MESH,
        )

    def places_of(g):
        return pltpu.make_async_copy(places.at[g], places.at[g], place_sem.at[g])

    offs_copy = pltpu.make_async_remote_copy(
        src_ref=offs, dst_ref=other_offs, send_sem=place_out_sem.at[0], recv_sem=own_sem.at[2],
        device_id=(other, d, c), device_id_type=MESH,
    )
    offs_copy.start()

    probe_copy = pltpu.make_async_remote_copy(
        src_ref=probe, dst_ref=probe_v.at[c], send_sem=out_sem.at[0], recv_sem=probe_sem,
        device_id=(pos, d, 1 - c), device_id_type=MESH,
    )
    probe_copy.start()
    meas_copy = pltpu.make_async_remote_copy(
        src_ref=measured.at[pl.ds(beside_slot, 2)], dst_ref=meas.at[c], send_sem=out_sem.at[1],
        recv_sem=meas_sem, device_id=(pos, d, 1 - c), device_id_type=MESH,
    )
    meas_copy.start()

    for column in load_obj:
        column.wait()

    row_of, col_of = iota((WIN, WIN), 0), iota((WIN, WIN), 1)

    def cut(r, col, plane, first, count):
        rows = pl.ds(first, count)
        band = jnp.minimum(r >> 8, BANDS - 2)
        block = jnp.minimum(col >> 8, BANDS - 2)
        late = iota((count, WIN), 1) >= col - block * WIN
        top = jnp.where(
            late, obj_v[block, plane, band, rows], obj_v[block + 1, plane, band, rows]
        )
        low = jnp.where(
            late, obj_v[block, plane, band + 1, rows], obj_v[block + 1, plane, band + 1, rows]
        )
        return jnp.where(iota((count, WIN), 0) >= r - band * WIN - first, top, low).astype(BF)

    def t_copy(i, part):
        rows = pl.ds(*PARTS[part])
        return pltpu.make_async_remote_copy(
            src_ref=t_send.at[i, :, rows], dst_ref=t_all.at[d, i, :, rows],
            send_sem=t_out_sem.at[i, part], recv_sem=t_sem.at[i, part],
            device_id=(other if part else pos, 1 - d, c), device_id_type=MESH,
        )

    def send_part(i, part):
        places_in = other_offs if part else offs
        for plane in range(2):
            t_send[i, plane, pl.ds(*PARTS[part])] = cut(
                places_in[0, across + i], places_in[1, across + i], plane, *PARTS[part]
            )
        t_copy(i, part).start()

    send_part(0, 0)
    offs_copy.wait_recv()
    send_part(0, 1)

    def window(s, i):
        return [t_all[s, i, p].astype(F32) for p in range(2)]

    def prepare(i):
        for plane in range(2):
            t_all[d, i, plane] = cut(offs[0, own + i], offs[1, own + i], plane, 0, WIN)
        flat = jnp.concatenate(
            [jnp.concatenate([probe_v[0, p], probe_v[1, p]], axis=0) for p in range(2)], axis=1
        )
        r, col = offs[0, own + i], offs[1, own + i]
        down = jnp.where(col_of == ((row_of - r) & (WIN - 1)), 1.0, 0.0).astype(BF)
        over = jnp.where(row_of == ((col_of - col) & (WIN - 1)), 1.0, 0.0).astype(BF)
        moved = dot(down, flat).astype(BF)
        moved = dot(jnp.concatenate([moved[:, :WIN], moved[:, WIN:]], axis=0), over)
        rolled[i, 0], rolled[i, 1] = moved[:WIN].astype(BF), moved[WIN:].astype(BF)
        amps[i] = jnp.concatenate([meas[0, i], meas[1, i]], axis=0).T

    own_probe.wait()
    own_meas.wait()
    probe_copy.wait_recv()
    meas_copy.wait_recv()
    prepare(0)
    send_part(1, 0)
    send_part(1, 1)
    for k in range(1, PLANE):
        place_copy(k).start()
    load_tabs.wait()

    def send_pieces(i, s):
        odd = d ^ s
        flip = c & odd
        for dy, far in ROUTE:
            yy = (y + (dy if dy % 2 == 0 else dy + 2 * c)) & 3
            xh = ((x + odd + 2 * (far ^ flip)) & 3) >> 1
            group = yy * 2 + xh
            for cc in range(2):
                if (dy, far, cc) == (0, 0, 0):
                    continue
                core = c ^ cc
                pltpu.make_async_remote_copy(
                    src_ref=grad.at[i, s, group * 2 + core],
                    dst_ref=pieces.at[i, q, 2 * d + c],
                    send_sem=piece_out_sem.at[i, s], recv_sem=piece_sem.at[i, q],
                    device_id=(first_of_plane + group, s, core), device_id_type=MESH,
                ).start()

    def send_here(i):
        xx = (x + 1 + 2 * c) % 4
        pltpu.make_async_remote_copy(
            src_ref=grad.at[i, 1 - d, (y * 2 + xx // 2) * 2 + c],
            dst_ref=pieces.at[i, q, 2 * d + c],
            send_sem=piece_out_sem.at[i, 0], recv_sem=piece_sem.at[i, q],
            device_id=(z * PLANE + y * 2 + xx // 2, 1 - d, c), device_id_type=MESH,
        ).start()
        pltpu.make_async_copy(
            grad.at[i, d, cls], pieces.at[i, q, 2 * d + c], piece_sem.at[i, q]
        ).start()

    def load(ref, i):
        return ref[i, 0].astype(F32), ref[i, 1].astype(F32)

    def rounded(pair):
        return pair[0].astype(BF).astype(F32), pair[1].astype(BF).astype(F32)

    def first_wave(i):
        for half in range(2):
            t_copy(i, half).wait_recv()
        (pr, pi), (tr, ti) = load(rolled, i), window(0, i)
        return rounded(
            right_left(pr * tr - pi * ti, pr * ti + pi * tr, tabs[2], tabs[3])
        )

    def far_field(i, wave):
        (wr, wi), (tr, ti) = wave, window(1, i)
        fr, fi = right_left(wr * tr - wi * ti, wr * ti + wi * tr, tabs[0], tabs[1])
        used = jnp.where(jnp.full((1, WIN), own + i, jnp.int32) < counts[0], 1.0, 0.0)
        scale = used * (1.0 - amps[i] * lax.rsqrt(jnp.maximum(fr * fr + fi * fi, 1.0)))
        return fr * scale, fi * scale

    def descent(residual):
        return rounded(left_right(residual[0], residual[1], tabs[0], tabs[1]))

    def put(i, s, wave, desc):
        (wr, wi), (dr, di) = wave, desc
        grad[i, s, :, 0] = (wr * dr + wi * di).astype(BF).reshape(CLS, 16, WIN)
        grad[i, s, :, 1] = (wr * di - wi * dr).astype(BF).reshape(CLS, 16, WIN)

    def first_descent(i, desc):
        (dr, di), (tr, ti) = desc, window(1, i)
        return rounded(
            right_left(tr * dr + ti * di, tr * di - ti * dr, tabs[3], tabs[2])
        )

    wave_a = first_wave(0)
    prepare(1)
    desc_a = descent(far_field(0, wave_a))
    put(0, 1, wave_a, desc_a)
    send_pieces(0, 1)
    desc_a = first_descent(0, desc_a)
    put(0, 0, load(rolled, 0), desc_a)
    send_pieces(0, 0)
    send_here(0)
    wave_b = first_wave(1)
    desc_b = descent(far_field(1, wave_b))
    put(1, 1, wave_b, desc_b)
    send_pieces(1, 1)
    put(1, 0, load(rolled, 1), first_descent(1, desc_b))
    send_pieces(1, 0)
    send_here(1)

    row16 = iota((2, 8, WIN), 0) * 8 + iota((2, 8, WIN), 1) + cls * 16
    col8 = iota((8, WIN), 1)

    def add_group(i, g):
        pltpu.make_async_copy(pieces.at[i, g], pieces.at[i, g], piece_sem.at[i, g]).wait()
        rows, cols = places[g, 0], places[g, 1]
        r0 = jnp.minimum(rows >> 8, BANDS - 2)
        c0 = jnp.minimum(cols >> 8, BANDS - 2)
        rm, cm = rows - r0 * WIN, cols - c0 * WIN

        def wide(x, k):
            one = jnp.broadcast_to(x[2 * k + i : 2 * k + i + 1], (8, 128))
            return jnp.concatenate([one, one], axis=1)

        band = [wide(r0, k) + jnp.where(row16 < wide(rm, k), 1, 0) for k in range(4)]
        block = [wide(c0, k) + jnp.where(col8 < wide(cm, k), 1, 0) for k in range(4)]
        for p in range(2):
            piece = [pieces[i, g, k, p].astype(F32).reshape(2, 8, WIN) for k in range(4)]
            for zb in range(BANDS):
                part = [jnp.where(b == zb, x, 0.0) for b, x in zip(band, piece)]
                for cb in range(BANDS):
                    total = acc[zb, p, :, :, cb * WIN : (cb + 1) * WIN]
                    for b, x in zip(block, part):
                        total += jnp.where(b == cb, x, 0.0)
                    acc[zb, p, :, :, cb * WIN : (cb + 1) * WIN] = total

    def add_first(k, carry):
        g = q ^ k ^ (k // 4 * 2)

        @pl.when(k > 0)
        def _():
            places_of(g).wait()

        add_group(0, g)
        return carry

    def add_second(k, carry):
        add_group(1, q ^ k ^ (k // 4 * 2))
        return carry

    lax.fori_loop(0, PLANE, add_first, 0)
    lax.fori_loop(0, PLANE, add_second, 0)

    def z_copy(k):
        there = (z + k) % BANDS
        return pltpu.make_async_remote_copy(
            src_ref=z_send.at[there], dst_ref=z_recv.at[k], send_sem=z_out_sem.at[k],
            recv_sem=z_sem.at[k], device_id=(there * PLANE + q, d, c), device_id_type=MESH,
        )

    for k in (1 + c, 2 - c, 3):
        z_send[(z + k) % BANDS] = acc[(z + k) % BANDS].reshape(2, 16, 1024).astype(BF)
        z_copy(k).start()
    total = acc[z].reshape(2, 16, 1024)
    for k in (3, 2, 1):
        z_copy(k).wait_recv()
        total += z_recv[k].astype(F32)
    out[...] = total

    for k in range(1, BANDS):
        z_copy(k).wait_send()
    offs_copy.wait_send()
    probe_copy.wait_send()
    meas_copy.wait_send()
    for i in range(2):
        for half in range(2):
            t_copy(i, half).wait_send()
    for k in range(1, PLANE):
        place_copy(k).wait_send()
    for i in range(2):
        for s, count in ((0, CLS), (1, CLS - 1)):
            sent = grad.at[i, s, pl.ds(0, count)]
            pltpu.make_async_copy(sent, sent, piece_out_sem.at[i, s]).wait()


def per_device(offsets, counts, probe_wave, object_slices, measured):
    smem = pl.BlockSpec(memory_space=pltpu.SMEM)
    anywhere = pl.BlockSpec(memory_space=pl.ANY)
    dma = pltpu.SemaphoreType.DMA
    planes = object_slices.reshape(2, BANDS, WIN, BANDS * WIN)
    operands = (offsets.T, probe_wave, planes, measured, jnp.asarray(tables()))
    grad = pl.pallas_call(
        kernel,
        out_shape=pltpu.VMEM((2, 16, 1024), F32),
        in_specs=[smem] + [anywhere] * 5,
        out_specs=pl.BlockSpec(memory_space=pltpu.VMEM),
        scratch_shapes=[
            pltpu.SMEM((2, CAP), jnp.int32),
            pltpu.SMEM((2, CAP), jnp.int32),
            pltpu.VMEM((BANDS, 2, BANDS, WIN, WIN), F32),
            pltpu.VMEM((4, 2 * WIN, 2 * WIN), BF),
            pltpu.VMEM((2, 2, 2, WIN, WIN), BF),
            pltpu.VMEM((2, 2, WIN, WIN), BF),
            pltpu.VMEM((2, 2, WIN // 2, WIN), BF),
            pltpu.VMEM((2, 2, WIN // 2, WIN), F32),
            pltpu.VMEM((2, 2, WIN, WIN), BF),
            pltpu.VMEM((2, WIN, WIN), F32),
            pltpu.VMEM((2, 2, CLS, 2, 16, WIN), BF),
            pltpu.VMEM((2, PLANE, CAP // 2, 2, 16, WIN), BF),
            pltpu.VMEM((PLANE, 2, CAP, 128), jnp.int32),
            pltpu.VMEM((BANDS, 2, 2, 8, 1024), F32),
            pltpu.VMEM((BANDS, 2, 16, 1024), BF),
            pltpu.VMEM((BANDS, 2, 16, 1024), BF),
            dma((BANDS + 1,)),
            dma((4,)),
            dma,
            dma,
            dma((2, 2)),
            dma((2, 2)),
            dma((2,)),
            dma((PLANE,)),
            dma((PLANE,)),
            dma((2, PLANE)),
            dma((2, 2)),
            dma((BANDS,)),
            dma((BANDS,)),
        ],
        compiler_params=pltpu.CompilerParams(
            collective_id=0, has_side_effects=True, vmem_limit_bytes=40 * 2**20
        ),
        cost_estimate=pl.CostEstimate(
            flops=2 * 16 * 2**27, bytes_accessed=12 * 2**20, transcendentals=0
        ),
    )(counts, *(pltpu.with_memory_space_constraint(a, pltpu.HBM) for a in operands))
    return grad[None]


def solution(mesh):
    in_specs = (
        P("pos", None),
        P("pos"),
        P(None, "det", None),
        P("depth", None, None, None),
        P("pos", "det", None),
    )
    out_specs = P("depth", None, ("pos", "det"), None)
    return jax.shard_map(
        per_device, mesh=mesh, in_specs=in_specs, out_specs=out_specs, check_vma=False
    )
```
